128 devices in a mesh: dp: 16 (over x, z_lo, core), ctx: 8 (over y, z_hi).
Axes of the slice: x: 4, y: 4, z: 4 (z_hi: 2, z_lo: 2; z = z_hi * 2 + z_lo), core: 2. Of those that a mesh axis runs over, the one named last changes fastest.
Arguments:
- layer_input: bfloat16 [16, 2048, 768], P('dp', 'ctx'), may hold values from -6 to 6
- cotangent: bfloat16 [16, 2048, 768], P('dp', 'ctx'), may hold values from -6 to 6
- lengths: int32 [16], P('dp'), may hold values from 1434 to 2048, as said below
- order: int32 [16, 16], P('dp'), may hold values from 0 to 15, each once within a row
- files: int32 [16, 2048], P('dp'), may hold values from 0 to 3, as said below
- ln1_gain: float32 [768], P(('dp', 'ctx')), may hold values from 0.25 to 1.75
- ln1_bias: float32 [768], P(('dp', 'ctx')), may hold values from -1.75 to 1.75
- w_attn: bfloat16 [768, 896], P(('dp', 'ctx')), may hold values from -0.21875 to 0.21875
- query_bias: float32 [768], P(('dp', 'ctx')), may hold values from -1.75 to 1.75
- value_bias: float32 [64], replicated, may hold values from -1.75 to 1.75
- w_out: bfloat16 [768, 768], P(('dp', 'ctx')), may hold values from -0.875 to 0.875
- out_bias: float32 [768], P(('dp', 'ctx')), may hold values from -1.75 to 1.75
- ln2_gain: float32 [768], P(('dp', 'ctx')), may hold values from 0.25 to 1.75
- ln2_bias: float32 [768], P(('dp', 'ctx')), may hold values from -1.75 to 1.75
- w_fc: bfloat16 [768, 3072], P(('dp', 'ctx')), may hold values from -0.21875 to 0.21875
- fc_bias: float32 [3072], P(('dp', 'ctx')), may hold values from -1.75 to 1.75
- w_proj: bfloat16 [768, 3072], P(('dp', 'ctx')), may hold values from -0.109375 to 0.109375
- proj_bias: float32 [768], P(('dp', 'ctx')), may hold values from -1.75 to 1.75
Outputs:
- output: bfloat16 [16, 2048, 768], P('dp', 'ctx')
- grad_input: bfloat16 [16, 2048, 768], P('dp', 'ctx')
- grad_ln1_gain: float32 [768], P(('dp', 'ctx'))
- grad_ln1_bias: float32 [768], P(('dp', 'ctx'))
- grad_w_attn: float32 [768, 896], P(('dp', 'ctx'))
- grad_query_bias: float32 [768], P(('dp', 'ctx'))
- grad_value_bias: float32 [64], replicated
- grad_w_out: float32 [768, 768], P(('dp', 'ctx'))
- grad_out_bias: float32 [768], P(('dp', 'ctx'))
- grad_ln2_gain: float32 [768], P(('dp', 'ctx'))
- grad_ln2_bias: float32 [768], P(('dp', 'ctx'))
- grad_w_fc: float32 [768, 3072], P(('dp', 'ctx'))
- grad_fc_bias: float32 [3072], P(('dp', 'ctx'))
- grad_w_proj: float32 [768, 3072], P(('dp', 'ctx'))
- grad_proj_bias: float32 [768], P(('dp', 'ctx'))
The draws below stay inside these ranges and needn't reach their ends.
Inputs may be any that keep to these rules, and one draw needn't show every extreme that they name: `lengths`: positions at or past a row's length are padding; some row's length is 2048. `order`: each row is a permutation of the 16 block numbers. `files`: file numbers never fall along initial positions and start at 0.
All inputs are finite; a program needn't handle non-finite values.
Results may differ from the reference program's by a relative error of at most 0.017.
Values may be sent and summed in bfloat16 or wider, within the bound.
No kernel may reach another device: no remote copies, remote signals or barrier semaphores. Data moves between devices by JAX's collectives and lax.ppermute only.
A program may use at most 128 MiB of HBM per device.

```python
import math
import jax
import jax.numpy as jnp
from jax import lax

D = 768
HEADS = 12
HD = 64
FF = 3072
LENGTH = 2048
BLOCKS = 16
ROWS = 16


def draw_lengths(key, part):
    key = jax.random.fold_in(key, 11)
    padding = jax.random.randint(key, (ROWS,), 0, 3 * LENGTH // 10 + 1)
    chosen = jax.random.randint(jax.random.fold_in(key, 1), (), 0, ROWS)
    values = LENGTH - padding
    return jnp.where(jnp.arange(ROWS) == chosen, LENGTH, values).astype(jnp.int32)


def draw_files(key, part):
    key = jax.random.fold_in(key, 12)
    first = jax.random.randint(jax.random.fold_in(key, 1), (ROWS, 1), LENGTH // 2, 3 * LENGTH // 4 + 1)
    second = first + 1 + jax.random.randint(jax.random.fold_in(key, 2), (ROWS, 1), 0, LENGTH - first - 1)
    third = first + 1 + jax.random.randint(jax.random.fold_in(key, 3), (ROWS, 1), 0, LENGTH - first - 1)
    places = jnp.arange(LENGTH)[None, :]
    number = (places >= first).astype(jnp.int32) + (places >= second).astype(jnp.int32) + (places >= third).astype(jnp.int32)
    return number.astype(jnp.int32)


def spiked(drawn, rng, source, target, parts, factor):
    owner, partner = [(jnp.arange(drawn.shape[position]) // (drawn.shape[position] // parts)).reshape([-1 if axis == position else 1 for axis in range(drawn.ndim)]) for position in (source, target)]
    chosen = jax.random.permutation(rng, parts)[partner]
    strong = (owner == chosen) | (owner == (partner + parts // 2) % parts)
    return jnp.where(strong, factor * drawn, drawn)


def block_levels(stream_key, shape, pieces, least, high):
    level, own = 1.0, jax.random.fold_in(stream_key, 6)
    for dim, shards_of in pieces:
        heights = jnp.exp(jax.random.uniform(jax.random.fold_in(own, dim), (shards_of,), jnp.float32, least / len(pieces), high / len(pieces)))
        level = level * jnp.repeat(heights, shape[dim] // shards_of).reshape([-1 if axis == dim else 1 for axis in range(len(shape))])
    return level


def scatter_about(rng, extent, deviation, most, shards=(), held_as=jnp.bfloat16):
    values = deviation * jax.random.normal(rng, extent, jnp.float32)
    if shards:
        values = values * block_levels(rng, extent, shards, -0.22, 0.18)
    return jnp.clip(values, -most, most).astype(held_as)


def bell_draw_with(stream_key, dims, scale, bound, shards, heavy, kind=jnp.bfloat16):
    entries = scale * jax.random.normal(stream_key, dims, jnp.float32)
    if shards:
        entries = entries * block_levels(stream_key, dims, shards, -0.22, 0.18)
    return jnp.clip(spiked(entries, jax.random.fold_in(stream_key, 3), *heavy), -bound, bound).astype(kind)


def setup_inputs(seed: int = 0) -> dict:
    arg_keys = jax.random.split(jax.random.key(seed), 19)
    layer_input = scatter_about(arg_keys[0], (ROWS, LENGTH, D), 1.0, 6.0, ((0, 16), (1, 8)))
    cotangent = bell_draw_with(arg_keys[1], (ROWS, LENGTH, D), 1.0, 6.0, ((0, 16), (1, 8)), (1, 2, 8, 2.0))
    lengths = draw_lengths(jax.random.fold_in(arg_keys[18], 71), 0)
    order = jax.vmap(lambda own: jax.random.permutation(own, BLOCKS))(jax.random.split(arg_keys[3], ROWS)).reshape((ROWS, BLOCKS)).astype(jnp.int32)
    files = draw_files(jax.random.fold_in(arg_keys[18], 71), 0)
    ln1_gain = jnp.clip(1.0 + 0.15 * jax.random.normal(arg_keys[5], (D,), jnp.float32), 0.25, 1.75)
    ln1_bias = scatter_about(arg_keys[6], (D,), 0.3, 1.75, ((0, 128),), jnp.float32)
    w_attn = scatter_about(arg_keys[7], (D, D + 2 * HD), D ** -0.5, 0.21875, ((0, 128),))
    query_bias = scatter_about(arg_keys[8], (D,), 0.3, 1.75, ((0, 128),), jnp.float32)
    value_bias = scatter_about(arg_keys[9], (HD,), 0.3, 1.75, (), jnp.float32)
    w_out = scatter_about(arg_keys[10], (D, D), (D // 16) ** -0.5, 0.875, ((0, 128),))
    out_bias = scatter_about(arg_keys[11], (D,), 0.3, 1.75, ((0, 128),), jnp.float32)
    ln2_gain = jnp.clip(1.0 + 0.15 * jax.random.normal(arg_keys[12], (D,), jnp.float32), 0.25, 1.75)
    ln2_bias = scatter_about(arg_keys[13], (D,), 0.3, 1.75, ((0, 128),), jnp.float32)
    w_fc = scatter_about(arg_keys[14], (D, FF), D ** -0.5, 0.21875, ((0, 128),))
    fc_bias = scatter_about(arg_keys[15], (FF,), 0.3, 1.75, ((0, 128),), jnp.float32)
    w_proj = scatter_about(arg_keys[16], (D, FF), FF ** -0.5, 0.109375, ((0, 128),))
    proj_bias = scatter_about(arg_keys[17], (D,), 0.3, 1.75, ((0, 128),), jnp.float32)
    return {"layer_input": layer_input, "cotangent": cotangent, "lengths": lengths, "order": order, "files": files, "ln1_gain": ln1_gain, "ln1_bias": ln1_bias, "w_attn": w_attn, "query_bias": query_bias, "value_bias": value_bias, "w_out": w_out, "out_bias": out_bias, "ln2_gain": ln2_gain, "ln2_bias": ln2_bias, "w_fc": w_fc, "fc_bias": fc_bias, "w_proj": w_proj, "proj_bias": proj_bias}


@jax.custom_vjp
def low(v):
    return lax.optimization_barrier(v.astype(jnp.bfloat16)).astype(jnp.float32)

@jax.custom_vjp
def low_back(v):
    return v

def low_keep(v):
    return (low(v), None)

def low_pass(kept, grad):
    return (grad,)

def back_keep(v):
    return (v, None)

def back_low(kept, grad):
    return (low(grad),)
low.defvjp(low_keep, low_pass)
low_back.defvjp(back_keep, back_low)

def layer_norm(values, gain, bias):
    center = values - lax.optimization_barrier(jnp.mean(values, -1, keepdims=True))
    spread = lax.optimization_barrier(jnp.mean(center * center, -1, keepdims=True))
    return center * lax.rsqrt(spread + 1e-05) * gain + bias

def project(left, right):
    return jnp.einsum('rtd,df->rtf', left, right, precision=lax.Precision.HIGHEST)

def attend_row(packed, places, file_ids, valid_length):
    query = packed[:, :D].reshape(LENGTH, HEADS, HD)
    key_rows = packed[:, D:D + HD]
    value_rows = packed[:, D + HD:]
    scores = jnp.einsum('qhd,kd->qhk', query, key_rows, precision=lax.Precision.HIGHEST) * (1.0 / math.sqrt(HD))
    scores = low_back(scores)
    allowed = (places[None, :] <= places[:, None]) & (file_ids[None, :] == file_ids[:, None])
    allowed = allowed & ((places[None, :] < valid_length) | (places[None, :] == places[:, None]))
    scores = jnp.where(allowed[:, None, :], scores, -1e+30)
    row_top = lax.optimization_barrier(jnp.max(scores, -1, keepdims=True))
    weights = jnp.exp(scores - row_top)
    attn_probs = low(weights / lax.optimization_barrier(jnp.sum(weights, -1, keepdims=True)))
    mixed = jnp.einsum('qhk,kd->qhd', attn_probs, value_rows, precision=lax.Precision.HIGHEST)
    return mixed.reshape(LENGTH, D)

def reference(layer_input, cotangent, lengths, order, files, ln1_gain, ln1_bias, w_attn, query_bias, value_bias, w_out, out_bias, ln2_gain, ln2_bias, w_fc, fc_bias, w_proj, proj_bias):
    span = LENGTH // BLOCKS
    within = (jnp.arange(LENGTH) % span).astype(jnp.int32)
    slots = (jnp.arange(LENGTH) // span).astype(jnp.int32)
    places = (order[:, slots] * span + within[None, :]).astype(jnp.int32)
    file_ids = jnp.take_along_axis(files, places, axis=1)
    attend = jax.checkpoint(attend_row)

    def forward(inputs, gain_one, bias_one, weight_attn, bias_query, bias_value, weight_out, bias_out, gain_two, bias_two, weight_fc, bias_fc, weight_proj, bias_proj):
        input_one = low(layer_norm(inputs, gain_one, bias_one))
        bias_full = jnp.concatenate([bias_query, jnp.zeros((HD,), jnp.float32), bias_value])
        projected = low(low_back(project(input_one, weight_attn) + bias_full))
        mixed = lax.map(lambda items: attend(*items), (projected, places, file_ids, lengths))
        attended = low(low_back(mixed))
        branch_one = low_back(project(attended, weight_out.T) + bias_out)
        middle = inputs + branch_one
        input_two = low(layer_norm(middle, gain_two, bias_two))
        before_gelu = low_back(project(input_two, weight_fc) + bias_fc)
        hidden = low(jax.nn.gelu(before_gelu, approximate=True))
        branch_two = low_back(project(hidden, weight_proj.T) + bias_proj)
        return middle + branch_two
    floats = [layer_input, ln1_gain, ln1_bias, w_attn, query_bias, value_bias, w_out, out_bias, ln2_gain, ln2_bias, w_fc, fc_bias, w_proj, proj_bias]
    floats = [item.astype(jnp.float32) for item in floats]
    result, pullback = jax.vjp(forward, *floats)
    pulled = pullback(cotangent.astype(jnp.float32))
    return (result.astype(jnp.bfloat16), pulled[0].astype(jnp.bfloat16), pulled[1], pulled[2], pulled[3], pulled[4], pulled[5], pulled[6], pulled[7], pulled[8], pulled[9], pulled[10], pulled[11], pulled[12], pulled[13])
```

```python
import functools

import jax
import jax.numpy as jnp
import numpy as np
from jax import lax
from jax.experimental import pallas as pl
from jax.experimental.pallas import tpu as pltpu
from jax.sharding import Mesh
from jax.sharding import PartitionSpec as P

D = 768
HEADS = 12
HD = 64
FF = 3072
TOK = 256
LENGTH = 2048
BLOCK = 128
BLOCKS = 16
PAIRS = 6
ROWS = 48
COLS = 384
NEG = -1e30

AXES = ("x", "zl", "core", "y", "zh")
SIZES = (4, 2, 2, 4, 2)
DP = ("x", "zl", "core")
CTX = ("y", "zh")

f32 = jnp.float32
bf16 = jnp.bfloat16


def route(dx=0, dy=0, dz=0, dc=0):
    pairs = []
    for device in range(128):
        x, zl, core, y, zh = (int(v) for v in np.unravel_index(device, SIZES))
        z = (zh * 2 + zl + dz) % 4
        target = ((x + dx) % 4, z % 2, core ^ dc, (y + dy) % 4, z // 2)
        pairs.append((device, int(np.ravel_multi_index(target, SIZES))))
    return pairs


def send(value, **shift):
    return lax.ppermute(value, AXES, route(**shift))


def mm(left, right):
    return lax.dot_general(left, right, (((1,), (0,)), ((), ())), preferred_element_type=f32)


def mm_nt(left, right):
    return lax.dot_general(left, right, (((1,), (1,)), ((), ())), preferred_element_type=f32)


def normalize(values):
    center = values - jnp.mean(values, -1, keepdims=True)
    spread = jnp.mean(center * center, -1, keepdims=True)
    factor = lax.rsqrt(spread + 1e-05)
    return center * factor, factor


def norm_back(grad_normed, normed, factor):
    return factor * (
        grad_normed
        - jnp.mean(grad_normed, -1, keepdims=True)
        - normed * jnp.mean(grad_normed * normed, -1, keepdims=True)
    )


def split_low(values):
    high = values.astype(bf16)
    return high, (values - high.astype(f32)).astype(bf16)


def first_kernel(x_ref, early_ref, vbias_ref, one_ref, kv_ref, vec_ref):
    turned = early_ref[:, BLOCK:].astype(f32).T
    vec = turned[0:16] + turned[16:32] + turned[32:48]
    vec_ref[...] = vec
    normed, _ = normalize(x_ref[...].astype(f32))
    one = (normed * vec[0:1] + vec[1:2]).astype(bf16)
    one_ref[...] = one
    bias = jnp.concatenate([jnp.zeros((1, HD), f32), vbias_ref[...]], 1)
    kv_ref[...] = (mm(one, early_ref[:, :BLOCK]) + bias).astype(bf16)


def block_plan(meta, b):
    place = meta[32 + b]
    length = meta[34]
    start = place * BLOCK
    first = jnp.int32(0)
    for f in range(3):
        bound = meta[35 + f]
        first = jnp.where(bound <= start, jnp.maximum(first, bound), first)
    low = first // BLOCK
    high = jnp.minimum(place - 1, (length - 1) // BLOCK)
    return place, low, jnp.maximum(high - low + 1, 0) + 1


def block_bias(meta, place, initial):
    lane = lax.broadcasted_iota(jnp.int32, (1, 2 * BLOCK), 1)
    query = place * BLOCK + (lane & (BLOCK - 1))
    first = jnp.zeros_like(query)
    for f in range(3):
        bound = meta[35 + f]
        first = jnp.where(bound <= query, jnp.maximum(first, bound), first)
    last = jnp.minimum(query, meta[34] - 1)
    key = initial * BLOCK + lax.broadcasted_iota(jnp.int32, (BLOCK, 2 * BLOCK), 0)
    allowed = ((key >= first) & (key <= last)) | (key == query)
    return jnp.where(allowed, 0.0, NEG)


def fold_heads(block):
    turned = block.T
    return jnp.concatenate([turned[:HD], turned[HD:]], 1)


def unfold_heads(wide):
    return jnp.concatenate([wide[:, :BLOCK], wide[:, BLOCK:]], 0).T


def forward_kernel(
    meta, one_ref, wq_ref, vec_ref, kv_ref, q_ref, att_ref, lse_ref, qt, vt, scores, mixed
):
    q = (mm(one_ref[...], wq_ref[...]) + vec_ref[2:3]).astype(bf16)
    q_ref[...] = q
    for b in range(2):
        for p in range(PAIRS):
            block = q[b * BLOCK : (b + 1) * BLOCK, p * BLOCK : (p + 1) * BLOCK].astype(f32) * 0.125
            qt[b, p, :HD] = fold_heads(block).astype(bf16)
            qt[b, p, HD:] = jnp.zeros((HD, 2 * BLOCK), bf16)
    for k in range(BLOCKS):
        vt[k] = kv_ref[k * BLOCK : (k + 1) * BLOCK].astype(f32).T[HD:].astype(bf16)

    for b in range(2):
        place, low, count = block_plan(meta, b)

        def initial_of(t):
            return jnp.where(t == count - 1, place, low + t)

        def score_step(t, tops):
            initial = initial_of(t)
            stored = meta[16 + initial]
            rows = kv_ref[pl.ds(pl.multiple_of(stored * BLOCK, BLOCK), BLOCK)]
            bias = block_bias(meta, place, initial)
            new = []
            for p in range(PAIRS):
                value = mm(rows, qt[b, p]) + bias
                scores[t, p] = value
                new.append(jnp.maximum(tops[p], jnp.max(value.reshape(16, 8, 2 * BLOCK), 0)))
            return tuple(new)

        tops = lax.fori_loop(
            0, count, score_step, tuple(jnp.full((8, 2 * BLOCK), NEG, f32) for _ in range(PAIRS))
        )
        tops = tuple(jnp.max(top, 0, keepdims=True) for top in tops)
        mixed[...] = jnp.zeros_like(mixed)

        def mix_step(t, sums):
            stored = meta[16 + initial_of(t)]
            values = vt[stored]
            new = []
            for p in range(PAIRS):
                weight = jnp.exp(scores[t, p] - tops[p])
                new.append(sums[p] + jnp.sum(weight.reshape(16, 8, 2 * BLOCK), 0))
                mixed[p] += mm(values, weight.astype(bf16))
            return tuple(new)

        sums = lax.fori_loop(
            0, count, mix_step, tuple(jnp.zeros((8, 2 * BLOCK), f32) for _ in range(PAIRS))
        )
        for p in range(PAIRS):
            total = jnp.sum(sums[p], 0, keepdims=True)
            lse_ref[b, p] = jnp.broadcast_to(tops[p] + jnp.log(total), (8, 2 * BLOCK))
            att_ref[b * BLOCK : (b + 1) * BLOCK, p * BLOCK : (p + 1) * BLOCK] = unfold_heads(
                mixed[p] / total
            ).astype(bf16)


def backward_kernel(
    meta,
    q_ref,
    do_ref,
    att_ref,
    lse_ref,
    kv_ref,
    one_ref,
    gq_ref,
    gwq_ref,
    dkv_ref,
    qt,
    dot_,
    qn,
    don,
    kt,
    delta,
    dq,
    dkv,
):
    zeros = jnp.zeros((BLOCK, HD), f32)
    for b in range(2):
        for p in range(PAIRS):
            span = (slice(b * BLOCK, (b + 1) * BLOCK), slice(p * BLOCK, (p + 1) * BLOCK))
            block = q_ref[span].astype(f32) * 0.125
            grad = do_ref[span].astype(f32)
            out = att_ref[span].astype(f32)
            qt[b, p, :HD] = fold_heads(block).astype(bf16)
            qt[b, p, HD:] = jnp.zeros((HD, 2 * BLOCK), bf16)
            wide = fold_heads(grad)
            dot_[b, p, :HD] = jnp.zeros((HD, 2 * BLOCK), bf16)
            dot_[b, p, HD:] = wide.astype(bf16)
            delta[b, p] = jnp.broadcast_to(
                jnp.sum(wide * fold_heads(out), 0, keepdims=True), (8, 2 * BLOCK)
            )
            qn[b, p, :BLOCK] = jnp.concatenate([block[:, :HD], zeros], 1).astype(bf16)
            qn[b, p, BLOCK:] = jnp.concatenate([block[:, HD:], zeros], 1).astype(bf16)
            don[b, p, :BLOCK] = jnp.concatenate([zeros, grad[:, :HD]], 1).astype(bf16)
            don[b, p, BLOCK:] = jnp.concatenate([zeros, grad[:, HD:]], 1).astype(bf16)
    for k in range(BLOCKS):
        kt[k] = kv_ref[k * BLOCK : (k + 1) * BLOCK].astype(f32).T[:HD].astype(bf16)
    dkv[...] = jnp.zeros_like(dkv)

    for b in range(2):
        place, low, count = block_plan(meta, b)
        dq[...] = jnp.zeros_like(dq)

        def step(t, carry):
            initial = jnp.where(t == count - 1, place, low + t)
            stored = meta[16 + initial]
            rows = kv_ref[pl.ds(pl.multiple_of(stored * BLOCK, BLOCK), BLOCK)]
            keys = kt[stored]
            bias = block_bias(meta, place, initial)
            total = dkv[stored]
            for p in range(PAIRS):
                value = mm(rows, qt[b, p]) + bias
                probs = jnp.exp(value - lse_ref[b, p, 0:1])
                grad = probs * (mm(rows, dot_[b, p]) - delta[b, p, 0:1])
                low_probs = probs.astype(bf16)
                low_grad = grad.astype(bf16)
                dq[p] += mm(keys, low_grad)
                total = total + mm(low_grad, qn[b, p]) + mm(low_probs, don[b, p])
            dkv[stored] = total
            return carry

        lax.fori_loop(0, count, step, 0)
        for p in range(PAIRS):
            gq_ref[b * BLOCK : (b + 1) * BLOCK, p * BLOCK : (p + 1) * BLOCK] = unfold_heads(
                dq[p] * 0.125
            ).astype(bf16)
    for k in range(BLOCKS):
        dkv_ref[k * BLOCK : (k + 1) * BLOCK] = dkv[k].astype(bf16)
    gwq_ref[...] = mm(one_ref[...].T, gq_ref[...]).astype(bf16)


def middle_kernel(meta, *refs):
    fc_parts = refs[0:8]
    proj_parts = refs[8:16]
    x_ref, ct_ref, att_ref, wout_ref, vec_ref, fcb_ref = refs[16:22]
    out_ref, gmid_ref, gatt_ref, gwout_ref, sums_ref, fcsum_ref = refs[22:28]
    keep_fc, send_fc, keep_proj, send_proj = refs[28:32]
    (wf, wg, gf, gg, in_sem, out_sem, x2, x2t, gtt, branch, gin, mid) = refs[32:]
    px, py, pz, pc = meta[38], meta[39], meta[40], meta[41]

    def places(dx, dc, zl, h):
        row = lax.rem(px + dx, 4) * 192 + zl * 96 + (pc if dc == 0 else 1 - pc) * ROWS
        return pl.ds(pl.multiple_of(row, 16), ROWS), lax.rem(2 * h + zl - pz + 4, 4)

    def fetch(c, slot):
        dy, h = c // 2, lax.rem(c, 2)
        for dx in range(4):
            for dc in range(2):
                for zl in range(2):
                    rows, dz = places(dx, dc, zl, h)
                    pltpu.make_async_copy(
                        fc_parts[dx * 2 + dc].at[dy, dz], wf.at[slot, rows], in_sem.at[slot, 0]
                    ).start()
        for k in range(4):

            @pl.when(dy == k)
            def _():
                for dx in range(4):
                    for dc in range(2):
                        for zl in range(2):
                            rows, dz = places(dx, dc, zl, h)
                            pltpu.make_async_copy(
                                proj_parts[k * 2 + dc].at[dx, dz],
                                wg.at[slot, rows],
                                in_sem.at[slot, 1],
                            ).start()

    def fetched(slot):
        pltpu.make_async_copy(wf.at[slot], wf.at[slot], in_sem.at[slot, 0]).wait()
        pltpu.make_async_copy(wg.at[slot], wg.at[slot], in_sem.at[slot, 1]).wait()

    def store(c, slot):
        dy, h = c // 2, lax.rem(c, 2)
        for dx in range(4):
            for dc in range(2):
                for zl in range(2):
                    rows, dz = places(dx, dc, zl, h)
                    fc_out = send_fc if dc else keep_fc
                    proj_out = send_proj if dc else keep_proj
                    pltpu.make_async_copy(
                        gf.at[slot, rows], fc_out.at[dx, dy, dz], out_sem.at[slot, 0]
                    ).start()
                    pltpu.make_async_copy(
                        gg.at[slot, rows], proj_out.at[dy, dx, dz], out_sem.at[slot, 1]
                    ).start()

    def stored(slot):
        pltpu.make_async_copy(gf.at[slot], gf.at[slot], out_sem.at[slot, 0]).wait()
        pltpu.make_async_copy(gg.at[slot], gg.at[slot], out_sem.at[slot, 1]).wait()

    fetch(0, 0)
    vec = vec_ref[...]
    att = att_ref[...]
    cot = ct_ref[...]
    middle = x_ref[...].astype(f32) + (mm_nt(att, wout_ref[...]) + vec[3:4])
    mid[...] = middle
    normed, factor = normalize(middle)
    two = (normed * vec[4:5] + vec[5:6]).astype(bf16)
    x2[...] = two
    x2t[...] = two.astype(f32).T.astype(bf16)
    gtt[...] = cot.astype(f32).T.astype(bf16)
    branch[...] = jnp.zeros_like(branch)
    gin[...] = jnp.zeros_like(gin)

    def chunk(c, carry):
        slot = lax.rem(c, 2)

        @pl.when(c + 1 < 8)
        def _():
            fetch(c + 1, 1 - slot)

        fetched(slot)
        col = (lax.rem(py + c // 2, 4) * 2 + lax.rem(c, 2)) * COLS
        span = pl.ds(pl.multiple_of(col, BLOCK), COLS)
        w_fc = wf[slot]
        w_proj = wg[slot]
        pre = mm(x2[...], w_fc) + fcb_ref[:, span]
        square = pre * pre
        tanh = jnp.tanh(0.7978845608028654 * (pre + 0.044715 * (pre * square)))
        half = 0.5 * (1.0 + tanh)
        hidden = (pre * half).astype(bf16)
        slope = half + (0.5 * pre) * (1.0 - tanh * tanh) * (
            0.7978845608028654 + (3 * 0.044715 * 0.7978845608028654) * square
        )
        branch[...] += mm_nt(hidden, w_proj)
        grad_pre = (mm(ct_ref[...], w_proj) * slope).astype(bf16)
        gin[...] += mm_nt(grad_pre, w_fc)
        fcsum_ref[:, span] = jnp.sum(grad_pre.astype(f32), 0, keepdims=True)

        @pl.when(c >= 2)
        def _():
            stored(slot)

        gf[slot] = mm(x2t[...], grad_pre).astype(bf16)
        gg[slot] = mm(gtt[...], hidden).astype(bf16)
        store(c, slot)
        return carry

    lax.fori_loop(0, 8, chunk, 0)
    middle = mid[...]
    cot = ct_ref[...].astype(f32)
    out_ref[...] = (middle + (branch[...] + vec[6:7])).astype(bf16)
    normed, factor = normalize(middle)
    grad_two = gin[...]
    grad_middle = cot + norm_back(grad_two * vec[4:5], normed, factor)
    gmid_ref[...] = grad_middle
    grad_branch = grad_middle.astype(bf16)
    gatt_ref[...] = mm(grad_branch, wout_ref[...]).astype(bf16)
    turned = grad_branch.astype(f32).T.astype(bf16)
    gwout_ref[...] = mm(turned, att).astype(bf16)
    sums_ref[...] = jnp.concatenate(
        [
            jnp.sum(grad_branch.astype(f32), 0, keepdims=True),
            jnp.sum(grad_two * normed, 0, keepdims=True),
            jnp.sum(grad_two, 0, keepdims=True),
            jnp.sum(cot, 0, keepdims=True),
            jnp.zeros((4, D), f32),
        ],
        0,
    )
    stored(0)
    stored(1)


def last_kernel(
    x_ref, one_ref, gq_ref, dkv_ref, gmid_ref, wq_ref, early_ref, vec_ref, sums_ref, fc4_ref,
    gx_ref, pack_ref,
):
    gkv = jnp.sum(dkv_ref[...].astype(f32), 0).astype(bf16)
    gq = gq_ref[...]
    vec = vec_ref[...]
    grad_one = mm_nt(gq, wq_ref[...]) + mm_nt(gkv, early_ref[:, :BLOCK])
    normed, factor = normalize(x_ref[...].astype(f32))
    gx_ref[...] = (gmid_ref[...] + norm_back(grad_one * vec[0:1], normed, factor)).astype(bf16)
    pack_ref[:, :BLOCK] = mm(one_ref[...].astype(f32).T.astype(bf16), gkv).astype(bf16)
    sums = sums_ref[...]
    rows = jnp.concatenate(
        [
            jnp.sum(grad_one * normed, 0, keepdims=True),
            jnp.sum(grad_one, 0, keepdims=True),
            jnp.sum(gq.astype(f32), 0, keepdims=True),
            sums[0:4],
            fc4_ref[0:4],
            jnp.zeros((5, D), f32),
        ],
        0,
    )
    high, low = split_low(rows)
    value = jnp.sum(gkv.astype(f32), 0, keepdims=True)[:, HD:]
    value_high, value_low = split_low(value)
    lane = lax.broadcasted_iota(jnp.int32, (16, HD), 1)
    mine = (lane & 15) == lax.broadcasted_iota(jnp.int32, (16, HD), 0)
    group = lax.broadcasted_iota(jnp.int32, (HD, D), 0) // 16
    spread = jnp.where(group == lax.broadcasted_iota(jnp.int32, (HD, D), 1) % 6, 1.0, 0.0).astype(bf16)
    put_high = mm(jnp.where(mine, value_high.astype(f32), 0.0).astype(bf16), spread)
    put_low = mm(jnp.where(mine, value_low.astype(f32), 0.0).astype(bf16), spread)
    packed = jnp.concatenate(
        [high.astype(f32), low.astype(f32), put_high, put_low, jnp.zeros((64, D), f32)], 0
    )
    pack_ref[:, BLOCK:] = packed.T.astype(bf16)


def whole(count):
    return [pl.BlockSpec(memory_space=pltpu.VMEM)] * count


def shape(*dims, dtype=bf16):
    return jax.ShapeDtypeStruct(dims, dtype)


def params(mib=56):
    return pltpu.CompilerParams(vmem_limit_bytes=mib * 1024 * 1024)


def cost(flops, moved, exps=0):
    return pl.CostEstimate(flops=flops, bytes_accessed=moved, transcendentals=exps)


SMEM = pl.BlockSpec(memory_space=pltpu.SMEM)
ANY = pl.BlockSpec(memory_space=pl.ANY)


def gather_rows(value):
    copies = jnp.broadcast_to(value[None], (128,) + value.shape)
    return lax.all_to_all(copies, AXES, 0, 0).reshape(D, value.shape[1])


def scatter_rows(value):
    pieces = lax.all_to_all(value.reshape(128, 6, value.shape[1]), AXES, 0, 0)
    return jnp.sum(pieces.astype(f32), 0)


def gather_mlp(w_fc, w_proj):
    both = jnp.concatenate(
        [w_fc.reshape(6, 8, COLS).transpose(1, 0, 2), w_proj.reshape(6, 8, COLS).transpose(1, 0, 2)],
        2,
    )
    block = lax.all_to_all(both, CTX, 0, 0).reshape(ROWS, 2 * COLS)
    ring = [block] + [send(block, dz=-k) for k in (1, 2, 3)]
    fc = jnp.stack([part[:, :COLS] for part in ring])
    proj = jnp.stack([part[:, COLS:] for part in ring])
    fc = jnp.stack([fc] + [send(fc, dy=-k) for k in (1, 2, 3)])
    proj = jnp.stack([proj] + [send(proj, dx=-k) for k in (1, 2, 3)])
    fc_parts = [fc] + [send(fc, dx=-k) for k in (1, 2, 3)]
    proj_parts = [proj] + [send(proj, dy=-k) for k in (1, 2, 3)]
    fc_all, proj_all = [], []
    for part in fc_parts:
        fc_all += [part, send(part, dc=1)]
    for part in proj_parts:
        proj_all += [part, send(part, dc=1)]
    return fc_all, proj_all


def add_all(parts, dtype=bf16):
    total = parts[0].astype(f32)
    for part in parts[1:]:
        total = total + part.astype(f32)
    return total.astype(dtype)


def scatter_mlp(keep_fc, send_fc, keep_proj, send_proj):
    got_fc = send(send_fc, dc=1)
    got_proj = send(send_proj, dc=1)
    fc = [add_all([keep_fc[k], got_fc[k]]) for k in range(4)]
    proj = [add_all([keep_proj[k], got_proj[k]]) for k in range(4)]
    fc = add_all([fc[0]] + [send(fc[k], dx=k) for k in (1, 2, 3)])
    proj = add_all([proj[0]] + [send(proj[k], dy=k) for k in (1, 2, 3)])
    fc = add_all([fc[0]] + [send(fc[k], dy=k) for k in (1, 2, 3)])
    proj = add_all([proj[0]] + [send(proj[k], dx=k) for k in (1, 2, 3)])
    both = [jnp.concatenate([fc[k], proj[k]], 1) for k in range(4)]
    block = add_all([both[0]] + [send(both[k], dz=k) for k in (1, 2, 3)], f32)
    mine = lax.all_to_all(block.reshape(8, 6, 2 * COLS), CTX, 0, 0).transpose(1, 0, 2)
    return mine[:, :, :COLS].reshape(6, FF), mine[:, :, COLS:].reshape(6, FF)


def local(
    layer_input,
    cotangent,
    lengths,
    order,
    files,
    ln1_gain,
    ln1_bias,
    w_attn,
    query_bias,
    value_bias,
    w_out,
    out_bias,
    ln2_gain,
    ln2_bias,
    w_fc,
    fc_bias,
    w_proj,
    proj_bias,
):
    x = layer_input[0]
    cot = cotangent[0]
    px, zl, pc, py, zh = (lax.axis_index(name) for name in AXES)
    own = py * 2 + zh
    order_row = order[0]
    slots = jnp.arange(BLOCKS, dtype=jnp.int32)
    inverse = jnp.sum(jnp.where(order_row[None, :] == slots[:, None], slots[None, :], 0), 1)
    bounds = [jnp.sum((files[0] < f).astype(jnp.int32)) for f in (1, 2, 3)]
    own_places = lax.dynamic_slice_in_dim(order_row, own * 2, 2)
    meta = jnp.concatenate(
        [
            order_row,
            inverse,
            own_places,
            lengths,
            jnp.stack(bounds + [px, py, zh * 2 + zl, pc]).astype(jnp.int32),
        ]
    )

    per_row = jnp.stack(
        [ln1_gain, ln1_bias, query_bias, out_bias, ln2_gain, ln2_bias, proj_bias], 1
    )
    per_row = jnp.concatenate([per_row, fc_bias.reshape(6, 4), jnp.zeros((6, 5), f32)], 1)
    high, rest = split_low(per_row)
    middle, low = split_low(per_row - high.astype(f32))
    early = jnp.concatenate(
        [w_attn[:, D:], high, middle, low, jnp.zeros((6, BLOCK - 48), bf16)], 1
    )
    early = gather_rows(early)
    wq = gather_rows(w_attn[:, :D])
    fc_all, proj_all = gather_mlp(w_fc, w_proj)
    wout = gather_rows(w_out)

    one, kv, vec = pl.pallas_call(
        first_kernel,
        out_shape=[shape(TOK, D), shape(TOK, BLOCK), shape(16, D, dtype=f32)],
        in_specs=whole(3),
        out_specs=whole(3),
        compiler_params=params(),
        cost_estimate=cost(2 * TOK * D * BLOCK, 1_000_000),
        name="first",
    )(x, early, value_bias[None])
    kv_all = lax.all_to_all(
        jnp.broadcast_to(kv[None], (8, TOK, BLOCK)), CTX, 0, 0
    ).reshape(LENGTH, BLOCK)
    fcb = vec[7:11].T.reshape(1, FF)

    wide = (2, PAIRS, BLOCK, 2 * BLOCK)
    q, att, lse = pl.pallas_call(
        forward_kernel,
        out_shape=[shape(TOK, D), shape(TOK, D), shape(2, PAIRS, 8, 2 * BLOCK, dtype=f32)],
        in_specs=[SMEM] + whole(4),
        out_specs=whole(3),
        scratch_shapes=[
            pltpu.VMEM(wide, bf16),
            pltpu.VMEM((BLOCKS, HD, BLOCK), bf16),
            pltpu.VMEM((BLOCKS, PAIRS, BLOCK, 2 * BLOCK), f32),
            pltpu.VMEM((PAIRS, HD, 2 * BLOCK), f32),
        ],
        compiler_params=params(),
        cost_estimate=cost(20_000_000_000, 4_000_000, 6_000_000),
        name="attend",
    )(meta, one, wq, vec, kv_all)

    block = shape(4, 4, 4, ROWS, COLS)
    results = pl.pallas_call(
        middle_kernel,
        out_shape=[
            shape(TOK, D),
            shape(TOK, D, dtype=f32),
            shape(TOK, D),
            shape(D, D),
            shape(8, D, dtype=f32),
            shape(1, FF, dtype=f32),
            block,
            block,
            block,
            block,
        ],
        in_specs=[SMEM] + [ANY] * 16 + whole(6),
        out_specs=whole(6) + [ANY] * 4,
        scratch_shapes=[
            pltpu.VMEM((2, D, COLS), bf16),
            pltpu.VMEM((2, D, COLS), bf16),
            pltpu.VMEM((2, D, COLS), bf16),
            pltpu.VMEM((2, D, COLS), bf16),
            pltpu.SemaphoreType.DMA((2, 2)),
            pltpu.SemaphoreType.DMA((2, 2)),
            pltpu.VMEM((TOK, D), bf16),
            pltpu.VMEM((D, TOK), bf16),
            pltpu.VMEM((D, TOK), bf16),
            pltpu.VMEM((TOK, D), f32),
            pltpu.VMEM((TOK, D), f32),
            pltpu.VMEM((TOK, D), f32),
        ],
        compiler_params=params(),
        cost_estimate=cost(8_000_000_000, 20_000_000, 1_000_000),
        name="feed",
    )(meta, *fc_all, *proj_all, x, cot, att, wout, vec, fcb)
    output, grad_middle, grad_att, gwout, sums, fcsum = results[:6]
    grad_w_fc, grad_w_proj = scatter_mlp(*results[6:])
    grad_w_out = scatter_rows(gwout)

    gq, gwq, dkv = pl.pallas_call(
        backward_kernel,
        out_shape=[shape(TOK, D), shape(D, D), shape(LENGTH, BLOCK)],
        in_specs=[SMEM] + whole(6),
        out_specs=whole(3),
        scratch_shapes=[
            pltpu.VMEM(wide, bf16),
            pltpu.VMEM(wide, bf16),
            pltpu.VMEM((2, PAIRS, 2 * BLOCK, BLOCK), bf16),
            pltpu.VMEM((2, PAIRS, 2 * BLOCK, BLOCK), bf16),
            pltpu.VMEM((BLOCKS, HD, BLOCK), bf16),
            pltpu.VMEM((2, PAIRS, 8, 2 * BLOCK), f32),
            pltpu.VMEM((PAIRS, HD, 2 * BLOCK), f32),
            pltpu.VMEM((BLOCKS, BLOCK, BLOCK), f32),
        ],
        compiler_params=params(),
        cost_estimate=cost(40_000_000_000, 6_000_000, 6_000_000),
        name="attend_back",
    )(meta, q, grad_att, att, lse, kv_all, one)
    got = lax.all_to_all(dkv.reshape(8, TOK, BLOCK), CTX, 0, 0)
    grad_wq = scatter_rows(gwq)

    fc4 = jnp.concatenate([fcsum.reshape(D, 4).T, jnp.zeros((4, D), f32)], 0)
    grad_x, pack = pl.pallas_call(
        last_kernel,
        out_shape=[shape(TOK, D), shape(D, 2 * BLOCK)],
        in_specs=whole(10),
        out_specs=whole(2),
        compiler_params=params(),
        cost_estimate=cost(1_000_000_000, 5_000_000),
        name="last",
    )(x, one, gq, got, grad_middle, wq, early, vec, sums, fc4)
    tail = scatter_rows(pack)
    rows = tail[:, BLOCK : BLOCK + 16] + tail[:, BLOCK + 16 : BLOCK + 32]
    value = tail[0:4, BLOCK + 32 : BLOCK + 48] + tail[0:4, BLOCK + 48 : BLOCK + 64]
    return (
        output[None],
        grad_x[None],
        rows[:, 0],
        rows[:, 1],
        jnp.concatenate([grad_wq, tail[:, :BLOCK]], 1),
        rows[:, 2],
        value.reshape(HD),
        grad_w_out,
        rows[:, 3],
        rows[:, 4],
        rows[:, 5],
        grad_w_fc,
        rows[:, 7:11].reshape(24),
        grad_w_proj,
        rows[:, 6],
    )


def solution(mesh):
    cells = Mesh(mesh.devices.reshape(SIZES), AXES)
    every = P(AXES)
    tall = P(AXES, None)
    tokens = P(DP, CTX, None)
    in_specs = (
        tokens,
        tokens,
        P(DP),
        P(DP, None),
        P(DP, None),
        every,
        every,
        tall,
        every,
        P(),
        tall,
        every,
        every,
        every,
        tall,
        every,
        tall,
        every,
    )
    out_specs = (
        tokens,
        tokens,
        every,
        every,
        tall,
        every,
        P(),
        tall,
        every,
        every,
        every,
        tall,
        every,
        tall,
        every,
    )
    return jax.shard_map(local, mesh=cells, in_specs=in_specs, out_specs=out_specs, check_vma=False)
```

```python
import functools

import jax
import jax.numpy as jnp
import numpy as np
from jax import lax
from jax.experimental import pallas as pl
from jax.experimental.pallas import tpu as pltpu
from jax.sharding import Mesh
from jax.sharding import PartitionSpec as P

D = 768
HEADS = 12
HD = 64
FF = 3072
TOK = 256
LENGTH = 2048
BLOCK = 128
BLOCKS = 16
PAIRS = 6
ROWS = 48
COLS = 384
NEG = -1e30

AXES = ("x", "zl", "core", "y", "zh")
SIZES = (4, 2, 2, 4, 2)
DP = ("x", "zl", "core")
CTX = ("y", "zh")

f32 = jnp.float32
bf16 = jnp.bfloat16


def route(dx=0, dy=0, dz=0, dc=0, dl=0, dh=0):
    pairs = []
    for device in range(128):
        x, zl, core, y, zh = (int(v) for v in np.unravel_index(device, SIZES))
        z = (zh * 2 + zl + dz) % 4
        target = ((x + dx) % 4, z % 2 ^ dl, core ^ dc, (y + dy) % 4, z // 2 ^ dh)
        pairs.append((device, int(np.ravel_multi_index(target, SIZES))))
    return pairs


def send(value, **shift):
    return lax.ppermute(value, AXES, route(**shift))


def row_span(group, other):
    core = lax.axis_index("core")
    return pl.ds(pl.multiple_of(group * 96 + (1 - core if other else core) * ROWS, 16), ROWS)


def mm(left, right):
    return lax.dot_general(left, right, (((1,), (0,)), ((), ())), preferred_element_type=f32)


def mm_nt(left, right):
    return lax.dot_general(left, right, (((1,), (1,)), ((), ())), preferred_element_type=f32)


def normalize(values):
    center = values - jnp.mean(values, -1, keepdims=True)
    spread = jnp.mean(center * center, -1, keepdims=True)
    factor = lax.rsqrt(spread + 1e-05)
    return center * factor, factor


def norm_back(grad_normed, normed, factor):
    return factor * (
        grad_normed
        - jnp.mean(grad_normed, -1, keepdims=True)
        - normed * jnp.mean(grad_normed * normed, -1, keepdims=True)
    )


def split_low(values):
    high = values.astype(bf16)
    return high, (values - high.astype(f32)).astype(bf16)


SLICE = 768
KEYS, SMALL, QUERY, OUT, FC, PROJ, WIDE = 0, 128, 256, 1024, 1792, 4864, 7936
G_PROJ, G_QUERY, G_OUT, G_FC, G_WIDE = 256, 1024, 1792, 2560, 5632


def piece_kernel(*refs):
    vectors, fcb_ref, attn_ref, out_ref, fc_ref, proj_ref, piece_ref = (refs[:7],) + refs[7:]
    row = lax.broadcasted_iota(jnp.int32, (8, BLOCK), 0)
    lane = lax.broadcasted_iota(jnp.int32, (8, BLOCK), 1)
    small = jnp.zeros((8, BLOCK), f32)
    for i in range(6):
        values = [ref[i] for ref in vectors] + [fcb_ref[4 * i + j] for j in range(4)]
        for j, value in enumerate(values):
            small = jnp.where((row == i) & (lane < 48) & ((lane & 15) == j), value, small)
    high = small.astype(bf16).astype(f32)
    middle = (small - high).astype(bf16).astype(f32)
    low = small - high - middle
    small = jnp.where(lane < 16, high, jnp.where(lane < 32, middle, low)).astype(bf16)[:6]
    for k in range(8):
        piece_ref[k, :, KEYS:SMALL] = attn_ref[:, D:]
        piece_ref[k, :, SMALL:QUERY] = small
        piece_ref[k, :, QUERY:OUT] = attn_ref[:, :D]
        piece_ref[k, :, OUT:FC] = out_ref[...]
        piece_ref[k, :, FC:PROJ] = fc_ref[...]
        piece_ref[k, :, PROJ:] = proj_ref[...]


def block_kernel(piece_ref, attn_ref, feed_ref, rows):
    for j in range(8):
        rows[6 * j : 6 * j + 6] = piece_ref[j].astype(f32)
    for k in range(8):
        attn_ref[k] = rows[:, :FC].astype(bf16)
    feed_ref[...] = rows[:, FC:].astype(bf16)


def unblock_kernel(attn_ref, feed_ref, piece_ref, rows):
    rows[:, :G_OUT] = jnp.sum(attn_ref[...].astype(f32), 0)
    rows[:, G_OUT:] = feed_ref[...].astype(f32)
    for j in range(8):
        piece_ref[j] = rows[6 * j : 6 * j + 6].astype(bf16)


def finish_kernel(piece_ref, attn_ref, out_ref, fc_ref, proj_ref, *refs):
    vectors, fcb_ref, value_ref = refs[:7], refs[7], refs[8]
    total = jnp.sum(piece_ref[...].astype(f32), 0)
    attn_ref[:, :D] = total[:, G_QUERY:G_OUT]
    attn_ref[:, D:] = total[:, KEYS:SMALL]
    out_ref[...] = total[:, G_OUT:G_FC]
    fc_ref[...] = total[:, G_FC:]
    for j in range(4):
        proj_ref[:, j * SLICE : (j + 1) * SLICE] = (
            piece_ref[2 * j, :, G_PROJ:G_QUERY].astype(f32)
            + piece_ref[2 * j + 1, :, G_PROJ:G_QUERY].astype(f32)
        )
    small = total[:, SMALL:QUERY]
    small = jnp.concatenate([small, jnp.zeros((2, BLOCK), f32)], 0).T
    rows = small[:16] + small[16:32]
    for j, ref in enumerate(vectors):
        ref[...] = rows[j : j + 1, :6]
    spread = jnp.where(
        lax.broadcasted_iota(jnp.int32, (8, 24), 1) // 4
        == lax.broadcasted_iota(jnp.int32, (8, 24), 0),
        1.0,
        0.0,
    )
    wide = jnp.dot(rows[7:11], spread, precision=lax.Precision.HIGHEST)
    mine = lax.broadcasted_iota(jnp.int32, (4, 24), 1) % 4 == lax.broadcasted_iota(
        jnp.int32, (4, 24), 0
    )
    fcb_ref[...] = jnp.sum(jnp.where(mine, wide, 0.0), 0, keepdims=True)
    value_ref[...] = total[:4, SMALL + 32 : SMALL + 48] + total[:4, SMALL + 48 : SMALL + 64]


def four_apart(rows, columns, turned):
    return jnp.where(
        lax.broadcasted_iota(jnp.int32, (rows, columns), 1 - turned) // 4
        == lax.broadcasted_iota(jnp.int32, (rows, columns), turned),
        1.0,
        0.0,
    ).astype(bf16)


def first_kernel(
    x_ref, vbias_ref, mine_ref, other_ref, one_ref, kv_ref, vec_ref, fcb_ref, wq_ref, wout_ref, early_ref
):
    for k in range(8):
        for other, part in enumerate((mine_ref, other_ref)):
            span = row_span(k, other)
            early_ref[span, :] = part[k, :, :QUERY]
            wq_ref[span, :] = part[k, :, QUERY:OUT]
            wout_ref[span, :] = part[k, :, OUT:]
    turned = early_ref[:, BLOCK:].astype(f32).T
    vec = turned[0:16] + turned[16:32] + turned[32:48]
    vec_ref[...] = vec
    normed, _ = normalize(x_ref[...].astype(f32))
    one = (normed * vec[0:1] + vec[1:2]).astype(bf16)
    one_ref[...] = one
    bias = jnp.concatenate([jnp.zeros((1, HD), f32), vbias_ref[...]], 1)
    kv = (mm(one, early_ref[:, :BLOCK]) + bias).astype(bf16)
    for k in range(8):
        kv_ref[k] = kv
    spread = four_apart(BLOCK, 512, 0)
    terms = turned[0:48].astype(bf16)
    term = lax.broadcasted_iota(jnp.int32, (48, 512), 0) % 16 - 7
    mine = term == lax.broadcasted_iota(jnp.int32, (48, 512), 1) % 4
    for g in range(6):
        wide = mm(terms[:, g * BLOCK : (g + 1) * BLOCK], spread)
        fcb_ref[:, g * 512 : (g + 1) * 512] = jnp.sum(
            jnp.where(mine, wide, 0.0), 0, keepdims=True
        )


def read_plan(length_ref, order_ref, files_ref, inverse):
    for k in range(BLOCKS):
        inverse[order_ref[0, k]] = k
    files = files_ref[...]
    bounds = [jnp.sum(jnp.where(files < f, 1, 0)) for f in (1, 2, 3)]
    return length_ref[0], bounds


def block_plan(plan, order_ref, b):
    length, bounds = plan
    own = lax.axis_index("y") * 2 + lax.axis_index("zh")
    place = order_ref[0, own * 2 + b]
    start = place * BLOCK
    first = jnp.int32(0)
    for bound in bounds:
        first = jnp.where(bound <= start, jnp.maximum(first, bound), first)
    low = first // BLOCK
    high = jnp.minimum(place - 1, (length - 1) // BLOCK)
    return place, low, jnp.maximum(high - low + 1, 0) + 1


def block_bias(plan, place, initial):
    length, bounds = plan
    lane = lax.broadcasted_iota(jnp.int32, (1, 2 * BLOCK), 1)
    query = place * BLOCK + (lane & (BLOCK - 1))
    first = jnp.zeros_like(query)
    for bound in bounds:
        first = jnp.where(bound <= query, jnp.maximum(first, bound), first)
    last = jnp.minimum(query, length - 1)
    key = initial * BLOCK + lax.broadcasted_iota(jnp.int32, (BLOCK, 2 * BLOCK), 0)
    allowed = ((key >= first) & (key <= last)) | (key == query)
    return jnp.where(allowed, 0.0, NEG)


def fold_heads(block):
    turned = block.T
    return jnp.concatenate([turned[:HD], turned[HD:]], 1)


def unfold_heads(wide):
    return jnp.concatenate([wide[:, :BLOCK], wide[:, BLOCK:]], 0).T


def forward_kernel(
    length_ref,
    order_ref,
    files_ref,
    one_ref,
    wq_ref,
    vec_ref,
    kv_ref,
    q_ref,
    att_ref,
    lse_ref,
    inverse,
    qt,
    vt,
    scores,
    mixed,
):
    plan = read_plan(length_ref, order_ref, files_ref, inverse)
    q = (mm(one_ref[...], wq_ref[...]) + vec_ref[2:3]).astype(bf16)
    q_ref[...] = q
    for b in range(2):
        for p in range(PAIRS):
            block = q[b * BLOCK : (b + 1) * BLOCK, p * BLOCK : (p + 1) * BLOCK].astype(f32) * 0.125
            qt[b, p, :HD] = fold_heads(block).astype(bf16)
            qt[b, p, HD:] = jnp.zeros((HD, 2 * BLOCK), bf16)
    for k in range(BLOCKS):
        vt[k] = kv_ref[k * BLOCK : (k + 1) * BLOCK].astype(f32).T[HD:].astype(bf16)

    for b in range(2):
        place, low, count = block_plan(plan, order_ref, b)

        def initial_of(t):
            return jnp.where(t == count - 1, place, low + t)

        def score_step(t, tops):
            initial = initial_of(t)
            stored = inverse[initial]
            rows = kv_ref[pl.ds(pl.multiple_of(stored * BLOCK, BLOCK), BLOCK)]
            bias = block_bias(plan, place, initial)
            new = []
            for p in range(PAIRS):
                value = mm(rows, qt[b, p]) + bias
                scores[t, p] = value
                new.append(jnp.maximum(tops[p], jnp.max(value.reshape(16, 8, 2 * BLOCK), 0)))
            return tuple(new)

        tops = lax.fori_loop(
            0, count, score_step, tuple(jnp.full((8, 2 * BLOCK), NEG, f32) for _ in range(PAIRS))
        )
        tops = tuple(jnp.max(top, 0, keepdims=True) for top in tops)
        mixed[...] = jnp.zeros_like(mixed)

        def mix_step(t, sums):
            stored = inverse[initial_of(t)]
            values = vt[stored]
            new = []
            for p in range(PAIRS):
                weight = jnp.exp(scores[t, p] - tops[p])
                new.append(sums[p] + jnp.sum(weight.reshape(16, 8, 2 * BLOCK), 0))
                mixed[p] += mm(values, weight.astype(bf16))
            return tuple(new)

        sums = lax.fori_loop(
            0, count, mix_step, tuple(jnp.zeros((8, 2 * BLOCK), f32) for _ in range(PAIRS))
        )
        for p in range(PAIRS):
            total = jnp.sum(sums[p], 0, keepdims=True)
            lse_ref[b, p] = jnp.broadcast_to(tops[p] + jnp.log(total), (8, 2 * BLOCK))
            att_ref[b * BLOCK : (b + 1) * BLOCK, p * BLOCK : (p + 1) * BLOCK] = unfold_heads(
                mixed[p] / total
            ).astype(bf16)


def backward_kernel(
    length_ref, order_ref, files_ref, q_ref, do_ref, att_ref, lse_ref, one_ref, kv_ref, *refs
):
    gq_ref, keep_ref, send_ref, grad_ref = refs[:4]
    inverse, qt, dot_, qn, don, kt, delta, dq, dkv, gwq = refs[4:]
    plan = read_plan(length_ref, order_ref, files_ref, inverse)
    zeros = jnp.zeros((BLOCK, HD), f32)
    for b in range(2):
        for p in range(PAIRS):
            span = (slice(b * BLOCK, (b + 1) * BLOCK), slice(p * BLOCK, (p + 1) * BLOCK))
            block = q_ref[span].astype(f32) * 0.125
            grad = do_ref[span].astype(f32)
            out = att_ref[span].astype(f32)
            qt[b, p, :HD] = fold_heads(block).astype(bf16)
            qt[b, p, HD:] = jnp.zeros((HD, 2 * BLOCK), bf16)
            wide = fold_heads(grad)
            dot_[b, p, :HD] = jnp.zeros((HD, 2 * BLOCK), bf16)
            dot_[b, p, HD:] = wide.astype(bf16)
            delta[b, p] = jnp.broadcast_to(
                jnp.sum(wide * fold_heads(out), 0, keepdims=True), (8, 2 * BLOCK)
            )
            qn[b, p, :BLOCK] = jnp.concatenate([block[:, :HD], zeros], 1).astype(bf16)
            qn[b, p, BLOCK:] = jnp.concatenate([block[:, HD:], zeros], 1).astype(bf16)
            don[b, p, :BLOCK] = jnp.concatenate([zeros, grad[:, :HD]], 1).astype(bf16)
            don[b, p, BLOCK:] = jnp.concatenate([zeros, grad[:, HD:]], 1).astype(bf16)
    for k in range(BLOCKS):
        kt[k] = kv_ref[k * BLOCK : (k + 1) * BLOCK].astype(f32).T[:HD].astype(bf16)
    dkv[...] = jnp.zeros_like(dkv)

    for b in range(2):
        place, low, count = block_plan(plan, order_ref, b)
        dq[...] = jnp.zeros_like(dq)

        def step(t, carry):
            initial = jnp.where(t == count - 1, place, low + t)
            stored = inverse[initial]
            rows = kv_ref[pl.ds(pl.multiple_of(stored * BLOCK, BLOCK), BLOCK)]
            keys = kt[stored]
            bias = block_bias(plan, place, initial)
            total = dkv[stored]
            for p in range(PAIRS):
                value = mm(rows, qt[b, p]) + bias
                probs = jnp.exp(value - lse_ref[b, p, 0:1])
                grad = probs * (mm(rows, dot_[b, p]) - delta[b, p, 0:1])
                low_probs = probs.astype(bf16)
                low_grad = grad.astype(bf16)
                dq[p] += mm(keys, low_grad)
                total = total + mm(low_grad, qn[b, p]) + mm(low_probs, don[b, p])
            dkv[stored] = total
            return carry

        lax.fori_loop(0, count, step, 0)
        for p in range(PAIRS):
            gq_ref[b * BLOCK : (b + 1) * BLOCK, p * BLOCK : (p + 1) * BLOCK] = unfold_heads(
                dq[p] * 0.125
            ).astype(bf16)
    for k in range(BLOCKS):
        grad_ref[k] = dkv[k].astype(bf16)
    gwq[...] = mm(one_ref[...].astype(f32).T.astype(bf16), gq_ref[...]).astype(bf16)
    deal_rows(gwq, keep_ref, send_ref)


def deal_rows(source, keep_ref, send_ref):
    for k in range(8):
        keep_ref[k] = source[row_span(k, 0), :]
        send_ref[k] = source[row_span(k, 1), :]


def middle_kernel(
    feed_ref,
    wout_ref,
    x_ref,
    ct_ref,
    att_ref,
    vec_ref,
    fcb_ref,
    out_ref,
    gmid_ref,
    gatt_ref,
    sums_ref,
    hidden_ref,
    grad_ref,
    wf,
    wg,
    gf,
    in_sem,
    out_sem,
    last_sem,
    gout,
    x2,
    x2t,
    branch,
    gin,
    mid,
    fcsum,
):
    def columns(c, start=0):
        return pl.ds(pl.multiple_of(start + c * COLS, BLOCK), COLS)

    def loads(c, slot):
        return (
            pltpu.make_async_copy(feed_ref.at[:, columns(c)], wf.at[slot], in_sem.at[slot, 0]),
            pltpu.make_async_copy(feed_ref.at[:, columns(c, FF)], wg.at[slot], in_sem.at[slot, 1]),
        )

    def store(c, slot):
        return pltpu.make_async_copy(gf.at[slot], grad_ref.at[:, columns(c, D)], out_sem.at[slot])

    def start(copies):
        for copy in copies:
            copy.start()

    start(loads(0, 0))
    vec = vec_ref[...]
    att = att_ref[...]
    middle = x_ref[...].astype(f32) + (mm_nt(att, wout_ref[...]) + vec[3:4])
    mid[...] = middle
    normed, factor = normalize(middle)
    two = (normed * vec[4:5] + vec[5:6]).astype(bf16)
    x2[...] = two
    x2t[...] = two.astype(f32).T.astype(bf16)
    branch[...] = jnp.zeros_like(branch)
    gin[...] = jnp.zeros_like(gin)

    def chunk(c, carry):
        slot = lax.rem(c, 2)

        @pl.when(c + 1 < 8)
        def _():
            start(loads(c + 1, 1 - slot))

        for copy in loads(c, slot):
            copy.wait()
        span = columns(c)
        w_fc = wf[slot]
        w_proj = wg[slot]
        pre = mm(x2[...], w_fc) + fcb_ref[:, span]
        square = pre * pre
        tanh = jnp.tanh(0.7978845608028654 * (pre + 0.044715 * (pre * square)))
        half = 0.5 * (1.0 + tanh)
        hidden = (pre * half).astype(bf16)
        slope = half + (0.5 * pre) * (1.0 - tanh * tanh) * (
            0.7978845608028654 + (3 * 0.044715 * 0.7978845608028654) * square
        )
        hidden_ref[:, span] = hidden
        branch[...] += mm_nt(hidden, w_proj)
        grad_pre = (mm(ct_ref[...], w_proj) * slope).astype(bf16)
        gin[...] += mm_nt(grad_pre, w_fc)
        fcsum[:, span] = jnp.sum(grad_pre.astype(f32), 0, keepdims=True)

        @pl.when(c >= 2)
        def _():
            store(c - 2, slot).wait()

        gf[slot] = mm(x2t[...], grad_pre).astype(bf16)
        store(c, slot).start()
        return carry

    lax.fori_loop(0, 8, chunk, 0)
    middle = mid[...]
    cot = ct_ref[...].astype(f32)
    out_ref[...] = (middle + (branch[...] + vec[6:7])).astype(bf16)
    normed, factor = normalize(middle)
    grad_two = gin[...]
    grad_middle = cot + norm_back(grad_two * vec[4:5], normed, factor)
    gmid_ref[...] = grad_middle
    grad_branch = grad_middle.astype(bf16)
    gatt_ref[...] = mm(grad_branch, wout_ref[...]).astype(bf16)
    gout[...] = mm(grad_branch.astype(f32).T.astype(bf16), att).astype(bf16)
    out = pltpu.make_async_copy(gout, grad_ref.at[:, :D], last_sem)
    out.start()
    sums_ref[0:4] = jnp.concatenate(
        [
            jnp.sum(grad_branch.astype(f32), 0, keepdims=True),
            jnp.sum(grad_two * normed, 0, keepdims=True),
            jnp.sum(grad_two, 0, keepdims=True),
            jnp.sum(cot, 0, keepdims=True),
        ],
        0,
    )
    gather = four_apart(512, BLOCK, 1)
    mine = lax.broadcasted_iota(jnp.int32, (4, 512), 0) == (
        lax.broadcasted_iota(jnp.int32, (4, 512), 1) % 4
    )
    for g in range(6):
        high, low = split_low(jnp.where(mine, fcsum[:, g * 512 : (g + 1) * 512], 0.0))
        sums_ref[4:8, g * BLOCK : (g + 1) * BLOCK] = mm(high, gather) + mm(low, gather)
    store(6, 0).wait()
    store(7, 1).wait()
    out.wait()


def rest_kernel(ct_ref, hidden_ref, keep_ref, send_ref, turned, grad):
    turned[...] = ct_ref[...].astype(f32).T.astype(bf16)
    for j in range(4):
        grad[...] = mm(turned[...], hidden_ref[:, j * SLICE : (j + 1) * SLICE]).astype(bf16)
        deal_rows(grad, keep_ref.at[j], send_ref.at[j])


def last_kernel(
    x_ref,
    one_ref,
    gq_ref,
    gmid_ref,
    wq_ref,
    early_ref,
    vec_ref,
    sums_ref,
    dkv_ref,
    gx_ref,
    keep_ref,
    send_ref,
    pack_ref,
):
    gkv = jnp.sum(dkv_ref[...].astype(f32), 0).astype(bf16)
    gq = gq_ref[...]
    vec = vec_ref[...]
    grad_one = mm_nt(gq, wq_ref[...]) + mm_nt(gkv, early_ref[:, :BLOCK])
    normed, factor = normalize(x_ref[...].astype(f32))
    gx_ref[...] = (gmid_ref[...] + norm_back(grad_one * vec[0:1], normed, factor)).astype(bf16)
    pack_ref[:, :BLOCK] = mm(one_ref[...].astype(f32).T.astype(bf16), gkv).astype(bf16)
    sums = sums_ref[...]
    rows = jnp.concatenate(
        [
            jnp.sum(grad_one * normed, 0, keepdims=True),
            jnp.sum(grad_one, 0, keepdims=True),
            jnp.sum(gq.astype(f32), 0, keepdims=True),
            sums,
            jnp.zeros((5, D), f32),
        ],
        0,
    )
    high, low = split_low(rows)
    value = jnp.sum(gkv.astype(f32), 0, keepdims=True)[:, HD:]
    value_high, value_low = split_low(value)
    lane = lax.broadcasted_iota(jnp.int32, (16, HD), 1)
    mine = (lane & 15) == lax.broadcasted_iota(jnp.int32, (16, HD), 0)
    group = lax.broadcasted_iota(jnp.int32, (HD, D), 0) // 16
    spread = jnp.where(group == lax.broadcasted_iota(jnp.int32, (HD, D), 1) % 6, 1.0, 0.0).astype(bf16)
    put_high = mm(jnp.where(mine, value_high.astype(f32), 0.0).astype(bf16), spread)
    put_low = mm(jnp.where(mine, value_low.astype(f32), 0.0).astype(bf16), spread)
    packed = jnp.concatenate(
        [high.astype(f32), low.astype(f32), put_high, put_low, jnp.zeros((64, D), f32)], 0
    )
    pack_ref[:, BLOCK:] = packed.T.astype(bf16)
    deal_rows(pack_ref, keep_ref, send_ref)


SMEM = pl.BlockSpec(memory_space=pltpu.SMEM)
VMEM = pl.BlockSpec(memory_space=pltpu.VMEM)
ANY = pl.BlockSpec(memory_space=pl.ANY)


def shape(*dims, dtype=bf16):
    return jax.ShapeDtypeStruct(dims, dtype)


def add_all(parts, dtype=bf16):
    total = parts[0].astype(f32)
    for part in parts[1:]:
        total = total + part.astype(f32)
    return total.astype(dtype)


def call(kernel, name, outs, args, scratch=(), smem=0, hbm=(), hbm_out=0, flops=0, moved=0, exps=0):
    places = [SMEM if i < smem else ANY if i in hbm else VMEM for i in range(len(args))]
    return pl.pallas_call(
        kernel,
        out_shape=outs,
        in_specs=places,
        out_specs=[VMEM] * (len(outs) - hbm_out) + [ANY] * hbm_out,
        scratch_shapes=list(scratch),
        compiler_params=pltpu.CompilerParams(vmem_limit_bytes=56 * 1024 * 1024),
        cost_estimate=pl.CostEstimate(flops=flops, bytes_accessed=moved, transcendentals=exps),
        name=name,
    )(*args)


def tie(value, after):
    return lax.optimization_barrier((value, after))[0]


def local(
    layer_input,
    cotangent,
    lengths,
    order,
    files,
    ln1_gain,
    ln1_bias,
    w_attn,
    query_bias,
    value_bias,
    w_out,
    out_bias,
    ln2_gain,
    ln2_bias,
    w_fc,
    fc_bias,
    w_proj,
    proj_bias,
):
    x = layer_input[0]
    cot = cotangent[0]
    vectors = [ln1_gain, ln1_bias, query_bias, out_bias, ln2_gain, ln2_bias, proj_bias, fc_bias]
    (pieces,) = call(
        piece_kernel,
        "pieces",
        [shape(8, 6, WIDE)],
        [*vectors, w_attn, w_out, w_fc, w_proj],
        smem=8,
        moved=2_000_000,
    )
    attn_block, feed_block = call(
        block_kernel,
        "blocks",
        [shape(8, ROWS, FC), shape(ROWS, 2 * FF)],
        [lax.all_to_all(pieces, CTX, 0, 0)],
        [pltpu.VMEM((ROWS, WIDE), f32)],
        moved=4_000_000,
    )
    feed = lax.all_gather(feed_block, DP, axis=0, tiled=True)
    attn = lax.all_to_all(attn_block, ("x", "zl"), 0, 0)
    one, kv, vec, fcb, wq, wout, early = call(
        first_kernel,
        "first",
        [
            shape(TOK, D),
            shape(8, TOK, BLOCK),
            shape(16, D, dtype=f32),
            shape(1, FF, dtype=f32),
            shape(D, D),
            shape(D, D),
            shape(D, 2 * BLOCK),
        ],
        [x, value_bias[None], attn, send(attn, dc=1)],
        flops=100_000_000,
        moved=8_000_000,
    )
    kv = lax.all_to_all(kv, CTX, 0, 0).reshape(LENGTH, BLOCK)

    wide = (2, PAIRS, BLOCK, 2 * BLOCK)
    plan = [lengths, order, files]
    q, att, lse = call(
        forward_kernel,
        "attend",
        [shape(TOK, D), shape(TOK, D), shape(2, PAIRS, 8, 2 * BLOCK, dtype=f32)],
        [*plan, one, wq, vec, kv],
        [
            pltpu.SMEM((BLOCKS,), jnp.int32),
            pltpu.VMEM(wide, bf16),
            pltpu.VMEM((BLOCKS, HD, BLOCK), bf16),
            pltpu.VMEM((BLOCKS, PAIRS, BLOCK, 2 * BLOCK), f32),
            pltpu.VMEM((PAIRS, HD, 2 * BLOCK), f32),
        ],
        smem=2,
        flops=10_000_000_000,
        moved=4_000_000,
        exps=6_000_000,
    )
    output, grad_middle, grad_att, sums, hidden, grad_feed = call(
        middle_kernel,
        "feed",
        [
            shape(TOK, D),
            shape(TOK, D, dtype=f32),
            shape(TOK, D),
            shape(8, D, dtype=f32),
            shape(TOK, FF),
            shape(D, D + FF),
        ],
        [feed, wout, x, cot, att, vec, fcb],
        [
            pltpu.VMEM((2, D, COLS), bf16),
            pltpu.VMEM((2, D, COLS), bf16),
            pltpu.VMEM((2, D, COLS), bf16),
            pltpu.SemaphoreType.DMA((2, 2)),
            pltpu.SemaphoreType.DMA((2,)),
            pltpu.SemaphoreType.DMA,
            pltpu.VMEM((D, D), bf16),
            pltpu.VMEM((TOK, D), bf16),
            pltpu.VMEM((D, TOK), bf16),
            pltpu.VMEM((TOK, D), f32),
            pltpu.VMEM((TOK, D), f32),
            pltpu.VMEM((TOK, D), f32),
            pltpu.VMEM((1, FF), f32),
        ],
        hbm=(0,),
        hbm_out=1,
        flops=8_000_000_000,
        moved=30_000_000,
        exps=1_000_000,
    )
    grad_feed = lax.psum_scatter(grad_feed, DP, scatter_dimension=0, tiled=True)
    half = shape(8, ROWS, D)
    sliced = shape(4, 8, ROWS, SLICE)
    keep_proj, send_proj = call(
        rest_kernel,
        "rest",
        [sliced, sliced],
        [cot, hidden],
        [pltpu.VMEM((D, TOK), bf16), pltpu.VMEM((D, D), bf16)],
        flops=1_500_000_000,
        moved=8_000_000,
    )
    got_proj = send(send_proj, dc=1)
    grad_proj = add_all([keep_proj, got_proj])
    grad_att = tie(grad_att, grad_proj)
    grad_proj = add_all(list(lax.all_to_all(grad_proj, "y", 0, 0)))

    gq, keep_q, send_q, grad_kv = call(
        backward_kernel,
        "attend_back",
        [shape(TOK, D), half, half, shape(BLOCKS, BLOCK, BLOCK)],
        [*plan, q, grad_att, att, lse, one, kv],
        [
            pltpu.SMEM((BLOCKS,), jnp.int32),
            pltpu.VMEM(wide, bf16),
            pltpu.VMEM(wide, bf16),
            pltpu.VMEM((2, PAIRS, 2 * BLOCK, BLOCK), bf16),
            pltpu.VMEM((2, PAIRS, 2 * BLOCK, BLOCK), bf16),
            pltpu.VMEM((BLOCKS, HD, BLOCK), bf16),
            pltpu.VMEM((2, PAIRS, 8, 2 * BLOCK), f32),
            pltpu.VMEM((PAIRS, HD, 2 * BLOCK), f32),
            pltpu.VMEM((BLOCKS, BLOCK, BLOCK), f32),
            pltpu.VMEM((D, D), bf16),
        ],
        smem=2,
        flops=20_000_000_000,
        moved=6_000_000,
        exps=6_000_000,
    )
    grad_kv = tie(grad_kv.reshape(8, TOK, BLOCK), grad_proj)
    grad_kv = lax.all_to_all(grad_kv, CTX, 0, 0)
    grad_q = add_all([keep_q, send(send_q, dc=1)])

    thin = shape(8, ROWS, 2 * BLOCK)
    grad_x, keep_pack, send_pack = call(
        last_kernel,
        "last",
        [shape(TOK, D), thin, thin],
        [x, one, gq, grad_middle, wq, early, vec, sums, grad_kv],
        [pltpu.VMEM((D, 2 * BLOCK), bf16)],
        flops=1_000_000_000,
        moved=5_000_000,
    )
    grad_pack = add_all([keep_pack, send(send_pack, dc=1)])
    parts = [grad_pack, grad_proj, grad_q]
    both = lax.all_to_all(jnp.concatenate(parts, 2), ("x", "zl"), 0, 0)
    (pieces,) = call(
        unblock_kernel,
        "unblock",
        [shape(8, 6, G_WIDE)],
        [both, grad_feed],
        [pltpu.VMEM((ROWS, G_WIDE), f32)],
    )
    results = call(
        finish_kernel,
        "finish",
        [
            shape(6, D + BLOCK, dtype=f32),
            shape(6, D, dtype=f32),
            shape(6, FF, dtype=f32),
            shape(6, FF, dtype=f32),
        ]
        + [shape(1, 6, dtype=f32)] * 7
        + [shape(1, 24, dtype=f32), shape(4, 16, dtype=f32)],
        [lax.all_to_all(pieces, CTX, 0, 0)],
    )
    grad_w_attn, grad_w_out, grad_w_fc, grad_w_proj = results[:4]
    gain_one, bias_one, bias_query, bias_out, gain_two, bias_two, bias_proj, bias_fc = (
        value.reshape(-1) for value in results[4:12]
    )
    return (
        output[None],
        grad_x[None],
        gain_one,
        bias_one,
        grad_w_attn,
        bias_query,
        results[12].reshape(HD),
        grad_w_out,
        bias_out,
        gain_two,
        bias_two,
        grad_w_fc,
        bias_fc,
        grad_w_proj,
        bias_proj,
    )


def solution(mesh):
    cells = Mesh(mesh.devices.reshape(SIZES), AXES)
    every = P(AXES)
    tall = P(AXES, None)
    tokens = P(DP, CTX, None)
    in_specs = (
        tokens,
        tokens,
        P(DP),
        P(DP, None),
        P(DP, None),
        every,
        every,
        tall,
        every,
        P(),
        tall,
        every,
        every,
        every,
        tall,
        every,
        tall,
        every,
    )
    out_specs = (
        tokens,
        tokens,
        every,
        every,
        tall,
        every,
        P(),
        tall,
        every,
        every,
        every,
        tall,
        every,
        tall,
        every,
    )
    return jax.shard_map(local, mesh=cells, in_specs=in_specs, out_specs=out_specs, check_vma=False)
```

```python
import functools

import jax
import jax.numpy as jnp
import numpy as np
from jax import lax
from jax.experimental import pallas as pl
from jax.experimental.pallas import tpu as pltpu
from jax.sharding import Mesh
from jax.sharding import PartitionSpec as P

D = 768
HEADS = 12
HD = 64
FF = 3072
TOK = 256
LENGTH = 2048
BLOCK = 128
BLOCKS = 16
PAIRS = 6
ROWS = 48
COLS = 384
NEG = -1e30

AXES = ("x", "zl", "core", "y", "zh")
SIZES = (4, 2, 2, 4, 2)
DP = ("x", "zl", "core")
CTX = ("y", "zh")

f32 = jnp.float32
bf16 = jnp.bfloat16


def route(dx=0, dy=0, dz=0, dc=0, dl=0, dh=0):
    pairs = []
    for device in range(128):
        x, zl, core, y, zh = (int(v) for v in np.unravel_index(device, SIZES))
        z = (zh * 2 + zl + dz) % 4
        target = ((x + dx) % 4, z % 2 ^ dl, core ^ dc, (y + dy) % 4, z // 2 ^ dh)
        pairs.append((device, int(np.ravel_multi_index(target, SIZES))))
    return pairs


def send(value, **shift):
    return lax.ppermute(value, AXES, route(**shift))


def row_span(group, other):
    core = lax.axis_index("core")
    return pl.ds(pl.multiple_of(group * 96 + (1 - core if other else core) * ROWS, 16), ROWS)


def row_copies(parts, lanes, target, sem):
    return [
        pltpu.make_async_copy(part.at[k, :, lanes], target.at[row_span(k, other)], sem)
        for k in range(8)
        for other, part in enumerate(parts)
    ]


def start(copies):
    for copy in copies:
        copy.start()


def finish(copies):
    for copy in copies:
        copy.wait()


def mm(left, right):
    return lax.dot_general(left, right, (((1,), (0,)), ((), ())), preferred_element_type=f32)


def mm_nt(left, right):
    return lax.dot_general(left, right, (((1,), (1,)), ((), ())), preferred_element_type=f32)


def normalize(values):
    center = values - jnp.mean(values, -1, keepdims=True)
    spread = jnp.mean(center * center, -1, keepdims=True)
    factor = lax.rsqrt(spread + 1e-05)
    return center * factor, factor


def norm_back(grad_normed, normed, factor):
    return factor * (
        grad_normed
        - jnp.mean(grad_normed, -1, keepdims=True)
        - normed * jnp.mean(grad_normed * normed, -1, keepdims=True)
    )


def split_low(values):
    high = values.astype(bf16)
    return high, (values - high.astype(f32)).astype(bf16)


SLICE = 768
KEYS, SMALL, QUERY, OUT, FC, PROJ, WIDE = 0, 128, 256, 1024, 1792, 4864, 7936
SENT = 512
REST = SLICE - SENT
G_PROJ, G_QUERY, G_FC, G_OUT, G_REST, G_WIDE = 256, 768, 1536, 4608, 5376, 6400
REDUCED = G_WIDE - G_FC


def piece_kernel(*refs):
    vectors, fcb_ref, attn_ref, out_ref, fc_ref, proj_ref, piece_ref = (refs[:7],) + refs[7:]
    row = lax.broadcasted_iota(jnp.int32, (8, BLOCK), 0)
    lane = lax.broadcasted_iota(jnp.int32, (8, BLOCK), 1)
    small = jnp.zeros((8, BLOCK), f32)
    for i in range(6):
        values = [ref[i] for ref in vectors] + [fcb_ref[4 * i + j] for j in range(4)]
        for j, value in enumerate(values):
            small = jnp.where((row == i) & (lane < 48) & ((lane & 15) == j), value, small)
    high = small.astype(bf16).astype(f32)
    middle = (small - high).astype(bf16).astype(f32)
    low = small - high - middle
    small = jnp.where(lane < 16, high, jnp.where(lane < 32, middle, low)).astype(bf16)[:6]
    for k in range(8):
        piece_ref[k, :, KEYS:SMALL] = attn_ref[:, D:]
        piece_ref[k, :, SMALL:QUERY] = small
        piece_ref[k, :, QUERY:OUT] = attn_ref[:, :D]
        piece_ref[k, :, OUT:FC] = out_ref[...]
        piece_ref[k, :, FC:PROJ] = fc_ref[...]
        piece_ref[k, :, PROJ:] = proj_ref[...]


def block_kernel(piece_ref, attn_ref, feed_ref, rows):
    for j in range(8):
        rows[6 * j : 6 * j + 6] = piece_ref[j].astype(f32)
    for k in range(8):
        attn_ref[k] = rows[:, :FC].astype(bf16)
    feed_ref[...] = rows[:, FC:].astype(bf16)


def unblock_kernel(attn_ref, mine_ref, other_ref, piece_ref, rows):
    rows[:, :G_FC] = jnp.sum(attn_ref[...].astype(f32), 0)
    rows[:, G_FC:] = mine_ref[lax.axis_index("zl")].astype(f32) + other_ref[...].astype(f32)
    for j in range(8):
        piece_ref[j] = rows[6 * j : 6 * j + 6].astype(bf16)


def finish_kernel(piece_ref, attn_ref, out_ref, fc_ref, proj_ref, *refs):
    vectors, fcb_ref, value_ref = refs[:7], refs[7], refs[8]
    total = jnp.sum(piece_ref[...].astype(f32), 0)
    attn_ref[:, :D] = total[:, G_QUERY:G_FC]
    attn_ref[:, D:] = total[:, KEYS:SMALL]
    out_ref[...] = total[:, G_OUT:G_REST]
    fc_ref[...] = total[:, G_FC:G_OUT]
    for j in range(4):
        proj_ref[:, j * SLICE + SENT : (j + 1) * SLICE] = total[
            :, G_REST + j * REST : G_REST + (j + 1) * REST
        ]
        proj_ref[:, j * SLICE : j * SLICE + SENT] = (
            piece_ref[2 * j, :, G_PROJ:G_QUERY].astype(f32)
            + piece_ref[2 * j + 1, :, G_PROJ:G_QUERY].astype(f32)
        )
    small = total[:, SMALL:QUERY]
    small = jnp.concatenate([small, jnp.zeros((2, BLOCK), f32)], 0).T
    rows = small[:16] + small[16:32]
    for j, ref in enumerate(vectors):
        ref[...] = rows[j : j + 1, :6]
    spread = jnp.where(
        lax.broadcasted_iota(jnp.int32, (8, 24), 1) // 4
        == lax.broadcasted_iota(jnp.int32, (8, 24), 0),
        1.0,
        0.0,
    )
    wide = jnp.dot(rows[7:11], spread, precision=lax.Precision.HIGHEST)
    mine = lax.broadcasted_iota(jnp.int32, (4, 24), 1) % 4 == lax.broadcasted_iota(
        jnp.int32, (4, 24), 0
    )
    fcb_ref[...] = jnp.sum(jnp.where(mine, wide, 0.0), 0, keepdims=True)
    value = total[:4, SMALL + 32 : SMALL + 48] + total[:4, SMALL + 48 : SMALL + 64]
    value_ref[...] = jnp.concatenate([value[j : j + 1] for j in range(4)], 1)


def four_apart(rows, columns, turned):
    return jnp.where(
        lax.broadcasted_iota(jnp.int32, (rows, columns), 1 - turned) // 4
        == lax.broadcasted_iota(jnp.int32, (rows, columns), turned),
        1.0,
        0.0,
    ).astype(bf16)


def first_kernel(
    x_ref, vbias_ref, mine_ref, other_ref, one_ref, kv_ref, vec_ref, fcb_ref, early_ref, sem
):
    copies = row_copies((mine_ref, other_ref), pl.ds(0, QUERY), early_ref, sem)
    start(copies)
    normed, _ = normalize(x_ref[...].astype(f32))
    finish(copies)
    turned = early_ref[:, BLOCK:].astype(f32).T
    vec = turned[0:16] + turned[16:32] + turned[32:48]
    vec_ref[...] = vec
    one = (normed * vec[0:1] + vec[1:2]).astype(bf16)
    one_ref[...] = one
    bias = jnp.concatenate([jnp.zeros((1, HD), f32), vbias_ref[...]], 1)
    kv = (mm(one, early_ref[:, :BLOCK]) + bias).astype(bf16)
    for k in range(8):
        kv_ref[k] = kv
    spread = four_apart(BLOCK, 512, 0)
    terms = turned[0:48].astype(bf16)
    term = lax.broadcasted_iota(jnp.int32, (48, 512), 0) % 16 - 7
    mine = term == lax.broadcasted_iota(jnp.int32, (48, 512), 1) % 4
    for g in range(6):
        wide = mm(terms[:, g * BLOCK : (g + 1) * BLOCK], spread)
        fcb_ref[:, g * 512 : (g + 1) * 512] = jnp.sum(
            jnp.where(mine, wide, 0.0), 0, keepdims=True
        )


def read_plan(length_ref, order_ref, files_ref):
    files = files_ref[...]
    bounds = [jnp.sum(jnp.where(files < f, 1, 0)) for f in (1, 2, 3)]
    return length_ref[0], bounds


def block_plan(plan, order_ref, b):
    length, bounds = plan
    own = lax.axis_index("y") * 2 + lax.axis_index("zh")
    place = order_ref[0, own * 2 + b]
    start = place * BLOCK
    first = jnp.int32(0)
    for bound in bounds:
        first = jnp.where(bound <= start, jnp.maximum(first, bound), first)
    low = first // BLOCK
    high = jnp.minimum(place - 1, (length - 1) // BLOCK)
    return place, low, jnp.maximum(high - low + 1, 0)


def own_bias(plan, place):
    length, bounds = plan
    lane = lax.broadcasted_iota(jnp.int32, (1, 2 * BLOCK), 1)
    query = place * BLOCK + (lane & (BLOCK - 1))
    first = jnp.zeros_like(query)
    for bound in bounds:
        first = jnp.where(bound <= query, jnp.maximum(first, bound), first)
    last = jnp.minimum(query, length - 1)
    key = place * BLOCK + lax.broadcasted_iota(jnp.int32, (BLOCK, 2 * BLOCK), 0)
    allowed = ((key >= first) & (key <= last)) | (key == query)
    return jnp.where(allowed, 0.0, NEG)


def file_of(plan, position):
    number = jnp.zeros_like(position)
    for bound in plan[1]:
        number = number + jnp.where(bound <= position, 1, 0)
    return number


def place_keys(plan, order_ref, kv_ref, keys):
    lane = lax.broadcasted_iota(jnp.int32, (BLOCK, BLOCK), 1)

    def place(k, carry):
        start = pl.multiple_of(order_ref[0, k] * BLOCK, BLOCK)
        position = start + lax.broadcasted_iota(jnp.int32, (BLOCK, BLOCK), 0)
        mark = (file_of(plan, position) == lane) | ((position >= plan[0]) & (lane == 4))
        mark = mark | ((lane >= 5) & (lane < 8))
        keys[pl.ds(start, BLOCK), :BLOCK] = kv_ref[pl.ds(pl.multiple_of(k * BLOCK, BLOCK), BLOCK)]
        keys[pl.ds(start, BLOCK), BLOCK:] = jnp.where(mark, 1.0, 0.0).astype(bf16)
        return carry

    lax.fori_loop(0, BLOCKS, place, 0)


def own_keys(keys, place):
    rows = keys[pl.ds(pl.multiple_of(place * BLOCK, BLOCK), BLOCK)]
    lane = lax.broadcasted_iota(jnp.int32, rows.shape, 1)
    return jnp.where((lane >= BLOCK) & (lane < BLOCK + 5), jnp.zeros_like(rows), rows)


def query_marks(plan, place):
    lane = lax.broadcasted_iota(jnp.int32, (8, 2 * BLOCK), 1)
    number = file_of(plan, place * BLOCK + (lane & (BLOCK - 1)))
    mark = lax.broadcasted_iota(jnp.int32, (8, 2 * BLOCK), 0)
    return jnp.where(((mark < 4) & (mark != number)) | (mark == 4), NEG, 0.0)


def minus_terms(row):
    high = row.astype(bf16).astype(f32)
    middle = (row - high).astype(bf16).astype(f32)
    low = row - high - middle
    mark = lax.broadcasted_iota(jnp.int32, (8, row.shape[1]), 0)
    return jnp.where(
        mark == 5, -high, jnp.where(mark == 6, -middle, jnp.where(mark == 7, -low, 0.0))
    )


def fill(target, top, marks):
    target[:BLOCK] = top
    zeros = jnp.zeros((BLOCK - 8, 2 * BLOCK), f32)
    target[BLOCK:] = jnp.concatenate([marks, zeros], 0).astype(bf16)


def sweep(low, count, step):
    def four(t, carry):
        step(low + 4 * t, 4)
        return carry

    lax.fori_loop(0, count // 4, four, 0)

    @pl.when(lax.rem(count, 4) >= 2)
    def _():
        step(low + count // 4 * 4, 2)

    @pl.when(lax.rem(count, 2) == 1)
    def _():
        step(low + count - 1, 1)


def fold_heads(block):
    turned = block.T
    return jnp.concatenate([turned[:HD], turned[HD:]], 1)


def unfold_heads(wide):
    return jnp.concatenate([wide[:, :BLOCK], wide[:, BLOCK:]], 0).T


def eights(values):
    return values.reshape(values.shape[0] // 8, 8, values.shape[1])


def forward_kernel(
    length_ref,
    order_ref,
    files_ref,
    one_ref,
    vec_ref,
    kv_ref,
    mine_ref,
    other_ref,
    q_ref,
    att_ref,
    lse_ref,
    wq_ref,
    keys,
    qt,
    vt,
    scores,
    tops,
    sums,
    mixed,
    sem,
):
    copies = row_copies((mine_ref, other_ref), pl.ds(QUERY, D), wq_ref, sem)
    start(copies)
    plan = read_plan(length_ref, order_ref, files_ref)
    place_keys(plan, order_ref, kv_ref, keys)
    for k in range(BLOCKS):
        vt[:, k * BLOCK : (k + 1) * BLOCK] = (
            keys[k * BLOCK : (k + 1) * BLOCK, :BLOCK].T[HD:]
        )
    finish(copies)
    q = (mm(one_ref[...], wq_ref[...]) + vec_ref[2:3]).astype(bf16)
    q_ref[...] = q
    empty = jnp.zeros((HD, 2 * BLOCK), bf16)
    for b in range(2):
        place, low, count = block_plan(plan, order_ref, b)
        marks = query_marks(plan, place)
        for p in range(PAIRS):
            block = q[b * BLOCK : (b + 1) * BLOCK, p * BLOCK : (p + 1) * BLOCK] * 0.125
            fill(qt.at[p], jnp.concatenate([fold_heads(block), empty], 0), marks)
        own = own_keys(keys, place)
        bias = own_bias(plan, place)
        for p in range(PAIRS):
            value = mm(own, qt[p]) + bias
            scores[p, 0:BLOCK] = value
            tops[p] = jnp.max(eights(value), 0)

        def score_step(first, blocks):
            rows = keys[pl.ds(pl.multiple_of(first * BLOCK, BLOCK), blocks * BLOCK)]
            at = pl.ds(pl.multiple_of((first - low + 1) * BLOCK, BLOCK), blocks * BLOCK)
            for p in range(PAIRS):
                value = mm(rows, qt[p])
                scores[p, at] = value
                tops[p] = jnp.maximum(tops[p], jnp.max(eights(value), 0))

        sweep(low, count, score_step)
        peaks = [jnp.max(tops[p], 0, keepdims=True) for p in range(PAIRS)]
        for p in range(PAIRS):
            tops[p] = jnp.broadcast_to(peaks[p], (8, 2 * BLOCK))
            weight = jnp.exp(scores[p, 0:BLOCK] - peaks[p])
            sums[p] = jnp.sum(eights(weight), 0)
            span = pl.ds(pl.multiple_of(place * BLOCK, BLOCK), BLOCK)
            mixed[p] = mm(vt[:, span], weight.astype(bf16))

        def mix_step(first, blocks):
            span = pl.ds(pl.multiple_of(first * BLOCK, BLOCK), blocks * BLOCK)
            at = pl.ds(pl.multiple_of((first - low + 1) * BLOCK, BLOCK), blocks * BLOCK)
            values = vt[:, span]
            for p in range(PAIRS):
                weight = jnp.exp(scores[p, at] - tops[p, 0:1])
                sums[p] += jnp.sum(eights(weight), 0)
                mixed[p] += mm(values, weight.astype(bf16))

        sweep(low, count, mix_step)
        for p in range(PAIRS):
            total = jnp.sum(sums[p], 0, keepdims=True)
            lse_ref[b, p] = tops[p] + jnp.log(total)
            att_ref[b * BLOCK : (b + 1) * BLOCK, p * BLOCK : (p + 1) * BLOCK] = unfold_heads(
                (mixed[p] / total).astype(bf16)
            )


def backward_kernel(
    length_ref,
    order_ref,
    files_ref,
    q_ref,
    do_ref,
    att_ref,
    lse_ref,
    one_ref,
    kv_ref,
    gq_ref,
    keep_ref,
    send_ref,
    grad_ref,
    keys,
    qt,
    dot_,
    qd,
    both,
    kt,
    dq,
    dkv,
    gwq,
):
    plan = read_plan(length_ref, order_ref, files_ref)
    place_keys(plan, order_ref, kv_ref, keys)
    for k in range(BLOCKS):
        kt[:, k * BLOCK : (k + 1) * BLOCK] = (
            keys[k * BLOCK : (k + 1) * BLOCK, :BLOCK].T[:HD]
        )
    dkv[...] = jnp.zeros_like(dkv)
    zeros = jnp.zeros((BLOCK, HD), bf16)
    empty = jnp.zeros((HD, 2 * BLOCK), bf16)
    for b in range(2):
        place, low, count = block_plan(plan, order_ref, b)
        marks = query_marks(plan, place)
        for p in range(PAIRS):
            span = (slice(b * BLOCK, (b + 1) * BLOCK), slice(p * BLOCK, (p + 1) * BLOCK))
            block = q_ref[span] * 0.125
            grad = do_ref[span]
            wide = fold_heads(grad)
            out = fold_heads(att_ref[span]).astype(f32)
            delta = jnp.sum(wide.astype(f32) * out, 0, keepdims=True)
            top = jnp.concatenate([fold_heads(block), empty], 0)
            fill(qt.at[p], top, marks + minus_terms(lse_ref[b, p, 0:1]))
            fill(dot_.at[p], jnp.concatenate([empty, wide], 0), minus_terms(delta))
            factors = [
                jnp.concatenate([block[:, :HD], zeros], 1),
                jnp.concatenate([block[:, HD:], zeros], 1),
                jnp.concatenate([zeros, grad[:, :HD]], 1),
                jnp.concatenate([zeros, grad[:, HD:]], 1),
            ]
            qd[512 * p : 512 * (p + 1)] = jnp.concatenate(factors, 0)
        dq[...] = jnp.zeros_like(dq)

        def step(first, blocks, rows=None, bias=None):
            span = pl.ds(pl.multiple_of(first * BLOCK, BLOCK), blocks * BLOCK)
            rows = keys[span] if rows is None else rows
            turned = kt[:, span]
            size = blocks * BLOCK
            for p in range(PAIRS):
                value = mm(rows, qt[p])
                probs = jnp.exp(value if bias is None else value + bias)
                grad = (probs * mm(rows, dot_[p])).astype(bf16)
                dq[p] += mm(turned, grad)
                both[:size, 512 * p : 512 * p + 256] = grad
                both[:size, 512 * p + 256 : 512 * p + 512] = probs.astype(bf16)
            dkv[span] += mm(both[:size], qd[...])

        step(place, 1, own_keys(keys, place), own_bias(plan, place))
        sweep(low, count, step)
        for p in range(PAIRS):
            gq_ref[b * BLOCK : (b + 1) * BLOCK, p * BLOCK : (p + 1) * BLOCK] = unfold_heads(
                (dq[p] * 0.125).astype(bf16)
            )

    def give(k, carry):
        initial = order_ref[0, k]
        grad_ref[k] = dkv[pl.ds(pl.multiple_of(initial * BLOCK, BLOCK), BLOCK)].astype(bf16)
        return carry

    lax.fori_loop(0, BLOCKS, give, 0)
    gwq[...] = mm(one_ref[...].T, gq_ref[...]).astype(bf16)
    deal_rows(gwq, keep_ref, send_ref)


def deal_rows(source, keep_ref, send_ref):
    for k in range(8):
        keep_ref[k] = source[row_span(k, 0), :]
        send_ref[k] = source[row_span(k, 1), :]


def columns(c, first=0):
    return pl.ds(pl.multiple_of(first + c * SLICE, BLOCK), SLICE)


def middle_kernel(
    feed_ref,
    mine_ref,
    other_ref,
    x_ref,
    ct_ref,
    att_ref,
    vec_ref,
    fcb_ref,
    out_ref,
    gmid_ref,
    gatt_ref,
    sums_ref,
    keep_ref,
    send_ref,
    grad_ref,
    wf,
    wg,
    gf,
    gg,
    in_sem,
    out_sem,
    last_sem,
    wout,
    gout,
    x2,
    x2t,
    ctt,
    branch,
    gin,
    mid,
    fcsum,
):
    def loads(c, slot):
        return (
            pltpu.make_async_copy(feed_ref.at[:, columns(c)], wf.at[slot], in_sem.at[slot, 0]),
            pltpu.make_async_copy(feed_ref.at[:, columns(c, FF)], wg.at[slot], in_sem.at[slot, 1]),
        )

    def store(c, slot):
        for k in range(16):
            pltpu.make_async_copy(
                gf.at[slot, pl.ds(k * ROWS, ROWS)],
                grad_ref.at[k // 4, k % 2, k // 2 % 2, :, columns(c)],
                out_sem.at[slot, 0],
            ).start()
            pltpu.make_async_copy(
                gg.at[slot, pl.ds(k * ROWS, ROWS), pl.ds(SENT, REST)],
                grad_ref.at[
                    k // 4,
                    k % 2,
                    k // 2 % 2,
                    :,
                    pl.ds(pl.multiple_of(FF + D + c * REST, BLOCK), REST),
                ],
                out_sem.at[slot, 1],
            ).start()
        for k in range(8):
            for other, ref in enumerate((keep_ref, send_ref)):
                pltpu.make_async_copy(
                    gg.at[slot, row_span(k, other), pl.ds(0, SENT)],
                    ref.at[c, k],
                    out_sem.at[slot, 1],
                ).start()

    def stored(slot):
        pltpu.make_async_copy(gf.at[slot], gf.at[slot], out_sem.at[slot, 0]).wait()
        pltpu.make_async_copy(gg.at[slot], gg.at[slot], out_sem.at[slot, 1]).wait()

    copies = row_copies((mine_ref, other_ref), pl.ds(OUT, D), wout, last_sem)
    start(copies)
    start(loads(0, 0))
    ctt[...] = ct_ref[...].T
    branch[...] = jnp.zeros_like(branch)
    gin[...] = jnp.zeros_like(gin)
    vec = vec_ref[...]
    finish(copies)
    middle = x_ref[...].astype(f32) + (mm_nt(att_ref[...], wout[...]) + vec[3:4])
    mid[...] = middle
    normed, factor = normalize(middle)
    two = (normed * vec[4:5] + vec[5:6]).astype(bf16)
    x2[...] = two
    x2t[...] = two.T

    def chunk(c, carry):
        slot = lax.rem(c, 2)

        @pl.when(c < 3)
        def _():
            start(loads(c + 1, 1 - slot))

        finish(loads(c, slot))
        span = columns(c)
        pre = mm(x2[...], wf[slot]) + fcb_ref[:, span]
        grad_hidden = mm(ct_ref[...], wg[slot])
        square = pre * pre
        tanh = jnp.tanh(0.7978845608028654 * (pre + 0.044715 * (pre * square)))
        half = 0.5 * (1.0 + tanh)
        hidden = (pre * half).astype(bf16)
        slope = half + (0.5 * pre) * (1.0 - tanh * tanh) * (
            0.7978845608028654 + (3 * 0.044715 * 0.7978845608028654) * square
        )
        grad_pre = (grad_hidden * slope).astype(bf16)
        branch[...] += mm_nt(hidden, wg[slot])
        gin[...] += mm_nt(grad_pre, wf[slot])
        fcsum[:, span] = jnp.sum(grad_pre.astype(f32), 0, keepdims=True)

        @pl.when(c >= 2)
        def _():
            stored(slot)

        gf[slot] = mm(x2t[...], grad_pre).astype(bf16)
        gg[slot] = mm(ctt[...], hidden).astype(bf16)
        store(c, slot)
        return carry

    lax.fori_loop(0, 4, chunk, 0)
    middle = mid[...]
    cot = ct_ref[...].astype(f32)
    out_ref[...] = (middle + (branch[...] + vec[6:7])).astype(bf16)
    normed, factor = normalize(middle)
    grad_two = gin[...]
    grad_middle = cot + norm_back(grad_two * vec[4:5], normed, factor)
    gmid_ref[...] = grad_middle
    grad_branch = grad_middle.astype(bf16)
    gout[...] = mm(grad_branch.T, att_ref[...]).astype(bf16)
    outs = [
        pltpu.make_async_copy(
            gout.at[pl.ds(k * ROWS, ROWS)],
            grad_ref.at[k // 4, k % 2, k // 2 % 2, :, pl.ds(FF, D)],
            last_sem,
        )
        for k in range(16)
    ]
    start(outs)
    gatt_ref[...] = mm(grad_branch, wout[...]).astype(bf16)
    sums_ref[0:4] = jnp.concatenate(
        [
            jnp.sum(grad_branch.astype(f32), 0, keepdims=True),
            jnp.sum(grad_two * normed, 0, keepdims=True),
            jnp.sum(grad_two, 0, keepdims=True),
            jnp.sum(cot, 0, keepdims=True),
        ],
        0,
    )
    gather = four_apart(512, BLOCK, 1)
    mine = lax.broadcasted_iota(jnp.int32, (4, 512), 0) == (
        lax.broadcasted_iota(jnp.int32, (4, 512), 1) % 4
    )
    for g in range(6):
        high, low = split_low(jnp.where(mine, fcsum[:, g * 512 : (g + 1) * 512], 0.0))
        sums_ref[4:8, g * BLOCK : (g + 1) * BLOCK] = mm(high, gather) + mm(low, gather)
    stored(0)
    stored(1)
    finish(outs)


def last_kernel(
    x_ref,
    one_ref,
    gq_ref,
    gmid_ref,
    wq_ref,
    early_ref,
    vec_ref,
    sums_ref,
    dkv_ref,
    gx_ref,
    keep_ref,
    send_ref,
    pack_ref,
):
    gkv = jnp.sum(dkv_ref[...].astype(f32), 0).astype(bf16)
    gq = gq_ref[...]
    vec = vec_ref[...]
    grad_one = mm_nt(gq, wq_ref[...]) + mm_nt(gkv, early_ref[:, :BLOCK])
    normed, factor = normalize(x_ref[...].astype(f32))
    gx_ref[...] = (gmid_ref[...] + norm_back(grad_one * vec[0:1], normed, factor)).astype(bf16)
    pack_ref[:, :BLOCK] = mm(one_ref[...].astype(f32).T.astype(bf16), gkv).astype(bf16)
    sums = sums_ref[...]
    rows = jnp.concatenate(
        [
            jnp.sum(grad_one * normed, 0, keepdims=True),
            jnp.sum(grad_one, 0, keepdims=True),
            jnp.sum(gq.astype(f32), 0, keepdims=True),
            sums,
            jnp.zeros((5, D), f32),
        ],
        0,
    )
    high, low = split_low(rows)
    value = jnp.sum(gkv.astype(f32), 0, keepdims=True)[:, HD:]
    value_high, value_low = split_low(value)
    lane = lax.broadcasted_iota(jnp.int32, (16, HD), 1)
    mine = (lane & 15) == lax.broadcasted_iota(jnp.int32, (16, HD), 0)
    group = lax.broadcasted_iota(jnp.int32, (HD, D), 0) // 16
    spread = jnp.where(group == lax.broadcasted_iota(jnp.int32, (HD, D), 1) % 6, 1.0, 0.0).astype(bf16)
    put_high = mm(jnp.where(mine, value_high.astype(f32), 0.0).astype(bf16), spread)
    put_low = mm(jnp.where(mine, value_low.astype(f32), 0.0).astype(bf16), spread)
    packed = jnp.concatenate(
        [high.astype(f32), low.astype(f32), put_high, put_low, jnp.zeros((64, D), f32)], 0
    )
    pack_ref[:, BLOCK:] = packed.T.astype(bf16)
    deal_rows(pack_ref, keep_ref, send_ref)


SMEM = pl.BlockSpec(memory_space=pltpu.SMEM)
VMEM = pl.BlockSpec(memory_space=pltpu.VMEM)
ANY = pl.BlockSpec(memory_space=pl.ANY)


def shape(*dims, dtype=bf16):
    return jax.ShapeDtypeStruct(dims, dtype)


def add_all(parts, dtype=bf16):
    total = parts[0].astype(f32)
    for part in parts[1:]:
        total = total + part.astype(f32)
    return total.astype(dtype)


def call(kernel, name, outs, args, scratch=(), smem=0, hbm=(), hbm_out=0, flops=0, moved=0, exps=0):
    places = [SMEM if i < smem else ANY if i in hbm else VMEM for i in range(len(args))]
    return pl.pallas_call(
        kernel,
        out_shape=outs,
        in_specs=places,
        out_specs=[VMEM] * (len(outs) - hbm_out) + [ANY] * hbm_out,
        scratch_shapes=list(scratch),
        compiler_params=pltpu.CompilerParams(vmem_limit_bytes=56 * 1024 * 1024),
        cost_estimate=pl.CostEstimate(flops=flops, bytes_accessed=moved, transcendentals=exps),
        name=name,
    )(*args)


def tie(value, after):
    return lax.optimization_barrier((value, after))[0]


def local(
    layer_input,
    cotangent,
    lengths,
    order,
    files,
    ln1_gain,
    ln1_bias,
    w_attn,
    query_bias,
    value_bias,
    w_out,
    out_bias,
    ln2_gain,
    ln2_bias,
    w_fc,
    fc_bias,
    w_proj,
    proj_bias,
):
    x = layer_input[0]
    cot = cotangent[0]
    vectors = [ln1_gain, ln1_bias, query_bias, out_bias, ln2_gain, ln2_bias, proj_bias, fc_bias]
    (pieces,) = call(
        piece_kernel,
        "pieces",
        [shape(8, 6, WIDE)],
        [*vectors, w_attn, w_out, w_fc, w_proj],
        smem=8,
        moved=2_000_000,
    )
    attn_block, feed_block = call(
        block_kernel,
        "blocks",
        [shape(8, ROWS, FC), shape(ROWS, 2 * FF)],
        [lax.all_to_all(pieces, CTX, 0, 0)],
        [pltpu.VMEM((ROWS, WIDE), f32)],
        moved=4_000_000,
    )
    feed = lax.all_gather(feed_block, DP, axis=0, tiled=True)
    attn = lax.all_to_all(attn_block, ("x", "zl"), 0, 0)
    parts = [attn, send(attn, dc=1)]
    one, kv, vec, fcb, early = call(
        first_kernel,
        "first",
        [
            shape(TOK, D),
            shape(8, TOK, BLOCK),
            shape(16, D, dtype=f32),
            shape(1, FF, dtype=f32),
            shape(D, 2 * BLOCK),
        ],
        [x, value_bias[None], *parts],
        [pltpu.SemaphoreType.DMA],
        hbm=(2, 3),
        flops=100_000_000,
        moved=4_000_000,
    )
    kv = lax.all_to_all(kv, CTX, 0, 0).reshape(LENGTH, BLOCK)

    wide = (PAIRS, 2 * BLOCK, 2 * BLOCK)
    plan = [lengths, order, files]
    q, att, lse, wq = call(
        forward_kernel,
        "attend",
        [
            shape(TOK, D),
            shape(TOK, D),
            shape(2, PAIRS, 8, 2 * BLOCK, dtype=f32),
            shape(D, D),
        ],
        [*plan, one, vec, kv, *parts],
        [
            pltpu.VMEM((LENGTH, 2 * BLOCK), bf16),
            pltpu.VMEM(wide, bf16),
            pltpu.VMEM((HD, LENGTH), bf16),
            pltpu.VMEM((PAIRS, LENGTH, 2 * BLOCK), f32),
            pltpu.VMEM((PAIRS, 8, 2 * BLOCK), f32),
            pltpu.VMEM((PAIRS, 8, 2 * BLOCK), f32),
            pltpu.VMEM((PAIRS, HD, 2 * BLOCK), f32),
            pltpu.SemaphoreType.DMA,
        ],
        smem=2,
        hbm=(6, 7),
        flops=10_000_000_000,
        moved=4_000_000,
        exps=6_000_000,
    )
    half = shape(8, ROWS, D)
    sliced = shape(4, 8, ROWS, SENT)
    output, grad_middle, grad_att, sums, keep_proj, send_proj, grad_fc = call(
        middle_kernel,
        "feed",
        [
            shape(TOK, D),
            shape(TOK, D, dtype=f32),
            shape(TOK, D),
            shape(8, D, dtype=f32),
            sliced,
            sliced,
            shape(4, 2, 2, ROWS, REDUCED),
        ],
        [feed, *parts, x, cot, att, vec, fcb],
        [
            pltpu.VMEM((2, D, SLICE), bf16),
            pltpu.VMEM((2, D, SLICE), bf16),
            pltpu.VMEM((2, D, SLICE), bf16),
            pltpu.VMEM((2, D, SLICE), bf16),
            pltpu.SemaphoreType.DMA((2, 2)),
            pltpu.SemaphoreType.DMA((2, 2)),
            pltpu.SemaphoreType.DMA,
            pltpu.VMEM((D, D), bf16),
            pltpu.VMEM((D, D), bf16),
            pltpu.VMEM((TOK, D), bf16),
            pltpu.VMEM((D, TOK), bf16),
            pltpu.VMEM((D, TOK), bf16),
            pltpu.VMEM((TOK, D), f32),
            pltpu.VMEM((TOK, D), f32),
            pltpu.VMEM((TOK, D), f32),
            pltpu.VMEM((1, FF), f32),
        ],
        hbm=(0, 1, 2),
        hbm_out=3,
        flops=8_000_000_000,
        moved=30_000_000,
        exps=1_000_000,
    )
    grad_fc = grad_fc.reshape(8, 2, ROWS, REDUCED)
    grad_fc = lax.psum_scatter(grad_fc, ("x", "core"), scatter_dimension=0, tiled=True)[0]
    grad_proj = add_all([keep_proj, send(send_proj, dc=1)])
    grad_att = tie(grad_att, grad_proj)
    grad_proj = add_all(list(lax.all_to_all(grad_proj, "y", 0, 0)))

    gq, keep_q, send_q, grad_kv = call(
        backward_kernel,
        "attend_back",
        [shape(TOK, D), half, half, shape(BLOCKS, BLOCK, BLOCK)],
        [*plan, q, grad_att, att, lse, one, kv],
        [
            pltpu.VMEM((LENGTH, 2 * BLOCK), bf16),
            pltpu.VMEM(wide, bf16),
            pltpu.VMEM(wide, bf16),
            pltpu.VMEM((PAIRS * 4 * BLOCK, BLOCK), bf16),
            pltpu.VMEM((4 * BLOCK, PAIRS * 4 * BLOCK), bf16),
            pltpu.VMEM((HD, LENGTH), bf16),
            pltpu.VMEM((PAIRS, HD, 2 * BLOCK), f32),
            pltpu.VMEM((LENGTH, BLOCK), f32),
            pltpu.VMEM((D, D), bf16),
        ],
        smem=2,
        flops=20_000_000_000,
        moved=6_000_000,
        exps=6_000_000,
    )
    grad_q = add_all([keep_q, send(send_q, dc=1)])
    grad_kv = tie(grad_kv.reshape(8, TOK, BLOCK), grad_proj)
    grad_kv = lax.all_to_all(grad_kv, CTX, 0, 0)

    grad_fc = tie(grad_fc, grad_kv)
    other_fc = lax.dynamic_index_in_dim(grad_fc, 1 - lax.axis_index("zl"), 0, False)
    other_fc = send(other_fc, dl=1)
    small = shape(8, ROWS, 2 * BLOCK)
    grad_x, keep_pack, send_pack = call(
        last_kernel,
        "last",
        [shape(TOK, D), small, small],
        [x, one, gq, grad_middle, wq, early, vec, sums, grad_kv],
        [pltpu.VMEM((D, 2 * BLOCK), bf16)],
        flops=1_000_000_000,
        moved=5_000_000,
    )
    grad_pack = add_all([keep_pack, send(send_pack, dc=1)])
    both = jnp.concatenate([tie(grad_pack, other_fc), grad_proj, grad_q], 2)
    both = lax.all_to_all(both, ("x", "zl"), 0, 0)
    (pieces,) = call(
        unblock_kernel,
        "unblock",
        [shape(8, 6, G_WIDE)],
        [both, grad_fc, other_fc],
        [pltpu.VMEM((ROWS, G_WIDE), f32)],
    )
    results = call(
        finish_kernel,
        "finish",
        [
            shape(6, D + BLOCK, dtype=f32),
            shape(6, D, dtype=f32),
            shape(6, FF, dtype=f32),
            shape(6, FF, dtype=f32),
        ]
        + [shape(1, 6, dtype=f32)] * 7
        + [shape(1, 24, dtype=f32), shape(1, HD, dtype=f32)],
        [lax.all_to_all(pieces, CTX, 0, 0)],
    )
    grad_w_attn, grad_w_out, grad_w_fc, grad_w_proj = results[:4]
    gain_one, bias_one, bias_query, bias_out, gain_two, bias_two, bias_proj, bias_fc = (
        value.reshape(-1) for value in results[4:12]
    )
    return (
        output[None],
        grad_x[None],
        gain_one,
        bias_one,
        grad_w_attn,
        bias_query,
        results[12].reshape(HD),
        grad_w_out,
        bias_out,
        gain_two,
        bias_two,
        grad_w_fc,
        bias_fc,
        grad_w_proj,
        bias_proj,
    )


def solution(mesh):
    cells = Mesh(mesh.devices.reshape(SIZES), AXES)
    every = P(AXES)
    tall = P(AXES, None)
    tokens = P(DP, CTX, None)
    in_specs = (
        tokens,
        tokens,
        P(DP),
        P(DP, None),
        P(DP, None),
        every,
        every,
        tall,
        every,
        P(),
        tall,
        every,
        every,
        every,
        tall,
        every,
        tall,
        every,
    )
    out_specs = (
        tokens,
        tokens,
        every,
        every,
        tall,
        every,
        P(),
        tall,
        every,
        every,
        every,
        tall,
        every,
        tall,
        every,
    )
    return jax.shard_map(local, mesh=cells, in_specs=in_specs, out_specs=out_specs, check_vma=False)
```

```python
import functools

import jax
import jax.numpy as jnp
import numpy as np
from jax import lax
from jax.experimental import pallas as pl
from jax.experimental.pallas import tpu as pltpu
from jax.sharding import Mesh
from jax.sharding import PartitionSpec as P

D = 768
HEADS = 12
HD = 64
FF = 3072
TOK = 256
LENGTH = 2048
BLOCK = 128
BLOCKS = 16
PAIRS = 6
ROWS = 48
COLS = 384
NEG = -1e30

AXES = ("x", "zl", "core", "y", "zh")
SIZES = (4, 2, 2, 4, 2)
DP = ("x", "zl", "core")
CTX = ("y", "zh")

f32 = jnp.float32
bf16 = jnp.bfloat16


def route(dx=0, dy=0, dz=0, dc=0, dl=0, dh=0):
    pairs = []
    for device in range(128):
        x, zl, core, y, zh = (int(v) for v in np.unravel_index(device, SIZES))
        z = (zh * 2 + zl + dz) % 4
        target = ((x + dx) % 4, z % 2 ^ dl, core ^ dc, (y + dy) % 4, z // 2 ^ dh)
        pairs.append((device, int(np.ravel_multi_index(target, SIZES))))
    return pairs


def send(value, **shift):
    return lax.ppermute(value, AXES, route(**shift))


def row_span(group, other):
    core = lax.axis_index("core")
    return pl.ds(pl.multiple_of(group * 96 + (1 - core if other else core) * ROWS, 16), ROWS)


def row_copies(parts, lanes, target, sem):
    return [
        pltpu.make_async_copy(part.at[k, :, lanes], target.at[row_span(k, other)], sem)
        for k in range(8)
        for other, part in enumerate(parts)
    ]


def start(copies):
    for copy in copies:
        copy.start()


def finish(copies):
    for copy in copies:
        copy.wait()


def mm(left, right):
    return lax.dot_general(left, right, (((1,), (0,)), ((), ())), preferred_element_type=f32)


def mm_nt(left, right):
    return lax.dot_general(left, right, (((1,), (1,)), ((), ())), preferred_element_type=f32)


def normalize(values):
    center = values - jnp.mean(values, -1, keepdims=True)
    spread = jnp.mean(center * center, -1, keepdims=True)
    factor = lax.rsqrt(spread + 1e-05)
    return center * factor, factor


def norm_back(grad_normed, normed, factor):
    return factor * (
        grad_normed
        - jnp.mean(grad_normed, -1, keepdims=True)
        - normed * jnp.mean(grad_normed * normed, -1, keepdims=True)
    )


def split_low(values):
    high = values.astype(bf16)
    return high, (values - high.astype(f32)).astype(bf16)


SLICE = 768
KEYS, SMALL, QUERY, OUT, FC, PROJ, WIDE = 0, 128, 256, 1024, 1792, 4864, 8192
FOLD = WIDE // 4
SENT = 128
REST = SLICE - SENT
G_PROJ, G_QUERY, G_FC, G_OUT, G_REST, G_WIDE = 256, 384, 1152, 4224, 4992, 7552
G_FOLD = (G_WIDE + 511) // 512 * BLOCK
REDUCED = G_WIDE - G_FC


def piece_kernel(*refs):
    vectors, fcb_ref, attn_ref, out_ref, fc_ref, proj_ref, piece_ref, row = (
        refs[:7],
    ) + refs[7:]
    line = lax.broadcasted_iota(jnp.int32, (8, BLOCK), 0)
    lane = lax.broadcasted_iota(jnp.int32, (8, BLOCK), 1)
    small = jnp.zeros((8, BLOCK), f32)
    for i in range(6):
        values = [ref[i] for ref in vectors] + [fcb_ref[4 * i + j] for j in range(4)]
        for j, value in enumerate(values):
            small = jnp.where((line == i) & (lane < 48) & ((lane & 15) == j), value, small)
    high = small.astype(bf16).astype(f32)
    middle = (small - high).astype(bf16).astype(f32)
    low = small - high - middle
    small = jnp.where(lane < 16, high, jnp.where(lane < 32, middle, low))[:6]
    row[:, KEYS:SMALL] = attn_ref[:, D:].astype(f32)
    row[:, SMALL:QUERY] = small
    row[:, QUERY:OUT] = attn_ref[:, :D].astype(f32)
    row[:, OUT:FC] = out_ref[...].astype(f32)
    row[:, FC:PROJ] = fc_ref[...].astype(f32)
    row[:, PROJ : PROJ + FF] = proj_ref[...].astype(f32)
    row[:, PROJ + FF :] = jnp.zeros((6, WIDE - PROJ - FF), f32)
    quarters = [row[:, k * FOLD : (k + 1) * FOLD] for k in range(4)]
    piece = jnp.concatenate(quarters, 0).astype(bf16)

    def copy(k, carry):
        piece_ref[k] = piece
        return carry

    lax.fori_loop(0, 16, copy, 0)


def block_kernel(piece_ref, attn_ref, feed_ref, rows):
    for j in range(16):
        piece = piece_ref[j].astype(f32)
        for k in range(4):
            rows[6 * j : 6 * j + 6, k * FOLD : (k + 1) * FOLD] = piece[6 * k : 6 * k + 6]
    for k in range(4):
        attn_ref[k] = rows[:, :FC].astype(bf16)
    feed_ref[...] = rows[:, FC : FC + 2 * FF].astype(bf16)


def fold_lanes(rows):
    width = rows.shape[1] // 4
    return jnp.concatenate([rows[:, k * width : (k + 1) * width] for k in range(4)], 0)


def unblock_kernel(attn_ref, feed_ref, piece_ref, rows):
    rows[:, :G_FC] = jnp.sum(attn_ref[...].astype(f32), 0)
    for zl in range(2):
        rows[zl * ROWS : (zl + 1) * ROWS, G_FC:G_WIDE] = feed_ref[zl].astype(f32)
    if G_WIDE < 4 * G_FOLD:
        rows[:, G_WIDE:] = jnp.zeros((2 * ROWS, 4 * G_FOLD - G_WIDE), f32)
    for j in range(16):
        piece_ref[j] = fold_lanes(rows[6 * j : 6 * j + 6]).astype(bf16)


def finish_kernel(piece_ref, attn_ref, out_ref, fc_ref, proj_ref, *refs):
    vectors, fcb_ref, value_ref, rows = refs[:7], refs[7], refs[8], refs[9]
    total = jnp.sum(piece_ref[...].astype(f32), 0)
    for k in range(4):
        rows[:, k * G_FOLD : (k + 1) * G_FOLD] = total[6 * k : 6 * k + 6]
    total = rows[...]
    attn_ref[:, :D] = total[:, G_QUERY:G_FC]
    attn_ref[:, D:] = total[:, KEYS:SMALL]
    fc_ref[...] = total[:, G_FC:G_OUT]
    out_ref[...] = total[:, G_OUT:G_REST]
    for j in range(4):
        sent = [piece_ref[k, :6, G_PROJ:G_QUERY].astype(f32) for k in (2 * j, 2 * j + 1, 2 * j + 8, 2 * j + 9)]
        proj_ref[:, j * SLICE : j * SLICE + SENT] = sent[0] + sent[1] + sent[2] + sent[3]
        proj_ref[:, j * SLICE + SENT : (j + 1) * SLICE] = total[
            :, G_REST + j * REST : G_REST + (j + 1) * REST
        ]
    small = total[:, SMALL:QUERY]
    small = jnp.concatenate([small, jnp.zeros((2, BLOCK), f32)], 0).T
    rows = small[:16] + small[16:32]
    for j, ref in enumerate(vectors):
        ref[...] = rows[j : j + 1, :6]
    spread = jnp.where(
        lax.broadcasted_iota(jnp.int32, (8, 24), 1) // 4
        == lax.broadcasted_iota(jnp.int32, (8, 24), 0),
        1.0,
        0.0,
    )
    wide = jnp.dot(rows[7:11], spread, precision=lax.Precision.HIGHEST)
    mine = lax.broadcasted_iota(jnp.int32, (4, 24), 1) % 4 == lax.broadcasted_iota(
        jnp.int32, (4, 24), 0
    )
    fcb_ref[...] = jnp.sum(jnp.where(mine, wide, 0.0), 0, keepdims=True)
    value = total[:4, SMALL + 32 : SMALL + 48] + total[:4, SMALL + 48 : SMALL + 64]
    value_ref[...] = jnp.concatenate([value[j : j + 1] for j in range(4)], 1)


def four_apart(rows, columns, turned):
    return jnp.where(
        lax.broadcasted_iota(jnp.int32, (rows, columns), 1 - turned) // 4
        == lax.broadcasted_iota(jnp.int32, (rows, columns), turned),
        1.0,
        0.0,
    ).astype(bf16)


def first_kernel(
    x_ref, vbias_ref, mine_ref, other_ref, one_ref, kv_ref, vec_ref, fcb_ref, early_ref, sem
):
    copies = row_copies((mine_ref, other_ref), pl.ds(0, QUERY), early_ref, sem)
    start(copies)
    normed, _ = normalize(x_ref[...].astype(f32))
    finish(copies)
    turned = early_ref[:, BLOCK:].astype(f32).T
    vec = turned[0:16] + turned[16:32] + turned[32:48]
    vec_ref[...] = vec
    one = (normed * vec[0:1] + vec[1:2]).astype(bf16)
    one_ref[...] = one
    bias = jnp.concatenate([jnp.zeros((1, HD), f32), vbias_ref[...]], 1)
    kv = (mm(one, early_ref[:, :BLOCK]) + bias).astype(bf16)
    for k in range(8):
        kv_ref[k] = kv
    spread = four_apart(BLOCK, 512, 0)
    terms = turned[0:48].astype(bf16)
    term = lax.broadcasted_iota(jnp.int32, (48, 512), 0) % 16 - 7
    mine = term == lax.broadcasted_iota(jnp.int32, (48, 512), 1) % 4
    for g in range(6):
        wide = mm(terms[:, g * BLOCK : (g + 1) * BLOCK], spread)
        fcb_ref[:, g * 512 : (g + 1) * 512] = jnp.sum(
            jnp.where(mine, wide, 0.0), 0, keepdims=True
        )


def read_plan(length_ref, order_ref, files_ref):
    files = files_ref[...]
    bounds = [jnp.sum(jnp.where(files < f, 1, 0)) for f in (1, 2, 3)]
    return length_ref[0], bounds


def block_plan(plan, order_ref, b):
    length, bounds = plan
    own = lax.axis_index("y") * 2 + lax.axis_index("zh")
    place = order_ref[0, own * 2 + b]
    start = place * BLOCK
    first = jnp.int32(0)
    for bound in bounds:
        first = jnp.where(bound <= start, jnp.maximum(first, bound), first)
    low = first // BLOCK
    high = jnp.minimum(place - 1, (length - 1) // BLOCK)
    return place, low, jnp.maximum(high - low + 1, 0)


def own_bias(plan, place):
    length, bounds = plan
    lane = lax.broadcasted_iota(jnp.int32, (1, 2 * BLOCK), 1)
    query = place * BLOCK + (lane & (BLOCK - 1))
    first = jnp.zeros_like(query)
    for bound in bounds:
        first = jnp.where(bound <= query, jnp.maximum(first, bound), first)
    last = jnp.minimum(query, length - 1)
    key = place * BLOCK + lax.broadcasted_iota(jnp.int32, (BLOCK, 2 * BLOCK), 0)
    allowed = ((key >= first) & (key <= last)) | (key == query)
    return jnp.where(allowed, 0.0, NEG)


def file_of(plan, position):
    number = jnp.zeros_like(position)
    for bound in plan[1]:
        number = number + jnp.where(bound <= position, 1, 0)
    return number


def place_keys(plan, order_ref, kv_ref, keys):
    lane = lax.broadcasted_iota(jnp.int32, (BLOCK, BLOCK), 1)

    def place(k, carry):
        start = pl.multiple_of(order_ref[0, k] * BLOCK, BLOCK)
        position = start + lax.broadcasted_iota(jnp.int32, (BLOCK, BLOCK), 0)
        mark = (file_of(plan, position) == lane) | ((position >= plan[0]) & (lane == 4))
        mark = mark | ((lane >= 5) & (lane < 8))
        keys[pl.ds(start, BLOCK), :BLOCK] = kv_ref[pl.ds(pl.multiple_of(k * BLOCK, BLOCK), BLOCK)]
        keys[pl.ds(start, BLOCK), BLOCK:] = jnp.where(mark, 1.0, 0.0).astype(bf16)
        return carry

    lax.fori_loop(0, BLOCKS, place, 0)


def own_keys(keys, place):
    rows = keys[pl.ds(pl.multiple_of(place * BLOCK, BLOCK), BLOCK)]
    lane = lax.broadcasted_iota(jnp.int32, rows.shape, 1)
    return jnp.where((lane >= BLOCK) & (lane < BLOCK + 5), jnp.zeros_like(rows), rows)


def query_marks(plan, place):
    lane = lax.broadcasted_iota(jnp.int32, (8, 2 * BLOCK), 1)
    number = file_of(plan, place * BLOCK + (lane & (BLOCK - 1)))
    mark = lax.broadcasted_iota(jnp.int32, (8, 2 * BLOCK), 0)
    return jnp.where(((mark < 4) & (mark != number)) | (mark == 4), NEG, 0.0)


def minus_terms(row):
    high = row.astype(bf16).astype(f32)
    middle = (row - high).astype(bf16).astype(f32)
    low = row - high - middle
    mark = lax.broadcasted_iota(jnp.int32, (8, row.shape[1]), 0)
    return jnp.where(
        mark == 5, -high, jnp.where(mark == 6, -middle, jnp.where(mark == 7, -low, 0.0))
    )


def fill(target, top, marks):
    target[:BLOCK] = top
    zeros = jnp.zeros((BLOCK - 8, 2 * BLOCK), f32)
    target[BLOCK:] = jnp.concatenate([marks, zeros], 0).astype(bf16)


def sweep(low, count, step):
    def four(t, carry):
        step(low + 4 * t, 4)
        return carry

    lax.fori_loop(0, count // 4, four, 0)

    @pl.when(lax.rem(count, 4) >= 2)
    def _():
        step(low + count // 4 * 4, 2)

    @pl.when(lax.rem(count, 2) == 1)
    def _():
        step(low + count - 1, 1)


def fold_heads(block):
    turned = block.T
    return jnp.concatenate([turned[:HD], turned[HD:]], 1)


def unfold_heads(wide):
    return jnp.concatenate([wide[:, :BLOCK], wide[:, BLOCK:]], 0).T


def eights(values):
    return values.reshape(values.shape[0] // 8, 8, values.shape[1])


def forward_kernel(
    length_ref,
    order_ref,
    files_ref,
    one_ref,
    vec_ref,
    kv_ref,
    mine_ref,
    other_ref,
    q_ref,
    att_ref,
    lse_ref,
    wq_ref,
    keys,
    qt,
    vt,
    scores,
    tops,
    sums,
    mixed,
    sem,
):
    copies = row_copies((mine_ref, other_ref), pl.ds(QUERY, D), wq_ref, sem)
    start(copies)
    plan = read_plan(length_ref, order_ref, files_ref)
    place_keys(plan, order_ref, kv_ref, keys)
    for k in range(BLOCKS):
        vt[:, k * BLOCK : (k + 1) * BLOCK] = (
            keys[k * BLOCK : (k + 1) * BLOCK, :BLOCK].T[HD:]
        )
    finish(copies)
    q = (mm(one_ref[...], wq_ref[...]) + vec_ref[2:3]).astype(bf16)
    q_ref[...] = q
    empty = jnp.zeros((HD, 2 * BLOCK), bf16)
    for b in range(2):
        place, low, count = block_plan(plan, order_ref, b)
        marks = query_marks(plan, place)
        for p in range(PAIRS):
            block = q[b * BLOCK : (b + 1) * BLOCK, p * BLOCK : (p + 1) * BLOCK] * 0.125
            fill(qt.at[p], jnp.concatenate([fold_heads(block), empty], 0), marks)
        own = own_keys(keys, place)
        bias = own_bias(plan, place)
        for p in range(PAIRS):
            value = mm(own, qt[p]) + bias
            scores[p, 0:BLOCK] = value
            tops[p] = jnp.max(eights(value), 0)

        def score_step(first, blocks):
            rows = keys[pl.ds(pl.multiple_of(first * BLOCK, BLOCK), blocks * BLOCK)]
            at = pl.ds(pl.multiple_of((first - low + 1) * BLOCK, BLOCK), blocks * BLOCK)
            for p in range(PAIRS):
                value = mm(rows, qt[p])
                scores[p, at] = value
                tops[p] = jnp.maximum(tops[p], jnp.max(eights(value), 0))

        sweep(low, count, score_step)
        peaks = [jnp.max(tops[p], 0, keepdims=True) for p in range(PAIRS)]
        for p in range(PAIRS):
            tops[p] = jnp.broadcast_to(peaks[p], (8, 2 * BLOCK))
            weight = jnp.exp(scores[p, 0:BLOCK] - peaks[p])
            sums[p] = jnp.sum(eights(weight), 0)
            span = pl.ds(pl.multiple_of(place * BLOCK, BLOCK), BLOCK)
            mixed[p] = mm(vt[:, span], weight.astype(bf16))

        def mix_step(first, blocks):
            span = pl.ds(pl.multiple_of(first * BLOCK, BLOCK), blocks * BLOCK)
            at = pl.ds(pl.multiple_of((first - low + 1) * BLOCK, BLOCK), blocks * BLOCK)
            values = vt[:, span]
            for p in range(PAIRS):
                weight = jnp.exp(scores[p, at] - tops[p, 0:1])
                sums[p] += jnp.sum(eights(weight), 0)
                mixed[p] += mm(values, weight.astype(bf16))

        sweep(low, count, mix_step)
        for p in range(PAIRS):
            total = jnp.sum(sums[p], 0, keepdims=True)
            lse_ref[b, p] = tops[p] + jnp.log(total)
            att_ref[b * BLOCK : (b + 1) * BLOCK, p * BLOCK : (p + 1) * BLOCK] = unfold_heads(
                (mixed[p] / total).astype(bf16)
            )


def backward_kernel(
    length_ref,
    order_ref,
    files_ref,
    q_ref,
    do_ref,
    att_ref,
    lse_ref,
    one_ref,
    kv_ref,
    gq_ref,
    keep_ref,
    send_ref,
    grad_ref,
    keys,
    qt,
    dot_,
    qd,
    both,
    kt,
    dq,
    dkv,
    gwq,
):
    plan = read_plan(length_ref, order_ref, files_ref)
    place_keys(plan, order_ref, kv_ref, keys)
    for k in range(BLOCKS):
        kt[:, k * BLOCK : (k + 1) * BLOCK] = (
            keys[k * BLOCK : (k + 1) * BLOCK, :BLOCK].T[:HD]
        )
    dkv[...] = jnp.zeros_like(dkv)
    zeros = jnp.zeros((BLOCK, HD), bf16)
    empty = jnp.zeros((HD, 2 * BLOCK), bf16)
    for b in range(2):
        place, low, count = block_plan(plan, order_ref, b)
        marks = query_marks(plan, place)
        for p in range(PAIRS):
            span = (slice(b * BLOCK, (b + 1) * BLOCK), slice(p * BLOCK, (p + 1) * BLOCK))
            block = q_ref[span] * 0.125
            grad = do_ref[span]
            wide = fold_heads(grad)
            out = fold_heads(att_ref[span]).astype(f32)
            delta = jnp.sum(wide.astype(f32) * out, 0, keepdims=True)
            top = jnp.concatenate([fold_heads(block), empty], 0)
            fill(qt.at[p], top, marks + minus_terms(lse_ref[b, p, 0:1]))
            fill(dot_.at[p], jnp.concatenate([empty, wide], 0), minus_terms(delta))
            factors = [
                jnp.concatenate([block[:, :HD], zeros], 1),
                jnp.concatenate([block[:, HD:], zeros], 1),
                jnp.concatenate([zeros, grad[:, :HD]], 1),
                jnp.concatenate([zeros, grad[:, HD:]], 1),
            ]
            qd[512 * p : 512 * (p + 1)] = jnp.concatenate(factors, 0)
        dq[...] = jnp.zeros_like(dq)

        def step(first, blocks, rows=None, bias=None):
            span = pl.ds(pl.multiple_of(first * BLOCK, BLOCK), blocks * BLOCK)
            rows = keys[span] if rows is None else rows
            turned = kt[:, span]
            size = blocks * BLOCK
            for p in range(PAIRS):
                value = mm(rows, qt[p])
                probs = jnp.exp(value if bias is None else value + bias)
                grad = (probs * mm(rows, dot_[p])).astype(bf16)
                dq[p] += mm(turned, grad)
                both[:size, 512 * p : 512 * p + 256] = grad
                both[:size, 512 * p + 256 : 512 * p + 512] = probs.astype(bf16)
            dkv[span] += mm(both[:size], qd[...])

        step(place, 1, own_keys(keys, place), own_bias(plan, place))
        sweep(low, count, step)
        for p in range(PAIRS):
            gq_ref[b * BLOCK : (b + 1) * BLOCK, p * BLOCK : (p + 1) * BLOCK] = unfold_heads(
                (dq[p] * 0.125).astype(bf16)
            )

    def give(k, carry):
        initial = order_ref[0, k]
        grad_ref[k] = dkv[pl.ds(pl.multiple_of(initial * BLOCK, BLOCK), BLOCK)].astype(bf16)
        return carry

    lax.fori_loop(0, BLOCKS, give, 0)
    gwq[...] = mm(one_ref[...].T, gq_ref[...]).astype(bf16)
    deal_rows(gwq, keep_ref, send_ref)


def deal_rows(source, keep_ref, send_ref):
    for k in range(8):
        keep_ref[k] = source[row_span(k, 0), :]
        send_ref[k] = source[row_span(k, 1), :]


def columns(c, first=0):
    return pl.ds(pl.multiple_of(first + c * SLICE, BLOCK), SLICE)


def middle_kernel(
    feed_ref,
    mine_ref,
    other_ref,
    x_ref,
    ct_ref,
    att_ref,
    vec_ref,
    fcb_ref,
    out_ref,
    gmid_ref,
    gatt_ref,
    sums_ref,
    keep_ref,
    send_ref,
    grad_ref,
    wf,
    wg,
    gf,
    gg,
    in_sem,
    out_sem,
    last_sem,
    wout,
    gout,
    x2,
    x2t,
    ctt,
    branch,
    gin,
    mid,
    fcsum,
):
    def load(c, slot):
        for k in range(16):
            rows = pl.ds((k // 4 * 4 + k % 2 * 2 + k // 2 % 2) * ROWS, ROWS)
            for half, (buffer, first) in enumerate(((wf, 0), (wg, FF))):
                pltpu.make_async_copy(
                    feed_ref.at[rows, columns(c, first)],
                    buffer.at[slot, pl.ds(k * ROWS, ROWS)],
                    in_sem.at[slot, half],
                ).start()

    def loaded(slot):
        pltpu.make_async_copy(wf.at[slot], wf.at[slot], in_sem.at[slot, 0]).wait()
        pltpu.make_async_copy(wg.at[slot], wg.at[slot], in_sem.at[slot, 1]).wait()

    def store(c, slot):
        for k in range(16):
            pltpu.make_async_copy(
                gf.at[slot, pl.ds(k * ROWS, ROWS)],
                grad_ref.at[k // 4, k % 2, k // 2 % 2, :, columns(c)],
                out_sem.at[slot, 0],
            ).start()
            pltpu.make_async_copy(
                gg.at[slot, pl.ds(k * ROWS, ROWS), pl.ds(SENT, REST)],
                grad_ref.at[
                    k // 4,
                    k % 2,
                    k // 2 % 2,
                    :,
                    pl.ds(pl.multiple_of(FF + D + c * REST, BLOCK), REST),
                ],
                out_sem.at[slot, 1],
            ).start()
        for k in range(8):
            for other, ref in enumerate((keep_ref, send_ref)):
                pltpu.make_async_copy(
                    gg.at[slot, row_span(k, other), pl.ds(0, SENT)],
                    ref.at[c, k],
                    out_sem.at[slot, 1],
                ).start()

    def stored(slot):
        pltpu.make_async_copy(gf.at[slot], gf.at[slot], out_sem.at[slot, 0]).wait()
        pltpu.make_async_copy(gg.at[slot], gg.at[slot], out_sem.at[slot, 1]).wait()

    copies = row_copies((mine_ref, other_ref), pl.ds(OUT, D), wout, last_sem)
    start(copies)
    load(0, 0)
    ctt[...] = ct_ref[...].T
    branch[...] = jnp.zeros_like(branch)
    gin[...] = jnp.zeros_like(gin)
    vec = vec_ref[...]
    finish(copies)
    middle = x_ref[...].astype(f32) + (mm_nt(att_ref[...], wout[...]) + vec[3:4])
    mid[...] = middle
    normed, factor = normalize(middle)
    two = (normed * vec[4:5] + vec[5:6]).astype(bf16)
    x2[...] = two
    x2t[...] = two.T

    def chunk(c, carry):
        slot = lax.rem(c, 2)

        @pl.when(c < 3)
        def _():
            load(c + 1, 1 - slot)

        loaded(slot)
        span = columns(c)
        pre = mm(x2[...], wf[slot]) + fcb_ref[:, span]
        grad_hidden = mm(ct_ref[...], wg[slot])
        square = pre * pre
        tanh = jnp.tanh(0.7978845608028654 * (pre + 0.044715 * (pre * square)))
        half = 0.5 * (1.0 + tanh)
        hidden = (pre * half).astype(bf16)
        slope = half + (0.5 * pre) * (1.0 - tanh * tanh) * (
            0.7978845608028654 + (3 * 0.044715 * 0.7978845608028654) * square
        )
        grad_pre = (grad_hidden * slope).astype(bf16)
        branch[...] += mm_nt(hidden, wg[slot])
        gin[...] += mm_nt(grad_pre, wf[slot])
        fcsum[:, span] = jnp.sum(grad_pre.astype(f32), 0, keepdims=True)

        @pl.when(c >= 2)
        def _():
            stored(slot)

        gf[slot] = mm(x2t[...], grad_pre).astype(bf16)
        gg[slot] = mm(ctt[...], hidden).astype(bf16)
        store(c, slot)
        return carry

    lax.fori_loop(0, 4, chunk, 0)
    middle = mid[...]
    cot = ct_ref[...].astype(f32)
    out_ref[...] = (middle + (branch[...] + vec[6:7])).astype(bf16)
    normed, factor = normalize(middle)
    grad_two = gin[...]
    grad_middle = cot + norm_back(grad_two * vec[4:5], normed, factor)
    gmid_ref[...] = grad_middle
    grad_branch = grad_middle.astype(bf16)
    gout[...] = mm(grad_branch.T, att_ref[...]).astype(bf16)
    outs = [
        pltpu.make_async_copy(
            gout.at[pl.ds(k * ROWS, ROWS)],
            grad_ref.at[k // 4, k % 2, k // 2 % 2, :, pl.ds(FF, D)],
            last_sem,
        )
        for k in range(16)
    ]
    start(outs)
    gatt_ref[...] = mm(grad_branch, wout[...]).astype(bf16)
    sums_ref[0:4] = jnp.concatenate(
        [
            jnp.sum(grad_branch.astype(f32), 0, keepdims=True),
            jnp.sum(grad_two * normed, 0, keepdims=True),
            jnp.sum(grad_two, 0, keepdims=True),
            jnp.sum(cot, 0, keepdims=True),
        ],
        0,
    )
    gather = four_apart(512, BLOCK, 1)
    mine = lax.broadcasted_iota(jnp.int32, (4, 512), 0) == (
        lax.broadcasted_iota(jnp.int32, (4, 512), 1) % 4
    )
    for g in range(6):
        high, low = split_low(jnp.where(mine, fcsum[:, g * 512 : (g + 1) * 512], 0.0))
        sums_ref[4:8, g * BLOCK : (g + 1) * BLOCK] = mm(high, gather) + mm(low, gather)
    stored(0)
    stored(1)
    finish(outs)


def last_kernel(
    x_ref,
    one_ref,
    gq_ref,
    gmid_ref,
    wq_ref,
    early_ref,
    vec_ref,
    sums_ref,
    dkv_ref,
    gx_ref,
    keep_ref,
    send_ref,
    pack_ref,
):
    gkv = jnp.sum(dkv_ref[...].astype(f32), 0).astype(bf16)
    gq = gq_ref[...]
    vec = vec_ref[...]
    grad_one = mm_nt(gq, wq_ref[...]) + mm_nt(gkv, early_ref[:, :BLOCK])
    normed, factor = normalize(x_ref[...].astype(f32))
    gx_ref[...] = (gmid_ref[...] + norm_back(grad_one * vec[0:1], normed, factor)).astype(bf16)
    pack_ref[:, :BLOCK] = mm(one_ref[...].astype(f32).T.astype(bf16), gkv).astype(bf16)
    sums = sums_ref[...]
    rows = jnp.concatenate(
        [
            jnp.sum(grad_one * normed, 0, keepdims=True),
            jnp.sum(grad_one, 0, keepdims=True),
            jnp.sum(gq.astype(f32), 0, keepdims=True),
            sums,
            jnp.zeros((5, D), f32),
        ],
        0,
    )
    high, low = split_low(rows)
    value = jnp.sum(gkv.astype(f32), 0, keepdims=True)[:, HD:]
    value_high, value_low = split_low(value)
    lane = lax.broadcasted_iota(jnp.int32, (16, HD), 1)
    mine = (lane & 15) == lax.broadcasted_iota(jnp.int32, (16, HD), 0)
    group = lax.broadcasted_iota(jnp.int32, (HD, D), 0) // 16
    spread = jnp.where(group == lax.broadcasted_iota(jnp.int32, (HD, D), 1) % 6, 1.0, 0.0).astype(bf16)
    put_high = mm(jnp.where(mine, value_high.astype(f32), 0.0).astype(bf16), spread)
    put_low = mm(jnp.where(mine, value_low.astype(f32), 0.0).astype(bf16), spread)
    packed = jnp.concatenate(
        [high.astype(f32), low.astype(f32), put_high, put_low, jnp.zeros((64, D), f32)], 0
    )
    pack_ref[:, BLOCK:] = packed.T.astype(bf16)
    deal_rows(pack_ref, keep_ref, send_ref)


SMEM = pl.BlockSpec(memory_space=pltpu.SMEM)
VMEM = pl.BlockSpec(memory_space=pltpu.VMEM)
ANY = pl.BlockSpec(memory_space=pl.ANY)


def shape(*dims, dtype=bf16):
    return jax.ShapeDtypeStruct(dims, dtype)


def add_all(parts, dtype=bf16):
    total = parts[0].astype(f32)
    for part in parts[1:]:
        total = total + part.astype(f32)
    return total.astype(dtype)


def call(kernel, name, outs, args, scratch=(), smem=0, hbm=(), hbm_out=0, flops=0, moved=0, exps=0):
    places = [SMEM if i < smem else ANY if i in hbm else VMEM for i in range(len(args))]
    return pl.pallas_call(
        kernel,
        out_shape=outs,
        in_specs=places,
        out_specs=[VMEM] * (len(outs) - hbm_out) + [ANY] * hbm_out,
        scratch_shapes=list(scratch),
        compiler_params=pltpu.CompilerParams(vmem_limit_bytes=56 * 1024 * 1024),
        cost_estimate=pl.CostEstimate(flops=flops, bytes_accessed=moved, transcendentals=exps),
        name=name,
    )(*args)


def tie(value, after):
    return lax.optimization_barrier((value, after))[0]


def local(
    layer_input,
    cotangent,
    lengths,
    order,
    files,
    ln1_gain,
    ln1_bias,
    w_attn,
    query_bias,
    value_bias,
    w_out,
    out_bias,
    ln2_gain,
    ln2_bias,
    w_fc,
    fc_bias,
    w_proj,
    proj_bias,
):
    x = layer_input[0]
    cot = cotangent[0]
    vectors = [ln1_gain, ln1_bias, query_bias, out_bias, ln2_gain, ln2_bias, proj_bias, fc_bias]
    (pieces,) = call(
        piece_kernel,
        "pieces",
        [shape(16, 24, FOLD)],
        [*vectors, w_attn, w_out, w_fc, w_proj],
        [pltpu.VMEM((6, WIDE), f32)],
        smem=8,
        moved=2_000_000,
    )
    attn_block, feed_block = call(
        block_kernel,
        "blocks",
        [shape(4, 2 * ROWS, FC), shape(2 * ROWS, 2 * FF)],
        [lax.all_to_all(pieces, ("zl", "y", "zh"), 0, 0)],
        [pltpu.VMEM((2 * ROWS, WIDE), f32)],
        moved=4_000_000,
    )
    feed = lax.all_gather(feed_block, ("x", "core"), axis=0, tiled=True)
    attn = lax.all_to_all(attn_block, "x", 0, 0).reshape(8, ROWS, FC)
    parts = [attn, send(attn, dc=1)]
    one, kv, vec, fcb, early = call(
        first_kernel,
        "first",
        [
            shape(TOK, D),
            shape(8, TOK, BLOCK),
            shape(16, D, dtype=f32),
            shape(1, FF, dtype=f32),
            shape(D, 2 * BLOCK),
        ],
        [x, value_bias[None], *parts],
        [pltpu.SemaphoreType.DMA],
        hbm=(2, 3),
        flops=100_000_000,
        moved=4_000_000,
    )
    kv = lax.all_to_all(kv, CTX, 0, 0).reshape(LENGTH, BLOCK)

    wide = (PAIRS, 2 * BLOCK, 2 * BLOCK)
    plan = [lengths, order, files]
    q, att, lse, wq = call(
        forward_kernel,
        "attend",
        [
            shape(TOK, D),
            shape(TOK, D),
            shape(2, PAIRS, 8, 2 * BLOCK, dtype=f32),
            shape(D, D),
        ],
        [*plan, one, vec, kv, *parts],
        [
            pltpu.VMEM((LENGTH, 2 * BLOCK), bf16),
            pltpu.VMEM(wide, bf16),
            pltpu.VMEM((HD, LENGTH), bf16),
            pltpu.VMEM((PAIRS, LENGTH, 2 * BLOCK), f32),
            pltpu.VMEM((PAIRS, 8, 2 * BLOCK), f32),
            pltpu.VMEM((PAIRS, 8, 2 * BLOCK), f32),
            pltpu.VMEM((PAIRS, HD, 2 * BLOCK), f32),
            pltpu.SemaphoreType.DMA,
        ],
        smem=2,
        hbm=(6, 7),
        flops=10_000_000_000,
        moved=4_000_000,
        exps=6_000_000,
    )
    half = shape(8, ROWS, D)
    sliced = shape(4, 8, ROWS, SENT)
    output, grad_middle, grad_att, sums, keep_proj, send_proj, grad_fc = call(
        middle_kernel,
        "feed",
        [
            shape(TOK, D),
            shape(TOK, D, dtype=f32),
            shape(TOK, D),
            shape(8, D, dtype=f32),
            sliced,
            sliced,
            shape(4, 2, 2, ROWS, REDUCED),
        ],
        [feed, *parts, x, cot, att, vec, fcb],
        [
            pltpu.VMEM((2, D, SLICE), bf16),
            pltpu.VMEM((2, D, SLICE), bf16),
            pltpu.VMEM((2, D, SLICE), bf16),
            pltpu.VMEM((2, D, SLICE), bf16),
            pltpu.SemaphoreType.DMA((2, 2)),
            pltpu.SemaphoreType.DMA((2, 2)),
            pltpu.SemaphoreType.DMA,
            pltpu.VMEM((D, D), bf16),
            pltpu.VMEM((D, D), bf16),
            pltpu.VMEM((TOK, D), bf16),
            pltpu.VMEM((D, TOK), bf16),
            pltpu.VMEM((D, TOK), bf16),
            pltpu.VMEM((TOK, D), f32),
            pltpu.VMEM((TOK, D), f32),
            pltpu.VMEM((TOK, D), f32),
            pltpu.VMEM((1, FF), f32),
        ],
        hbm=(0, 1, 2),
        hbm_out=3,
        flops=8_000_000_000,
        moved=30_000_000,
        exps=1_000_000,
    )
    grad_fc = grad_fc.reshape(8, 2, ROWS, REDUCED)
    grad_fc = lax.psum_scatter(grad_fc, ("x", "core"), scatter_dimension=0, tiled=True)[0]
    grad_proj = add_all([keep_proj, send(send_proj, dc=1)])
    grad_att = tie(grad_att, grad_proj)
    grad_proj = add_all(list(lax.all_to_all(grad_proj, "y", 0, 0)))

    gq, keep_q, send_q, grad_kv = call(
        backward_kernel,
        "attend_back",
        [shape(TOK, D), half, half, shape(BLOCKS, BLOCK, BLOCK)],
        [*plan, q, grad_att, att, lse, one, kv],
        [
            pltpu.VMEM((LENGTH, 2 * BLOCK), bf16),
            pltpu.VMEM(wide, bf16),
            pltpu.VMEM(wide, bf16),
            pltpu.VMEM((PAIRS * 4 * BLOCK, BLOCK), bf16),
            pltpu.VMEM((4 * BLOCK, PAIRS * 4 * BLOCK), bf16),
            pltpu.VMEM((HD, LENGTH), bf16),
            pltpu.VMEM((PAIRS, HD, 2 * BLOCK), f32),
            pltpu.VMEM((LENGTH, BLOCK), f32),
            pltpu.VMEM((D, D), bf16),
        ],
        smem=2,
        flops=20_000_000_000,
        moved=6_000_000,
        exps=6_000_000,
    )
    grad_q = add_all([keep_q, send(send_q, dc=1)])
    grad_kv = tie(grad_kv.reshape(8, TOK, BLOCK), grad_proj)
    grad_kv = lax.all_to_all(grad_kv, CTX, 0, 0)

    small = shape(8, ROWS, 2 * BLOCK)
    grad_x, keep_pack, send_pack = call(
        last_kernel,
        "last",
        [shape(TOK, D), small, small],
        [x, one, gq, grad_middle, wq, early, vec, sums, grad_kv],
        [pltpu.VMEM((D, 2 * BLOCK), bf16)],
        flops=1_000_000_000,
        moved=5_000_000,
    )
    grad_pack = add_all([keep_pack, send(send_pack, dc=1)])
    both = jnp.concatenate([grad_pack, grad_proj, grad_q], 2).reshape(4, 2 * ROWS, G_FC)
    both = lax.all_to_all(both, "x", 0, 0)
    (pieces,) = call(
        unblock_kernel,
        "unblock",
        [shape(16, 24, G_FOLD)],
        [both, grad_fc],
        [pltpu.VMEM((2 * ROWS, 4 * G_FOLD), f32)],
    )
    results = call(
        finish_kernel,
        "finish",
        [
            shape(6, D + BLOCK, dtype=f32),
            shape(6, D, dtype=f32),
            shape(6, FF, dtype=f32),
            shape(6, FF, dtype=f32),
        ]
        + [shape(1, 6, dtype=f32)] * 7
        + [shape(1, 24, dtype=f32), shape(1, HD, dtype=f32)],
        [lax.all_to_all(pieces, ("zl", "y", "zh"), 0, 0)],
        [pltpu.VMEM((6, 4 * G_FOLD), f32)],
    )
    grad_w_attn, grad_w_out, grad_w_fc, grad_w_proj = results[:4]
    gain_one, bias_one, bias_query, bias_out, gain_two, bias_two, bias_proj, bias_fc = (
        value.reshape(-1) for value in results[4:12]
    )
    return (
        output[None],
        grad_x[None],
        gain_one,
        bias_one,
        grad_w_attn,
        bias_query,
        results[12].reshape(HD),
        grad_w_out,
        bias_out,
        gain_two,
        bias_two,
        grad_w_fc,
        bias_fc,
        grad_w_proj,
        bias_proj,
    )


def solution(mesh):
    cells = Mesh(mesh.devices.reshape(SIZES), AXES)
    every = P(AXES)
    tall = P(AXES, None)
    tokens = P(DP, CTX, None)
    in_specs = (
        tokens,
        tokens,
        P(DP),
        P(DP, None),
        P(DP, None),
        every,
        every,
        tall,
        every,
        P(),
        tall,
        every,
        every,
        every,
        tall,
        every,
        tall,
        every,
    )
    out_specs = (
        tokens,
        tokens,
        every,
        every,
        tall,
        every,
        P(),
        tall,
        every,
        every,
        every,
        tall,
        every,
        tall,
        every,
    )
    return jax.shard_map(local, mesh=cells, in_specs=in_specs, out_specs=out_specs, check_vma=False)
```

```python
import functools

import jax
import jax.numpy as jnp
import numpy as np
from jax import lax
from jax.experimental import pallas as pl
from jax.experimental.pallas import tpu as pltpu
from jax.sharding import Mesh
from jax.sharding import PartitionSpec as P

D = 768
HEADS = 12
HD = 64
FF = 3072
TOK = 256
LENGTH = 2048
BLOCK = 128
BLOCKS = 16
PAIRS = 6
ROWS = 48
COLS = 384
NEG = -1e30

AXES = ("x", "zl", "core", "y", "zh")
SIZES = (4, 2, 2, 4, 2)
DP = ("x", "zl", "core")
CTX = ("y", "zh")

f32 = jnp.float32
bf16 = jnp.bfloat16


def route(dx=0, dy=0, dz=0, dc=0, dl=0, dh=0):
    pairs = []
    for device in range(128):
        x, zl, core, y, zh = (int(v) for v in np.unravel_index(device, SIZES))
        z = (zh * 2 + zl + dz) % 4
        target = ((x + dx) % 4, z % 2 ^ dl, core ^ dc, (y + dy) % 4, z // 2 ^ dh)
        pairs.append((device, int(np.ravel_multi_index(target, SIZES))))
    return pairs


def send(value, **shift):
    return lax.ppermute(value, AXES, route(**shift))


def row_span(group, other):
    core = lax.axis_index("core")
    return pl.ds(pl.multiple_of(group * 96 + (1 - core if other else core) * ROWS, 16), ROWS)


def row_copies(parts, lanes, target, sem):
    return [
        pltpu.make_async_copy(part.at[k, :, lanes], target.at[row_span(k, other)], sem)
        for k in range(8)
        for other, part in enumerate(parts)
    ]


def start(copies):
    for copy in copies:
        copy.start()


def finish(copies):
    for copy in copies:
        copy.wait()


def mm(left, right):
    return lax.dot_general(left, right, (((1,), (0,)), ((), ())), preferred_element_type=f32)


def mm_nt(left, right):
    return lax.dot_general(left, right, (((1,), (1,)), ((), ())), preferred_element_type=f32)


def normalize(values):
    center = values - jnp.mean(values, -1, keepdims=True)
    spread = jnp.mean(center * center, -1, keepdims=True)
    factor = lax.rsqrt(spread + 1e-05)
    return center * factor, factor


def norm_back(grad_normed, normed, factor):
    return factor * (
        grad_normed
        - jnp.mean(grad_normed, -1, keepdims=True)
        - normed * jnp.mean(grad_normed * normed, -1, keepdims=True)
    )


def split_low(values):
    high = values.astype(bf16)
    return high, (values - high.astype(f32)).astype(bf16)


SLICE = 768
KEYS, SMALL, QUERY, OUT, FC, PROJ, WIDE = 0, 128, 256, 1024, 1792, 4864, 8192
FOLD = WIDE // 4
SENT = 256
REST = SLICE - SENT
G_PROJ, G_QUERY, G_FC, G_OUT, G_REST, G_WIDE = 256, 512, 1280, 4352, 5120, 7168
G_FOLD = (G_WIDE + 511) // 512 * BLOCK
REDUCED = G_WIDE - G_FC


def piece_kernel(*refs):
    vectors, fcb_ref, attn_ref, out_ref, fc_ref, proj_ref, piece_ref, row = (
        refs[:7],
    ) + refs[7:]
    line = lax.broadcasted_iota(jnp.int32, (8, BLOCK), 0)
    lane = lax.broadcasted_iota(jnp.int32, (8, BLOCK), 1)
    small = jnp.zeros((8, BLOCK), f32)
    for i in range(6):
        values = [ref[i] for ref in vectors] + [fcb_ref[4 * i + j] for j in range(4)]
        for j, value in enumerate(values):
            small = jnp.where((line == i) & (lane < 48) & ((lane & 15) == j), value, small)
    high = small.astype(bf16).astype(f32)
    middle = (small - high).astype(bf16).astype(f32)
    low = small - high - middle
    small = jnp.where(lane < 16, high, jnp.where(lane < 32, middle, low))[:6]
    row[:, KEYS:SMALL] = attn_ref[:, D:].astype(f32)
    row[:, SMALL:QUERY] = small
    row[:, QUERY:OUT] = attn_ref[:, :D].astype(f32)
    row[:, OUT:FC] = out_ref[...].astype(f32)
    row[:, FC:PROJ] = fc_ref[...].astype(f32)
    row[:, PROJ : PROJ + FF] = proj_ref[...].astype(f32)
    row[:, PROJ + FF :] = jnp.zeros((6, WIDE - PROJ - FF), f32)
    quarters = [row[:, k * FOLD : (k + 1) * FOLD] for k in range(4)]
    piece = jnp.concatenate(quarters, 0).astype(bf16)

    def copy(k, carry):
        piece_ref[k] = piece
        return carry

    lax.fori_loop(0, 16, copy, 0)


def block_kernel(piece_ref, attn_ref, feed_ref, rows):
    for j in range(16):
        piece = piece_ref[j].astype(f32)
        for k in range(4):
            rows[6 * j : 6 * j + 6, k * FOLD : (k + 1) * FOLD] = piece[6 * k : 6 * k + 6]
    for k in range(4):
        attn_ref[k] = rows[:, :FC].astype(bf16)
    feed_ref[...] = rows[:, FC : FC + 2 * FF].astype(bf16)


def fold_lanes(rows):
    width = rows.shape[1] // 4
    return jnp.concatenate([rows[:, k * width : (k + 1) * width] for k in range(4)], 0)


def unblock_kernel(attn_ref, query_ref, feed_ref, piece_ref, rows):
    rows[:, :G_QUERY] = jnp.sum(attn_ref[...].astype(f32), 0)
    rows[:, G_QUERY:G_FC] = query_ref[...].astype(f32)
    for zl in range(2):
        rows[zl * ROWS : (zl + 1) * ROWS, G_FC:G_WIDE] = feed_ref[zl].astype(f32)
    if G_WIDE < 4 * G_FOLD:
        rows[:, G_WIDE:] = jnp.zeros((2 * ROWS, 4 * G_FOLD - G_WIDE), f32)
    for j in range(16):
        piece_ref[j] = fold_lanes(rows[6 * j : 6 * j + 6]).astype(bf16)


def finish_kernel(piece_ref, attn_ref, out_ref, fc_ref, proj_ref, *refs):
    vectors, fcb_ref, value_ref, rows = refs[:7], refs[7], refs[8], refs[9]
    total = jnp.sum(piece_ref[...].astype(f32), 0)
    for k in range(4):
        rows[:, k * G_FOLD : (k + 1) * G_FOLD] = total[6 * k : 6 * k + 6]
    total = rows[...]
    attn_ref[:, :D] = total[:, G_QUERY:G_FC]
    attn_ref[:, D:] = total[:, KEYS:SMALL]
    fc_ref[...] = total[:, G_FC:G_OUT]
    out_ref[...] = total[:, G_OUT:G_REST]
    for j in range(4):
        sent = [piece_ref[k, :6, G_PROJ:G_QUERY].astype(f32) for k in (2 * j, 2 * j + 1, 2 * j + 8, 2 * j + 9)]
        proj_ref[:, j * SLICE : j * SLICE + SENT] = sent[0] + sent[1] + sent[2] + sent[3]
        proj_ref[:, j * SLICE + SENT : (j + 1) * SLICE] = total[
            :, G_REST + j * REST : G_REST + (j + 1) * REST
        ]
    small = total[:, SMALL:QUERY]
    small = jnp.concatenate([small, jnp.zeros((2, BLOCK), f32)], 0).T
    rows = small[:16] + small[16:32]
    for j, ref in enumerate(vectors):
        ref[...] = rows[j : j + 1, :6]
    spread = jnp.where(
        lax.broadcasted_iota(jnp.int32, (8, 24), 1) // 4
        == lax.broadcasted_iota(jnp.int32, (8, 24), 0),
        1.0,
        0.0,
    )
    wide = jnp.dot(rows[7:11], spread, precision=lax.Precision.HIGHEST)
    mine = lax.broadcasted_iota(jnp.int32, (4, 24), 1) % 4 == lax.broadcasted_iota(
        jnp.int32, (4, 24), 0
    )
    fcb_ref[...] = jnp.sum(jnp.where(mine, wide, 0.0), 0, keepdims=True)
    value = total[:4, SMALL + 32 : SMALL + 48] + total[:4, SMALL + 48 : SMALL + 64]
    value_ref[...] = jnp.concatenate([value[j : j + 1] for j in range(4)], 1)


def four_apart(rows, columns, turned):
    return jnp.where(
        lax.broadcasted_iota(jnp.int32, (rows, columns), 1 - turned) // 4
        == lax.broadcasted_iota(jnp.int32, (rows, columns), turned),
        1.0,
        0.0,
    ).astype(bf16)


def first_kernel(
    x_ref, vbias_ref, mine_ref, other_ref, one_ref, kv_ref, vec_ref, early_ref, sem
):
    copies = row_copies((mine_ref, other_ref), pl.ds(0, QUERY), early_ref, sem)
    start(copies)
    normed, _ = normalize(x_ref[...].astype(f32))
    finish(copies)
    turned = early_ref[:, BLOCK:].astype(f32).T
    vec = turned[0:16] + turned[16:32] + turned[32:48]
    vec_ref[...] = vec
    one = (normed * vec[0:1] + vec[1:2]).astype(bf16)
    one_ref[...] = one
    bias = jnp.concatenate([jnp.zeros((1, HD), f32), vbias_ref[...]], 1)
    kv = (mm(one, early_ref[:, :BLOCK]) + bias).astype(bf16)
    for k in range(8):
        kv_ref[k] = kv


def read_plan(length_ref, order_ref, files_ref):
    files = files_ref[...]
    bounds = [jnp.sum(jnp.where(files < f, 1, 0)) for f in (1, 2, 3)]
    return length_ref[0], bounds


def block_plan(plan, order_ref, b):
    length, bounds = plan
    own = lax.axis_index("y") * 2 + lax.axis_index("zh")
    place = order_ref[0, own * 2 + b]
    start = place * BLOCK
    first = jnp.int32(0)
    for bound in bounds:
        first = jnp.where(bound <= start, jnp.maximum(first, bound), first)
    low = first // BLOCK
    high = jnp.minimum(place - 1, (length - 1) // BLOCK)
    return place, low, jnp.maximum(high - low + 1, 0)


def own_bias(plan, place):
    length, bounds = plan
    lane = lax.broadcasted_iota(jnp.int32, (1, 2 * BLOCK), 1)
    query = place * BLOCK + (lane & (BLOCK - 1))
    first = jnp.zeros_like(query)
    for bound in bounds:
        first = jnp.where(bound <= query, jnp.maximum(first, bound), first)
    last = jnp.minimum(query, length - 1)
    key = place * BLOCK + lax.broadcasted_iota(jnp.int32, (BLOCK, 2 * BLOCK), 0)
    allowed = ((key >= first) & (key <= last)) | (key == query)
    return jnp.where(allowed, 0.0, NEG)


def file_of(plan, position):
    number = jnp.zeros_like(position)
    for bound in plan[1]:
        number = number + jnp.where(bound <= position, 1, 0)
    return number


def place_keys(plan, order_ref, kv_ref, keys):
    lane = lax.broadcasted_iota(jnp.int32, (BLOCK, BLOCK), 1)

    def place(k, carry):
        start = pl.multiple_of(order_ref[0, k] * BLOCK, BLOCK)
        position = start + lax.broadcasted_iota(jnp.int32, (BLOCK, BLOCK), 0)
        mark = (file_of(plan, position) == lane) | ((position >= plan[0]) & (lane == 4))
        mark = mark | ((lane >= 5) & (lane < 8))
        keys[pl.ds(start, BLOCK), :BLOCK] = kv_ref[pl.ds(pl.multiple_of(k * BLOCK, BLOCK), BLOCK)]
        keys[pl.ds(start, BLOCK), BLOCK:] = jnp.where(mark, 1.0, 0.0).astype(bf16)
        return carry

    lax.fori_loop(0, BLOCKS, place, 0)


def own_keys(keys, place):
    rows = keys[pl.ds(pl.multiple_of(place * BLOCK, BLOCK), BLOCK)]
    lane = lax.broadcasted_iota(jnp.int32, rows.shape, 1)
    return jnp.where((lane >= BLOCK) & (lane < BLOCK + 5), jnp.zeros_like(rows), rows)


def query_marks(plan, place):
    lane = lax.broadcasted_iota(jnp.int32, (8, 2 * BLOCK), 1)
    number = file_of(plan, place * BLOCK + (lane & (BLOCK - 1)))
    mark = lax.broadcasted_iota(jnp.int32, (8, 2 * BLOCK), 0)
    return jnp.where(((mark < 4) & (mark != number)) | (mark == 4), NEG, 0.0)


def minus_terms(row):
    high = row.astype(bf16).astype(f32)
    middle = (row - high).astype(bf16).astype(f32)
    low = row - high - middle
    mark = lax.broadcasted_iota(jnp.int32, (8, row.shape[1]), 0)
    return jnp.where(
        mark == 5, -high, jnp.where(mark == 6, -middle, jnp.where(mark == 7, -low, 0.0))
    )


def fill(target, top, marks):
    target[:BLOCK] = top
    zeros = jnp.zeros((BLOCK - 8, 2 * BLOCK), f32)
    target[BLOCK:] = jnp.concatenate([marks, zeros], 0).astype(bf16)


def sweep(low, count, step):
    def four(t, carry):
        step(low + 4 * t, 4)
        return carry

    lax.fori_loop(0, count // 4, four, 0)

    @pl.when(lax.rem(count, 4) >= 2)
    def _():
        step(low + count // 4 * 4, 2)

    @pl.when(lax.rem(count, 2) == 1)
    def _():
        step(low + count - 1, 1)


def fold_heads(block):
    turned = block.T
    return jnp.concatenate([turned[:HD], turned[HD:]], 1)


def unfold_heads(wide):
    return jnp.concatenate([wide[:, :BLOCK], wide[:, BLOCK:]], 0).T


def eights(values):
    return values.reshape(values.shape[0] // 8, 8, values.shape[1])


def query_kernel(
    length_ref,
    order_ref,
    files_ref,
    one_ref,
    vec_ref,
    early_ref,
    mine_ref,
    other_ref,
    q_ref,
    qt_ref,
    fcb_ref,
    wq,
    sem,
):
    copies = row_copies((mine_ref, other_ref), pl.ds(QUERY, D), wq, sem)
    start(copies)
    plan = read_plan(length_ref, order_ref, files_ref)
    finish(copies)
    q = (mm(one_ref[...], wq[...]) + vec_ref[2:3]).astype(bf16)
    q_ref[...] = q
    terms = early_ref[:, BLOCK:].T[:48]
    spread = four_apart(BLOCK, 512, 0)
    term = lax.broadcasted_iota(jnp.int32, (48, 512), 0) % 16 - 7
    mine = term == lax.broadcasted_iota(jnp.int32, (48, 512), 1) % 4
    for g in range(6):
        wide = mm(terms[:, g * BLOCK : (g + 1) * BLOCK], spread)
        fcb_ref[:, g * 512 : (g + 1) * 512] = jnp.sum(
            jnp.where(mine, wide, 0.0), 0, keepdims=True
        )
    empty = jnp.zeros((HD, 2 * BLOCK), bf16)
    for b in range(2):
        place, _, _ = block_plan(plan, order_ref, b)
        marks = query_marks(plan, place)
        for p in range(PAIRS):
            block = q[b * BLOCK : (b + 1) * BLOCK, p * BLOCK : (p + 1) * BLOCK] * 0.125
            top = jnp.concatenate([fold_heads(block), empty], 0)
            fill(qt_ref.at[b, p], top, marks)


def forward_kernel(
    length_ref,
    order_ref,
    files_ref,
    kv_ref,
    qt_ref,
    att_ref,
    lse_ref,
    keys,
    vt,
    scores,
    tops,
    sums,
    mixed,
):
    plan = read_plan(length_ref, order_ref, files_ref)
    place_keys(plan, order_ref, kv_ref, keys)
    for k in range(BLOCKS):
        vt[:, k * BLOCK : (k + 1) * BLOCK] = keys[k * BLOCK : (k + 1) * BLOCK, :BLOCK].T[HD:]
    for b in range(2):
        place, low, count = block_plan(plan, order_ref, b)
        qt = qt_ref.at[b]
        own = own_keys(keys, place)
        bias = own_bias(plan, place)
        for p in range(PAIRS):
            value = mm(own, qt[p]) + bias
            scores[p, 0:BLOCK] = value
            tops[p] = jnp.max(eights(value), 0)

        def score_step(first, blocks):
            rows = keys[pl.ds(pl.multiple_of(first * BLOCK, BLOCK), blocks * BLOCK)]
            at = pl.ds(pl.multiple_of((first - low + 1) * BLOCK, BLOCK), blocks * BLOCK)
            for p in range(PAIRS):
                value = mm(rows, qt[p])
                scores[p, at] = value
                tops[p] = jnp.maximum(tops[p], jnp.max(eights(value), 0))

        sweep(low, count, score_step)
        peaks = [jnp.max(tops[p], 0, keepdims=True) for p in range(PAIRS)]
        for p in range(PAIRS):
            tops[p] = jnp.broadcast_to(peaks[p], (8, 2 * BLOCK))
            weight = jnp.exp(scores[p, 0:BLOCK] - peaks[p])
            sums[p] = jnp.sum(eights(weight), 0)
            span = pl.ds(pl.multiple_of(place * BLOCK, BLOCK), BLOCK)
            mixed[p] = mm(vt[:, span], weight.astype(bf16))

        def mix_step(first, blocks):
            span = pl.ds(pl.multiple_of(first * BLOCK, BLOCK), blocks * BLOCK)
            at = pl.ds(pl.multiple_of((first - low + 1) * BLOCK, BLOCK), blocks * BLOCK)
            values = vt[:, span]
            for p in range(PAIRS):
                weight = jnp.exp(scores[p, at] - tops[p, 0:1])
                sums[p] += jnp.sum(eights(weight), 0)
                mixed[p] += mm(values, weight.astype(bf16))

        sweep(low, count, mix_step)
        for p in range(PAIRS):
            total = jnp.sum(sums[p], 0, keepdims=True)
            lse_ref[b, p] = tops[p] + jnp.log(total)
            att_ref[b * BLOCK : (b + 1) * BLOCK, p * BLOCK : (p + 1) * BLOCK] = unfold_heads(
                (mixed[p] / total).astype(bf16)
            )


def backward_kernel(
    length_ref,
    order_ref,
    files_ref,
    q_ref,
    do_ref,
    att_ref,
    lse_ref,
    one_ref,
    kv_ref,
    gq_ref,
    keep_ref,
    send_ref,
    grad_ref,
    keys,
    qt,
    dot_,
    qd,
    both,
    kt,
    dq,
    dkv,
    gwq,
):
    plan = read_plan(length_ref, order_ref, files_ref)
    place_keys(plan, order_ref, kv_ref, keys)
    for k in range(BLOCKS):
        kt[:, k * BLOCK : (k + 1) * BLOCK] = (
            keys[k * BLOCK : (k + 1) * BLOCK, :BLOCK].T[:HD]
        )
    dkv[...] = jnp.zeros_like(dkv)
    zeros = jnp.zeros((BLOCK, HD), bf16)
    empty = jnp.zeros((HD, 2 * BLOCK), bf16)
    for b in range(2):
        place, low, count = block_plan(plan, order_ref, b)
        marks = query_marks(plan, place)
        for p in range(PAIRS):
            span = (slice(b * BLOCK, (b + 1) * BLOCK), slice(p * BLOCK, (p + 1) * BLOCK))
            block = q_ref[span] * 0.125
            grad = do_ref[span]
            wide = fold_heads(grad)
            out = fold_heads(att_ref[span]).astype(f32)
            delta = jnp.sum(wide.astype(f32) * out, 0, keepdims=True)
            top = jnp.concatenate([fold_heads(block), empty], 0)
            fill(qt.at[p], top, marks + minus_terms(lse_ref[b, p, 0:1]))
            fill(dot_.at[p], jnp.concatenate([empty, wide], 0), minus_terms(delta))
            factors = [
                jnp.concatenate([block[:, :HD], zeros], 1),
                jnp.concatenate([block[:, HD:], zeros], 1),
                jnp.concatenate([zeros, grad[:, :HD]], 1),
                jnp.concatenate([zeros, grad[:, HD:]], 1),
            ]
            qd[512 * p : 512 * (p + 1)] = jnp.concatenate(factors, 0)
        dq[...] = jnp.zeros_like(dq)

        def step(first, blocks, rows=None, bias=None):
            span = pl.ds(pl.multiple_of(first * BLOCK, BLOCK), blocks * BLOCK)
            rows = keys[span] if rows is None else rows
            turned = kt[:, span]
            size = blocks * BLOCK
            for p in range(PAIRS):
                value = mm(rows, qt[p])
                probs = jnp.exp(value if bias is None else value + bias)
                grad = (probs * mm(rows, dot_[p])).astype(bf16)
                dq[p] += mm(turned, grad)
                both[:size, 512 * p : 512 * p + 256] = grad
                both[:size, 512 * p + 256 : 512 * p + 512] = probs.astype(bf16)
            dkv[span] += mm(both[:size], qd[...])

        step(place, 1, own_keys(keys, place), own_bias(plan, place))
        sweep(low, count, step)
        for p in range(PAIRS):
            gq_ref[b * BLOCK : (b + 1) * BLOCK, p * BLOCK : (p + 1) * BLOCK] = unfold_heads(
                (dq[p] * 0.125).astype(bf16)
            )

    def give(k, carry):
        initial = order_ref[0, k]
        grad_ref[k] = dkv[pl.ds(pl.multiple_of(initial * BLOCK, BLOCK), BLOCK)].astype(bf16)
        return carry

    lax.fori_loop(0, BLOCKS, give, 0)
    gwq[...] = mm(one_ref[...].T, gq_ref[...]).astype(bf16)
    deal_rows(gwq, keep_ref, send_ref, lax.axis_index("x"))


def deal_rows(source, keep_ref, send_ref, x=0):
    for k in range(8):
        there = lax.rem(k // 2 - x + 4, 4) * 2 + k % 2
        keep_ref[there] = source[row_span(k, 0), :]
        send_ref[there] = source[row_span(k, 1), :]


def columns(c, first=0):
    return pl.ds(pl.multiple_of(first + c * SLICE, BLOCK), SLICE)


def middle_kernel(
    feed_ref,
    mine_ref,
    other_ref,
    x_ref,
    ct_ref,
    att_ref,
    vec_ref,
    fcb_ref,
    out_ref,
    gmid_ref,
    gatt_ref,
    sums_ref,
    keep_ref,
    send_ref,
    grad_ref,
    wf,
    wg,
    gf,
    gg,
    in_sem,
    out_sem,
    last_sem,
    wout,
    gout,
    x2,
    x2t,
    ctt,
    branch,
    gin,
    mid,
    fcsum,
):
    def load(c, slot):
        for k in range(16):
            rows = pl.ds((k // 4 * 4 + k % 2 * 2 + k // 2 % 2) * ROWS, ROWS)
            for half, (buffer, first) in enumerate(((wf, 0), (wg, FF))):
                pltpu.make_async_copy(
                    feed_ref.at[rows, columns(c, first)],
                    buffer.at[slot, pl.ds(k * ROWS, ROWS)],
                    in_sem.at[slot, half],
                ).start()

    def loaded(slot):
        pltpu.make_async_copy(wf.at[slot], wf.at[slot], in_sem.at[slot, 0]).wait()
        pltpu.make_async_copy(wg.at[slot], wg.at[slot], in_sem.at[slot, 1]).wait()

    def store(c, slot):
        for k in range(16):
            pltpu.make_async_copy(
                gf.at[slot, pl.ds(k * ROWS, ROWS)],
                grad_ref.at[k // 4, k % 2, k // 2 % 2, :, columns(c)],
                out_sem.at[slot, 0],
            ).start()
            pltpu.make_async_copy(
                gg.at[slot, pl.ds(k * ROWS, ROWS), pl.ds(SENT, REST)],
                grad_ref.at[
                    k // 4,
                    k % 2,
                    k // 2 % 2,
                    :,
                    pl.ds(pl.multiple_of(FF + D + c * REST, BLOCK), REST),
                ],
                out_sem.at[slot, 1],
            ).start()
        for k in range(8):
            for other, ref in enumerate((keep_ref, send_ref)):
                pltpu.make_async_copy(
                    gg.at[slot, row_span(k, other), pl.ds(0, SENT)],
                    ref.at[c, k],
                    out_sem.at[slot, 1],
                ).start()

    def stored(slot):
        pltpu.make_async_copy(gf.at[slot], gf.at[slot], out_sem.at[slot, 0]).wait()
        pltpu.make_async_copy(gg.at[slot], gg.at[slot], out_sem.at[slot, 1]).wait()

    copies = row_copies((mine_ref, other_ref), pl.ds(OUT, D), wout, last_sem)
    start(copies)
    load(0, 0)
    ctt[...] = ct_ref[...].T
    branch[...] = jnp.zeros_like(branch)
    gin[...] = jnp.zeros_like(gin)
    vec = vec_ref[...]
    finish(copies)
    middle = x_ref[...].astype(f32) + (mm_nt(att_ref[...], wout[...]) + vec[3:4])
    mid[...] = middle
    normed, factor = normalize(middle)
    two = (normed * vec[4:5] + vec[5:6]).astype(bf16)
    x2[...] = two
    x2t[...] = two.T

    def chunk(c, carry):
        slot = lax.rem(c, 2)

        @pl.when(c < 3)
        def _():
            load(c + 1, 1 - slot)

        loaded(slot)
        span = columns(c)
        pre = mm(x2[...], wf[slot]) + fcb_ref[:, span]
        grad_hidden = mm(ct_ref[...], wg[slot])
        square = pre * pre
        tanh = jnp.tanh(0.7978845608028654 * (pre + 0.044715 * (pre * square)))
        half = 0.5 * (1.0 + tanh)
        hidden = (pre * half).astype(bf16)
        slope = half + (0.5 * pre) * (1.0 - tanh * tanh) * (
            0.7978845608028654 + (3 * 0.044715 * 0.7978845608028654) * square
        )
        grad_pre = (grad_hidden * slope).astype(bf16)
        branch[...] += mm_nt(hidden, wg[slot])
        gin[...] += mm_nt(grad_pre, wf[slot])
        fcsum[:, span] = jnp.sum(grad_pre.astype(f32), 0, keepdims=True)

        @pl.when(c >= 2)
        def _():
            stored(slot)

        gf[slot] = mm(x2t[...], grad_pre).astype(bf16)
        gg[slot] = mm(ctt[...], hidden).astype(bf16)
        store(c, slot)
        return carry

    lax.fori_loop(0, 4, chunk, 0)
    middle = mid[...]
    cot = ct_ref[...].astype(f32)
    out_ref[...] = (middle + (branch[...] + vec[6:7])).astype(bf16)
    normed, factor = normalize(middle)
    grad_two = gin[...]
    grad_middle = cot + norm_back(grad_two * vec[4:5], normed, factor)
    gmid_ref[...] = grad_middle
    grad_branch = grad_middle.astype(bf16)
    gout[...] = mm(grad_branch.T, att_ref[...]).astype(bf16)
    outs = [
        pltpu.make_async_copy(
            gout.at[pl.ds(k * ROWS, ROWS)],
            grad_ref.at[k // 4, k % 2, k // 2 % 2, :, pl.ds(FF, D)],
            last_sem,
        )
        for k in range(16)
    ]
    start(outs)
    gatt_ref[...] = mm(grad_branch, wout[...]).astype(bf16)
    sums_ref[0:4] = jnp.concatenate(
        [
            jnp.sum(grad_branch.astype(f32), 0, keepdims=True),
            jnp.sum(grad_two * normed, 0, keepdims=True),
            jnp.sum(grad_two, 0, keepdims=True),
            jnp.sum(cot, 0, keepdims=True),
        ],
        0,
    )
    gather = four_apart(512, BLOCK, 1)
    mine = lax.broadcasted_iota(jnp.int32, (4, 512), 0) == (
        lax.broadcasted_iota(jnp.int32, (4, 512), 1) % 4
    )
    for g in range(6):
        high, low = split_low(jnp.where(mine, fcsum[:, g * 512 : (g + 1) * 512], 0.0))
        sums_ref[4:8, g * BLOCK : (g + 1) * BLOCK] = mm(high, gather) + mm(low, gather)
    stored(0)
    stored(1)
    finish(outs)


def last_kernel(
    x_ref,
    one_ref,
    gq_ref,
    gmid_ref,
    wq_ref,
    early_ref,
    vec_ref,
    sums_ref,
    dkv_ref,
    gx_ref,
    keep_ref,
    send_ref,
    pack_ref,
):
    gkv = jnp.sum(dkv_ref[...].astype(f32), 0).astype(bf16)
    gq = gq_ref[...]
    vec = vec_ref[...]
    grad_one = mm_nt(gq, wq_ref[...]) + mm_nt(gkv, early_ref[:, :BLOCK])
    normed, factor = normalize(x_ref[...].astype(f32))
    gx_ref[...] = (gmid_ref[...] + norm_back(grad_one * vec[0:1], normed, factor)).astype(bf16)
    pack_ref[:, :BLOCK] = mm(one_ref[...].astype(f32).T.astype(bf16), gkv).astype(bf16)
    sums = sums_ref[...]
    rows = jnp.concatenate(
        [
            jnp.sum(grad_one * normed, 0, keepdims=True),
            jnp.sum(grad_one, 0, keepdims=True),
            jnp.sum(gq.astype(f32), 0, keepdims=True),
            sums,
            jnp.zeros((5, D), f32),
        ],
        0,
    )
    high, low = split_low(rows)
    value = jnp.sum(gkv.astype(f32), 0, keepdims=True)[:, HD:]
    value_high, value_low = split_low(value)
    lane = lax.broadcasted_iota(jnp.int32, (16, HD), 1)
    mine = (lane & 15) == lax.broadcasted_iota(jnp.int32, (16, HD), 0)
    group = lax.broadcasted_iota(jnp.int32, (HD, D), 0) // 16
    spread = jnp.where(group == lax.broadcasted_iota(jnp.int32, (HD, D), 1) % 6, 1.0, 0.0).astype(bf16)
    put_high = mm(jnp.where(mine, value_high.astype(f32), 0.0).astype(bf16), spread)
    put_low = mm(jnp.where(mine, value_low.astype(f32), 0.0).astype(bf16), spread)
    packed = jnp.concatenate(
        [high.astype(f32), low.astype(f32), put_high, put_low, jnp.zeros((64, D), f32)], 0
    )
    pack_ref[:, BLOCK:] = packed.T.astype(bf16)
    deal_rows(pack_ref, keep_ref, send_ref)


SMEM = pl.BlockSpec(memory_space=pltpu.SMEM)
VMEM = pl.BlockSpec(memory_space=pltpu.VMEM)
ANY = pl.BlockSpec(memory_space=pl.ANY)


def shape(*dims, dtype=bf16):
    return jax.ShapeDtypeStruct(dims, dtype)


def add_all(parts, dtype=bf16):
    total = parts[0].astype(f32)
    for part in parts[1:]:
        total = total + part.astype(f32)
    return total.astype(dtype)


def call(kernel, name, outs, args, scratch=(), smem=0, hbm=(), hbm_out=0, flops=0, moved=0, exps=0):
    places = [SMEM if i < smem else ANY if i in hbm else VMEM for i in range(len(args))]
    return pl.pallas_call(
        kernel,
        out_shape=outs,
        in_specs=places,
        out_specs=[VMEM] * (len(outs) - hbm_out) + [ANY] * hbm_out,
        scratch_shapes=list(scratch),
        compiler_params=pltpu.CompilerParams(vmem_limit_bytes=56 * 1024 * 1024),
        cost_estimate=pl.CostEstimate(flops=flops, bytes_accessed=moved, transcendentals=exps),
        name=name,
    )(*args)


def tie(value, after):
    return lax.optimization_barrier((value, after))[0]


def local(
    layer_input,
    cotangent,
    lengths,
    order,
    files,
    ln1_gain,
    ln1_bias,
    w_attn,
    query_bias,
    value_bias,
    w_out,
    out_bias,
    ln2_gain,
    ln2_bias,
    w_fc,
    fc_bias,
    w_proj,
    proj_bias,
):
    x = layer_input[0]
    cot = cotangent[0]
    vectors = [ln1_gain, ln1_bias, query_bias, out_bias, ln2_gain, ln2_bias, proj_bias, fc_bias]
    (pieces,) = call(
        piece_kernel,
        "pieces",
        [shape(16, 24, FOLD)],
        [*vectors, w_attn, w_out, w_fc, w_proj],
        [pltpu.VMEM((6, WIDE), f32)],
        smem=8,
        moved=2_000_000,
    )
    attn_block, feed_block = call(
        block_kernel,
        "blocks",
        [shape(4, 2 * ROWS, FC), shape(2 * ROWS, 2 * FF)],
        [lax.all_to_all(pieces, ("zl", "y", "zh"), 0, 0)],
        [pltpu.VMEM((2 * ROWS, WIDE), f32)],
        moved=4_000_000,
    )
    feed = lax.all_gather(feed_block, ("x", "core"), axis=0, tiled=True)
    attn = lax.all_to_all(attn_block, "x", 0, 0).reshape(8, ROWS, FC)
    parts = [attn, send(attn, dc=1)]
    one, kv, vec, early = call(
        first_kernel,
        "first",
        [
            shape(TOK, D),
            shape(8, TOK, BLOCK),
            shape(16, D, dtype=f32),
            shape(D, 2 * BLOCK),
        ],
        [x, value_bias[None], *parts],
        [pltpu.SemaphoreType.DMA],
        hbm=(2, 3),
        flops=100_000_000,
        moved=4_000_000,
    )
    kv = lax.all_to_all(kv, CTX, 0, 0).reshape(LENGTH, BLOCK)

    wide = (PAIRS, 2 * BLOCK, 2 * BLOCK)
    plan = [lengths, order, files]
    q, qt, fcb, wq = call(
        query_kernel,
        "query",
        [shape(TOK, D), shape(2, *wide), shape(1, FF, dtype=f32), shape(D, D)],
        [*plan, one, vec, early, *parts],
        [pltpu.SemaphoreType.DMA],
        smem=2,
        hbm=(6, 7),
        flops=300_000_000,
        moved=4_000_000,
    )
    att, lse = call(
        forward_kernel,
        "attend",
        [shape(TOK, D), shape(2, PAIRS, 8, 2 * BLOCK, dtype=f32)],
        [*plan, kv, qt],
        [
            pltpu.VMEM((LENGTH, 2 * BLOCK), bf16),
            pltpu.VMEM((HD, LENGTH), bf16),
            pltpu.VMEM((PAIRS, LENGTH, 2 * BLOCK), f32),
            pltpu.VMEM((PAIRS, 8, 2 * BLOCK), f32),
            pltpu.VMEM((PAIRS, 8, 2 * BLOCK), f32),
            pltpu.VMEM((PAIRS, HD, 2 * BLOCK), f32),
        ],
        smem=2,
        flops=10_000_000_000,
        moved=4_000_000,
        exps=6_000_000,
    )

    half = shape(8, ROWS, D)
    sliced = shape(4, 8, ROWS, SENT)
    output, grad_middle, grad_att, sums, keep_proj, send_proj, grad_fc = call(
        middle_kernel,
        "feed",
        [
            shape(TOK, D),
            shape(TOK, D, dtype=f32),
            shape(TOK, D),
            shape(8, D, dtype=f32),
            sliced,
            sliced,
            shape(4, 2, 2, ROWS, REDUCED),
        ],
        [feed, *parts, x, cot, att, vec, fcb],
        [
            pltpu.VMEM((2, D, SLICE), bf16),
            pltpu.VMEM((2, D, SLICE), bf16),
            pltpu.VMEM((2, D, SLICE), bf16),
            pltpu.VMEM((2, D, SLICE), bf16),
            pltpu.SemaphoreType.DMA((2, 2)),
            pltpu.SemaphoreType.DMA((2, 2)),
            pltpu.SemaphoreType.DMA,
            pltpu.VMEM((D, D), bf16),
            pltpu.VMEM((D, D), bf16),
            pltpu.VMEM((TOK, D), bf16),
            pltpu.VMEM((D, TOK), bf16),
            pltpu.VMEM((D, TOK), bf16),
            pltpu.VMEM((TOK, D), f32),
            pltpu.VMEM((TOK, D), f32),
            pltpu.VMEM((TOK, D), f32),
            pltpu.VMEM((1, FF), f32),
        ],
        hbm=(0, 1, 2),
        hbm_out=3,
        flops=8_000_000_000,
        moved=30_000_000,
        exps=1_000_000,
    )
    grad_fc = grad_fc.reshape(8, 2, ROWS, REDUCED)
    grad_fc = lax.psum_scatter(grad_fc, ("x", "core"), scatter_dimension=0, tiled=True)[0]
    grad_proj = add_all([keep_proj, send(send_proj, dc=1)])
    grad_att = tie(grad_att, grad_proj)
    grad_proj = add_all(list(lax.all_to_all(grad_proj, "y", 0, 0)))

    gq, keep_q, send_q, grad_kv = call(
        backward_kernel,
        "attend_back",
        [shape(TOK, D), half, half, shape(BLOCKS, BLOCK, BLOCK)],
        [*plan, q, grad_att, att, lse, one, kv],
        [
            pltpu.VMEM((LENGTH, 2 * BLOCK), bf16),
            pltpu.VMEM(wide, bf16),
            pltpu.VMEM(wide, bf16),
            pltpu.VMEM((PAIRS * 4 * BLOCK, BLOCK), bf16),
            pltpu.VMEM((4 * BLOCK, PAIRS * 4 * BLOCK), bf16),
            pltpu.VMEM((HD, LENGTH), bf16),
            pltpu.VMEM((PAIRS, HD, 2 * BLOCK), f32),
            pltpu.VMEM((LENGTH, BLOCK), f32),
            pltpu.VMEM((D, D), bf16),
        ],
        smem=2,
        flops=20_000_000_000,
        moved=6_000_000,
        exps=6_000_000,
    )
    got_q = send(send_q, dc=1)
    parts_q = [add_all([keep_q[2 * k : 2 * k + 2], got_q[2 * k : 2 * k + 2]]) for k in range(4)]
    parts_q = [parts_q[0]] + [send(parts_q[k], dx=k) for k in (1, 2, 3)]
    grad_q = add_all(parts_q).reshape(2 * ROWS, D)
    grad_kv = tie(grad_kv.reshape(8, TOK, BLOCK), grad_proj)
    grad_kv = lax.all_to_all(grad_kv, CTX, 0, 0)

    small = shape(8, ROWS, 2 * BLOCK)
    grad_x, keep_pack, send_pack = call(
        last_kernel,
        "last",
        [shape(TOK, D), small, small],
        [x, one, gq, grad_middle, wq, early, vec, sums, grad_kv],
        [pltpu.VMEM((D, 2 * BLOCK), bf16)],
        flops=1_000_000_000,
        moved=5_000_000,
    )
    grad_pack = add_all([keep_pack, send(send_pack, dc=1)])
    both = jnp.concatenate([grad_pack, grad_proj], 2).reshape(4, 2 * ROWS, G_QUERY)
    both = tie(both, grad_q)
    both = lax.all_to_all(both, "x", 0, 0)
    (pieces,) = call(
        unblock_kernel,
        "unblock",
        [shape(16, 24, G_FOLD)],
        [both, grad_q, grad_fc],
        [pltpu.VMEM((2 * ROWS, 4 * G_FOLD), f32)],
    )
    results = call(
        finish_kernel,
        "finish",
        [
            shape(6, D + BLOCK, dtype=f32),
            shape(6, D, dtype=f32),
            shape(6, FF, dtype=f32),
            shape(6, FF, dtype=f32),
        ]
        + [shape(1, 6, dtype=f32)] * 7
        + [shape(1, 24, dtype=f32), shape(1, HD, dtype=f32)],
        [lax.all_to_all(pieces, ("zl", "y", "zh"), 0, 0)],
        [pltpu.VMEM((6, 4 * G_FOLD), f32)],
    )
    grad_w_attn, grad_w_out, grad_w_fc, grad_w_proj = results[:4]
    gain_one, bias_one, bias_query, bias_out, gain_two, bias_two, bias_proj, bias_fc = (
        value.reshape(-1) for value in results[4:12]
    )
    return (
        output[None],
        grad_x[None],
        gain_one,
        bias_one,
        grad_w_attn,
        bias_query,
        results[12].reshape(HD),
        grad_w_out,
        bias_out,
        gain_two,
        bias_two,
        grad_w_fc,
        bias_fc,
        grad_w_proj,
        bias_proj,
    )


def solution(mesh):
    cells = Mesh(mesh.devices.reshape(SIZES), AXES)
    every = P(AXES)
    tall = P(AXES, None)
    tokens = P(DP, CTX, None)
    in_specs = (
        tokens,
        tokens,
        P(DP),
        P(DP, None),
        P(DP, None),
        every,
        every,
        tall,
        every,
        P(),
        tall,
        every,
        every,
        every,
        tall,
        every,
        tall,
        every,
    )
    out_specs = (
        tokens,
        tokens,
        every,
        every,
        tall,
        every,
        P(),
        tall,
        every,
        every,
        every,
        tall,
        every,
        tall,
        every,
    )
    return jax.shard_map(local, mesh=cells, in_specs=in_specs, out_specs=out_specs, check_vma=False)
```

```python
import functools

import jax
import jax.numpy as jnp
import numpy as np
from jax import lax
from jax.experimental import pallas as pl
from jax.experimental.pallas import tpu as pltpu
from jax.sharding import Mesh
from jax.sharding import PartitionSpec as P

D = 768
HEADS = 12
HD = 64
FF = 3072
TOK = 256
LENGTH = 2048
BLOCK = 128
BLOCKS = 16
PAIRS = 6
ROWS = 48
COLS = 384
NEG = -1e30

AXES = ("x", "zl", "core", "y", "zh")
SIZES = (4, 2, 2, 4, 2)
DP = ("x", "zl", "core")
CTX = ("y", "zh")

f32 = jnp.float32
bf16 = jnp.bfloat16


def route(dx=0, dy=0, dz=0, dc=0, dl=0, dh=0):
    pairs = []
    for device in range(128):
        x, zl, core, y, zh = (int(v) for v in np.unravel_index(device, SIZES))
        z = (zh * 2 + zl + dz) % 4
        target = ((x + dx) % 4, z % 2 ^ dl, core ^ dc, (y + dy) % 4, z // 2 ^ dh)
        pairs.append((device, int(np.ravel_multi_index(target, SIZES))))
    return pairs


def send(value, **shift):
    return lax.ppermute(value, AXES, route(**shift))


def row_span(group, other):
    core = lax.axis_index("core")
    return pl.ds(pl.multiple_of(group * 96 + (1 - core if other else core) * ROWS, 16), ROWS)


def row_copies(parts, lanes, target, sem):
    return [
        pltpu.make_async_copy(part.at[k, :, lanes], target.at[row_span(k, other)], sem)
        for k in range(8)
        for other, part in enumerate(parts)
    ]


def start(copies):
    for copy in copies:
        copy.start()


def finish(copies):
    for copy in copies:
        copy.wait()


def mm(left, right):
    return lax.dot_general(left, right, (((1,), (0,)), ((), ())), preferred_element_type=f32)


def mm_nt(left, right):
    return lax.dot_general(left, right, (((1,), (1,)), ((), ())), preferred_element_type=f32)


def normalize(values):
    center = values - jnp.mean(values, -1, keepdims=True)
    spread = jnp.mean(center * center, -1, keepdims=True)
    factor = lax.rsqrt(spread + 1e-05)
    return center * factor, factor


def norm_back(grad_normed, normed, factor):
    return factor * (
        grad_normed
        - jnp.mean(grad_normed, -1, keepdims=True)
        - normed * jnp.mean(grad_normed * normed, -1, keepdims=True)
    )


def split_low(values):
    high = values.astype(bf16)
    return high, (values - high.astype(f32)).astype(bf16)


SLICE = 768
KEYS, SMALL, QUERY, OUT, FC, PROJ, WIDE = 0, 128, 256, 1024, 1792, 4864, 8192
FOLD = WIDE // 4
SENT = 256
REST = SLICE - SENT
G_PROJ, G_QUERY, G_FC, G_OUT, G_REST, G_WIDE = 256, 512, 1280, 4352, 5120, 7168
G_FOLD = (G_WIDE + 511) // 512 * BLOCK
REDUCED = G_WIDE - G_FC


def piece_kernel(*refs):
    vectors, fcb_ref, attn_ref, out_ref, fc_ref, proj_ref, piece_ref, row = (
        refs[:7],
    ) + refs[7:]
    line = lax.broadcasted_iota(jnp.int32, (8, BLOCK), 0)
    lane = lax.broadcasted_iota(jnp.int32, (8, BLOCK), 1)
    small = jnp.zeros((8, BLOCK), f32)
    for i in range(6):
        values = [ref[i] for ref in vectors] + [fcb_ref[4 * i + j] for j in range(4)]
        for j, value in enumerate(values):
            small = jnp.where((line == i) & (lane < 48) & ((lane & 15) == j), value, small)
    high = small.astype(bf16).astype(f32)
    middle = (small - high).astype(bf16).astype(f32)
    low = small - high - middle
    small = jnp.where(lane < 16, high, jnp.where(lane < 32, middle, low))[:6]
    row[:6, KEYS:SMALL] = attn_ref[:, D:].astype(f32)
    row[:6, SMALL:QUERY] = small
    row[:6, QUERY:OUT] = attn_ref[:, :D].astype(f32)
    row[:6, OUT:FC] = out_ref[...].astype(f32)
    row[:6, FC:PROJ] = fc_ref[...].astype(f32)
    row[:6, PROJ : PROJ + FF] = proj_ref[...].astype(f32)
    row[:6, PROJ + FF :] = jnp.zeros((6, WIDE - PROJ - FF), f32)
    quarters = [row[:6, k * FOLD : (k + 1) * FOLD] for k in range(4)]
    piece = jnp.concatenate(quarters, 0).astype(bf16)

    def copy(k, carry):
        piece_ref[k] = piece
        return carry

    lax.fori_loop(0, 16, copy, 0)


def block_kernel(piece_ref, attn_ref, feed_ref, rows):
    for j in range(16):
        piece = piece_ref[j].astype(f32)
        for k in range(4):
            rows[6 * j : 6 * j + 6, k * FOLD : (k + 1) * FOLD] = piece[6 * k : 6 * k + 6]
    for k in range(4):
        attn_ref[k] = rows[: 2 * ROWS, :FC].astype(bf16)
    feed_ref[...] = rows[: 2 * ROWS, FC : FC + 2 * FF].astype(bf16)


def fold_lanes(rows):
    width = rows.shape[1] // 4
    return jnp.concatenate([rows[:, k * width : (k + 1) * width] for k in range(4)], 0)


def unblock_kernel(attn_ref, query_ref, feed_ref, piece_ref, rows):
    rows[: 2 * ROWS, :G_QUERY] = jnp.sum(attn_ref[...].astype(f32), 0)
    rows[: 2 * ROWS, G_QUERY:G_FC] = query_ref[...].astype(f32)
    for zl in range(2):
        rows[zl * ROWS : (zl + 1) * ROWS, G_FC:G_WIDE] = feed_ref[zl].astype(f32)
    if G_WIDE < 4 * G_FOLD:
        rows[: 2 * ROWS, G_WIDE:] = jnp.zeros((2 * ROWS, 4 * G_FOLD - G_WIDE), f32)
    for j in range(16):
        piece_ref[j] = fold_lanes(rows[6 * j : 6 * j + 6]).astype(bf16)


def finish_kernel(piece_ref, attn_ref, out_ref, fc_ref, proj_ref, *refs):
    vectors, fcb_ref, value_ref, rows = refs[:7], refs[7], refs[8], refs[9]
    total = jnp.sum(piece_ref[...].astype(f32), 0)
    for k in range(4):
        rows[:6, k * G_FOLD : (k + 1) * G_FOLD] = total[6 * k : 6 * k + 6]
    total = rows[:6]
    attn_ref[:, :D] = total[:, G_QUERY:G_FC]
    attn_ref[:, D:] = total[:, KEYS:SMALL]
    fc_ref[...] = total[:, G_FC:G_OUT]
    out_ref[...] = total[:, G_OUT:G_REST]
    for j in range(4):
        sent = [piece_ref[k, :6, G_PROJ:G_QUERY].astype(f32) for k in (2 * j, 2 * j + 1, 2 * j + 8, 2 * j + 9)]
        proj_ref[:, j * SLICE : j * SLICE + SENT] = sent[0] + sent[1] + sent[2] + sent[3]
        proj_ref[:, j * SLICE + SENT : (j + 1) * SLICE] = total[
            :, G_REST + j * REST : G_REST + (j + 1) * REST
        ]
    small = total[:, SMALL:QUERY]
    small = jnp.concatenate([small, jnp.zeros((2, BLOCK), f32)], 0).T
    rows = small[:16] + small[16:32]
    for j, ref in enumerate(vectors):
        ref[...] = rows[j : j + 1, :6]
    spread = jnp.where(
        lax.broadcasted_iota(jnp.int32, (8, 24), 1) // 4
        == lax.broadcasted_iota(jnp.int32, (8, 24), 0),
        1.0,
        0.0,
    )
    wide = jnp.dot(rows[7:11], spread, precision=lax.Precision.HIGHEST)
    mine = lax.broadcasted_iota(jnp.int32, (4, 24), 1) % 4 == lax.broadcasted_iota(
        jnp.int32, (4, 24), 0
    )
    fcb_ref[...] = jnp.sum(jnp.where(mine, wide, 0.0), 0, keepdims=True)
    value = total[:4, SMALL + 32 : SMALL + 48] + total[:4, SMALL + 48 : SMALL + 64]
    value_ref[...] = jnp.concatenate([value[j : j + 1] for j in range(4)], 1)


def four_apart(rows, columns, turned):
    return jnp.where(
        lax.broadcasted_iota(jnp.int32, (rows, columns), 1 - turned) // 4
        == lax.broadcasted_iota(jnp.int32, (rows, columns), turned),
        1.0,
        0.0,
    ).astype(bf16)


def first_kernel(
    x_ref, vbias_ref, mine_ref, other_ref, one_ref, kv_ref, vec_ref, early_ref, sem
):
    copies = row_copies((mine_ref, other_ref), pl.ds(0, QUERY), early_ref, sem)
    start(copies)
    normed, _ = normalize(x_ref[...].astype(f32))
    finish(copies)
    turned = early_ref[:, BLOCK:].astype(f32).T
    vec = turned[0:16] + turned[16:32] + turned[32:48]
    vec_ref[...] = vec
    one = (normed * vec[0:1] + vec[1:2]).astype(bf16)
    one_ref[...] = one
    bias = jnp.concatenate([jnp.zeros((1, HD), f32), vbias_ref[...]], 1)
    kv = (mm(one, early_ref[:, :BLOCK]) + bias).astype(bf16)
    for k in range(8):
        kv_ref[k] = kv


def read_plan(length_ref, order_ref, files_ref):
    files = files_ref[...]
    bounds = [jnp.sum(jnp.where(files < f, 1, 0)) for f in (1, 2, 3)]
    return length_ref[0], bounds


def block_plan(plan, order_ref, b):
    length, bounds = plan
    own = lax.axis_index("y") * 2 + lax.axis_index("zh")
    place = order_ref[0, own * 2 + b]
    start = place * BLOCK
    first = jnp.int32(0)
    for bound in bounds:
        first = jnp.where(bound <= start, jnp.maximum(first, bound), first)
    low = first // BLOCK
    high = jnp.minimum(place - 1, (length - 1) // BLOCK)
    return place, low, jnp.maximum(high - low + 1, 0)


def own_bias(plan, place):
    length, bounds = plan
    lane = lax.broadcasted_iota(jnp.int32, (1, 2 * BLOCK), 1)
    query = place * BLOCK + (lane & (BLOCK - 1))
    first = jnp.zeros_like(query)
    for bound in bounds:
        first = jnp.where(bound <= query, jnp.maximum(first, bound), first)
    last = jnp.minimum(query, length - 1)
    key = place * BLOCK + lax.broadcasted_iota(jnp.int32, (BLOCK, 2 * BLOCK), 0)
    allowed = ((key >= first) & (key <= last)) | (key == query)
    return jnp.where(allowed, 0.0, NEG)


def file_of(plan, position):
    number = jnp.zeros_like(position)
    for bound in plan[1]:
        number = number + jnp.where(bound <= position, 1, 0)
    return number


def place_keys(plan, order_ref, kv_ref, keys):
    lane = lax.broadcasted_iota(jnp.int32, (BLOCK, BLOCK), 1)

    def place(k, carry):
        start = pl.multiple_of(order_ref[0, k] * BLOCK, BLOCK)
        position = start + lax.broadcasted_iota(jnp.int32, (BLOCK, BLOCK), 0)
        mark = (file_of(plan, position) == lane) | ((position >= plan[0]) & (lane == 4))
        mark = mark | ((lane >= 5) & (lane < 8))
        keys[pl.ds(start, BLOCK), :BLOCK] = kv_ref[pl.ds(pl.multiple_of(k * BLOCK, BLOCK), BLOCK)]
        keys[pl.ds(start, BLOCK), BLOCK:] = jnp.where(mark, 1.0, 0.0).astype(bf16)
        return carry

    lax.fori_loop(0, BLOCKS, place, 0)


def own_keys(keys, place):
    rows = keys[pl.ds(pl.multiple_of(place * BLOCK, BLOCK), BLOCK)]
    lane = lax.broadcasted_iota(jnp.int32, rows.shape, 1)
    return jnp.where((lane >= BLOCK) & (lane < BLOCK + 5), jnp.zeros_like(rows), rows)


def query_marks(plan, place):
    lane = lax.broadcasted_iota(jnp.int32, (8, 2 * BLOCK), 1)
    number = file_of(plan, place * BLOCK + (lane & (BLOCK - 1)))
    mark = lax.broadcasted_iota(jnp.int32, (8, 2 * BLOCK), 0)
    return jnp.where(((mark < 4) & (mark != number)) | (mark == 4), NEG, 0.0)


def minus_terms(row):
    high = row.astype(bf16).astype(f32)
    middle = (row - high).astype(bf16).astype(f32)
    low = row - high - middle
    mark = lax.broadcasted_iota(jnp.int32, (8, row.shape[1]), 0)
    return jnp.where(
        mark == 5, -high, jnp.where(mark == 6, -middle, jnp.where(mark == 7, -low, 0.0))
    )


def fill(target, top, marks):
    target[:BLOCK] = top
    zeros = jnp.zeros((BLOCK - 8, 2 * BLOCK), f32)
    target[BLOCK:] = jnp.concatenate([marks, zeros], 0).astype(bf16)


def sweep(low, count, step):
    def four(t, carry):
        step(low + 4 * t, 4)
        return carry

    lax.fori_loop(0, count // 4, four, 0)

    @pl.when(lax.rem(count, 4) >= 2)
    def _():
        step(low + count // 4 * 4, 2)

    @pl.when(lax.rem(count, 2) == 1)
    def _():
        step(low + count - 1, 1)


def fold_heads(block):
    turned = block.T
    return jnp.concatenate([turned[:HD], turned[HD:]], 1)


def unfold_heads(wide):
    return jnp.concatenate([wide[:, :BLOCK], wide[:, BLOCK:]], 0).T


def eights(values):
    return values.reshape(values.shape[0] // 8, 8, values.shape[1])


def query_kernel(
    length_ref,
    order_ref,
    files_ref,
    one_ref,
    vec_ref,
    early_ref,
    mine_ref,
    other_ref,
    q_ref,
    qt_ref,
    fcb_ref,
    wq,
    sem,
):
    copies = row_copies((mine_ref, other_ref), pl.ds(QUERY, D), wq, sem)
    start(copies)
    plan = read_plan(length_ref, order_ref, files_ref)
    finish(copies)
    q = (mm(one_ref[...], wq[...]) + vec_ref[2:3]).astype(bf16)
    q_ref[...] = q
    terms = early_ref[:, BLOCK:].T[:48]
    spread = four_apart(BLOCK, 512, 0)
    term = lax.broadcasted_iota(jnp.int32, (48, 512), 0) % 16 - 7
    mine = term == lax.broadcasted_iota(jnp.int32, (48, 512), 1) % 4
    for g in range(6):
        wide = mm(terms[:, g * BLOCK : (g + 1) * BLOCK], spread)
        fcb_ref[:, g * 512 : (g + 1) * 512] = jnp.sum(
            jnp.where(mine, wide, 0.0), 0, keepdims=True
        )
    empty = jnp.zeros((HD, 2 * BLOCK), bf16)
    for b in range(2):
        place, _, _ = block_plan(plan, order_ref, b)
        marks = query_marks(plan, place)
        for p in range(PAIRS):
            block = q[b * BLOCK : (b + 1) * BLOCK, p * BLOCK : (p + 1) * BLOCK] * 0.125
            top = jnp.concatenate([fold_heads(block), empty], 0)
            fill(qt_ref.at[b, p], top, marks)


def forward_kernel(
    length_ref,
    order_ref,
    files_ref,
    kv_ref,
    qt_ref,
    att_ref,
    lse_ref,
    keys,
    vt,
    scores,
    tops,
    sums,
    mixed,
):
    plan = read_plan(length_ref, order_ref, files_ref)
    place_keys(plan, order_ref, kv_ref, keys)
    for k in range(BLOCKS):
        vt[:, k * BLOCK : (k + 1) * BLOCK] = keys[k * BLOCK : (k + 1) * BLOCK, :BLOCK].T[HD:]
    for b in range(2):
        place, low, count = block_plan(plan, order_ref, b)
        qt = qt_ref.at[b]
        own = own_keys(keys, place)
        bias = own_bias(plan, place)
        for p in range(PAIRS):
            value = mm(own, qt[p]) + bias
            scores[p, 0:BLOCK] = value
            tops[p] = jnp.max(eights(value), 0)

        def score_step(first, blocks):
            rows = keys[pl.ds(pl.multiple_of(first * BLOCK, BLOCK), blocks * BLOCK)]
            at = pl.ds(pl.multiple_of((first - low + 1) * BLOCK, BLOCK), blocks * BLOCK)
            for p in range(PAIRS):
                value = mm(rows, qt[p])
                scores[p, at] = value
                tops[p] = jnp.maximum(tops[p], jnp.max(eights(value), 0))

        sweep(low, count, score_step)
        peaks = [jnp.max(tops[p], 0, keepdims=True) for p in range(PAIRS)]
        for p in range(PAIRS):
            tops[p] = jnp.broadcast_to(peaks[p], (8, 2 * BLOCK))
            weight = jnp.exp(scores[p, 0:BLOCK] - peaks[p])
            sums[p] = jnp.sum(eights(weight), 0)
            span = pl.ds(pl.multiple_of(place * BLOCK, BLOCK), BLOCK)
            mixed[p] = mm(vt[:, span], weight.astype(bf16))

        def mix_step(first, blocks):
            span = pl.ds(pl.multiple_of(first * BLOCK, BLOCK), blocks * BLOCK)
            at = pl.ds(pl.multiple_of((first - low + 1) * BLOCK, BLOCK), blocks * BLOCK)
            values = vt[:, span]
            for p in range(PAIRS):
                weight = jnp.exp(scores[p, at] - tops[p, 0:1])
                sums[p] += jnp.sum(eights(weight), 0)
                mixed[p] += mm(values, weight.astype(bf16))

        sweep(low, count, mix_step)
        for p in range(PAIRS):
            total = jnp.sum(sums[p], 0, keepdims=True)
            lse_ref[b, p] = tops[p] + jnp.log(total)
            att_ref[b * BLOCK : (b + 1) * BLOCK, p * BLOCK : (p + 1) * BLOCK] = unfold_heads(
                (mixed[p] / total).astype(bf16)
            )


def backward_kernel(
    length_ref,
    order_ref,
    files_ref,
    q_ref,
    do_ref,
    att_ref,
    lse_ref,
    one_ref,
    kv_ref,
    gq_ref,
    keep_ref,
    send_ref,
    grad_ref,
    keys,
    qt,
    dot_,
    qd,
    both,
    kt,
    dq,
    dkv,
    gwq,
):
    plan = read_plan(length_ref, order_ref, files_ref)
    place_keys(plan, order_ref, kv_ref, keys)
    for k in range(BLOCKS):
        kt[:, k * BLOCK : (k + 1) * BLOCK] = (
            keys[k * BLOCK : (k + 1) * BLOCK, :BLOCK].T[:HD]
        )
    dkv[...] = jnp.zeros_like(dkv)
    zeros = jnp.zeros((BLOCK, HD), bf16)
    empty = jnp.zeros((HD, 2 * BLOCK), bf16)
    for b in range(2):
        place, low, count = block_plan(plan, order_ref, b)
        marks = query_marks(plan, place)
        for p in range(PAIRS):
            span = (slice(b * BLOCK, (b + 1) * BLOCK), slice(p * BLOCK, (p + 1) * BLOCK))
            block = q_ref[span] * 0.125
            grad = do_ref[span]
            wide = fold_heads(grad)
            out = fold_heads(att_ref[span]).astype(f32)
            delta = jnp.sum(wide.astype(f32) * out, 0, keepdims=True)
            top = jnp.concatenate([fold_heads(block), empty], 0)
            fill(qt.at[p], top, marks + minus_terms(lse_ref[b, p, 0:1]))
            fill(dot_.at[p], jnp.concatenate([empty, wide], 0), minus_terms(delta))
            factors = [
                jnp.concatenate([block[:, :HD], zeros], 1),
                jnp.concatenate([block[:, HD:], zeros], 1),
                jnp.concatenate([zeros, grad[:, :HD]], 1),
                jnp.concatenate([zeros, grad[:, HD:]], 1),
            ]
            qd[512 * p : 512 * (p + 1)] = jnp.concatenate(factors, 0)
        dq[...] = jnp.zeros_like(dq)

        def step(first, blocks, rows=None, bias=None):
            span = pl.ds(pl.multiple_of(first * BLOCK, BLOCK), blocks * BLOCK)
            rows = keys[span] if rows is None else rows
            turned = kt[:, span]
            size = blocks * BLOCK
            for p in range(PAIRS):
                value = mm(rows, qt[p])
                probs = jnp.exp(value if bias is None else value + bias)
                grad = (probs * mm(rows, dot_[p])).astype(bf16)
                dq[p] += mm(turned, grad)
                both[:size, 512 * p : 512 * p + 256] = grad
                both[:size, 512 * p + 256 : 512 * p + 512] = probs.astype(bf16)
            dkv[span] += mm(both[:size], qd[...])

        step(place, 1, own_keys(keys, place), own_bias(plan, place))
        sweep(low, count, step)
        for p in range(PAIRS):
            gq_ref[b * BLOCK : (b + 1) * BLOCK, p * BLOCK : (p + 1) * BLOCK] = unfold_heads(
                (dq[p] * 0.125).astype(bf16)
            )

    def give(k, carry):
        initial = order_ref[0, k]
        grad_ref[k] = dkv[pl.ds(pl.multiple_of(initial * BLOCK, BLOCK), BLOCK)].astype(bf16)
        return carry

    lax.fori_loop(0, BLOCKS, give, 0)
    gwq[...] = mm(one_ref[...].T, gq_ref[...]).astype(bf16)
    deal_rows(gwq, keep_ref, send_ref, lax.axis_index("x"))


def deal_rows(source, keep_ref, send_ref, x=0):
    for k in range(8):
        there = lax.rem(k // 2 - x + 4, 4) * 2 + k % 2
        keep_ref[there] = source[row_span(k, 0), :]
        send_ref[there] = source[row_span(k, 1), :]


def columns(c, first=0):
    return pl.ds(pl.multiple_of(first + c * SLICE, BLOCK), SLICE)


def middle_kernel(
    feed_ref,
    mine_ref,
    other_ref,
    x_ref,
    ct_ref,
    att_ref,
    vec_ref,
    fcb_ref,
    out_ref,
    gmid_ref,
    gatt_ref,
    sums_ref,
    keep_ref,
    send_ref,
    grad_ref,
    wf,
    wg,
    gf,
    gg,
    in_sem,
    out_sem,
    last_sem,
    wout,
    gout,
    x2,
    x2t,
    ctt,
    branch,
    gin,
    mid,
    fcsum,
):
    def load(c, slot):
        for k in range(16):
            rows = pl.ds((k // 4 * 4 + k % 2 * 2 + k // 2 % 2) * ROWS, ROWS)
            for half, (buffer, first) in enumerate(((wf, 0), (wg, FF))):
                pltpu.make_async_copy(
                    feed_ref.at[rows, columns(c, first)],
                    buffer.at[slot, pl.ds(k * ROWS, ROWS)],
                    in_sem.at[slot, half],
                ).start()

    def loaded(slot):
        pltpu.make_async_copy(wf.at[slot], wf.at[slot], in_sem.at[slot, 0]).wait()
        pltpu.make_async_copy(wg.at[slot], wg.at[slot], in_sem.at[slot, 1]).wait()

    def store(c, slot):
        for k in range(16):
            pltpu.make_async_copy(
                gf.at[slot, pl.ds(k * ROWS, ROWS)],
                grad_ref.at[k // 4, k % 2, k // 2 % 2, :, columns(c)],
                out_sem.at[slot, 0],
            ).start()
            pltpu.make_async_copy(
                gg.at[slot, pl.ds(k * ROWS, ROWS), pl.ds(SENT, REST)],
                grad_ref.at[
                    k // 4,
                    k % 2,
                    k // 2 % 2,
                    :,
                    pl.ds(pl.multiple_of(FF + D + c * REST, BLOCK), REST),
                ],
                out_sem.at[slot, 1],
            ).start()
        for k in range(8):
            for other, ref in enumerate((keep_ref, send_ref)):
                pltpu.make_async_copy(
                    gg.at[slot, row_span(k, other), pl.ds(0, SENT)],
                    ref.at[c, k],
                    out_sem.at[slot, 1],
                ).start()

    def stored(slot):
        pltpu.make_async_copy(gf.at[slot], gf.at[slot], out_sem.at[slot, 0]).wait()
        pltpu.make_async_copy(gg.at[slot], gg.at[slot], out_sem.at[slot, 1]).wait()

    copies = row_copies((mine_ref, other_ref), pl.ds(OUT, D), wout, last_sem)
    start(copies)
    load(0, 0)
    ctt[...] = ct_ref[...].T
    branch[...] = jnp.zeros_like(branch)
    gin[...] = jnp.zeros_like(gin)
    vec = vec_ref[...]
    finish(copies)
    middle = x_ref[...].astype(f32) + (mm_nt(att_ref[...], wout[...]) + vec[3:4])
    mid[...] = middle
    normed, factor = normalize(middle)
    two = (normed * vec[4:5] + vec[5:6]).astype(bf16)
    x2[...] = two
    x2t[...] = two.T

    def chunk(c, carry):
        slot = lax.rem(c, 2)

        @pl.when(c < 3)
        def _():
            load(c + 1, 1 - slot)

        loaded(slot)
        span = columns(c)
        pre = mm(x2[...], wf[slot]) + fcb_ref[:, span]
        grad_hidden = mm(ct_ref[...], wg[slot])
        square = pre * pre
        tanh = jnp.tanh(0.7978845608028654 * (pre + 0.044715 * (pre * square)))
        half = 0.5 * (1.0 + tanh)
        hidden = (pre * half).astype(bf16)
        slope = half + (0.5 * pre) * (1.0 - tanh * tanh) * (
            0.7978845608028654 + (3 * 0.044715 * 0.7978845608028654) * square
        )
        grad_pre = (grad_hidden * slope).astype(bf16)
        branch[...] += mm_nt(hidden, wg[slot])
        gin[...] += mm_nt(grad_pre, wf[slot])
        fcsum[:, span] = jnp.sum(grad_pre.astype(f32), 0, keepdims=True)

        @pl.when(c >= 2)
        def _():
            stored(slot)

        gf[slot] = mm(x2t[...], grad_pre).astype(bf16)
        gg[slot] = mm(ctt[...], hidden).astype(bf16)
        store(c, slot)
        return carry

    lax.fori_loop(0, 4, chunk, 0)
    middle = mid[...]
    cot = ct_ref[...].astype(f32)
    out_ref[...] = (middle + (branch[...] + vec[6:7])).astype(bf16)
    normed, factor = normalize(middle)
    grad_two = gin[...]
    grad_middle = cot + norm_back(grad_two * vec[4:5], normed, factor)
    gmid_ref[...] = grad_middle
    grad_branch = grad_middle.astype(bf16)
    gout[...] = mm(grad_branch.T, att_ref[...]).astype(bf16)
    outs = [
        pltpu.make_async_copy(
            gout.at[pl.ds(k * ROWS, ROWS)],
            grad_ref.at[k // 4, k % 2, k // 2 % 2, :, pl.ds(FF, D)],
            last_sem,
        )
        for k in range(16)
    ]
    start(outs)
    gatt_ref[...] = mm(grad_branch, wout[...]).astype(bf16)
    sums = jnp.concatenate(
        [
            jnp.sum(grad_branch.astype(f32), 0, keepdims=True),
            jnp.sum(grad_two * normed, 0, keepdims=True),
            jnp.sum(grad_two, 0, keepdims=True),
            jnp.sum(cot, 0, keepdims=True),
        ],
        0,
    )
    gather = four_apart(512, BLOCK, 1)
    mine = lax.broadcasted_iota(jnp.int32, (4, 512), 0) == (
        lax.broadcasted_iota(jnp.int32, (4, 512), 1) % 4
    )
    fc_sums = []
    for g in range(6):
        high, low = split_low(jnp.where(mine, fcsum[:, g * 512 : (g + 1) * 512], 0.0))
        fc_sums.append(mm(high, gather) + mm(low, gather))
    sums_ref[...] = jnp.concatenate([sums, jnp.concatenate(fc_sums, 1)], 0)
    stored(0)
    stored(1)
    finish(outs)


def last_kernel(
    x_ref,
    one_ref,
    gq_ref,
    gmid_ref,
    wq_ref,
    early_ref,
    vec_ref,
    sums_ref,
    dkv_ref,
    gx_ref,
    keep_ref,
    send_ref,
    pack_ref,
):
    gkv = jnp.sum(dkv_ref[...].astype(f32), 0).astype(bf16)
    gq = gq_ref[...]
    vec = vec_ref[...]
    grad_one = mm_nt(gq, wq_ref[...]) + mm_nt(gkv, early_ref[:, :BLOCK])
    normed, factor = normalize(x_ref[...].astype(f32))
    gx_ref[...] = (gmid_ref[...] + norm_back(grad_one * vec[0:1], normed, factor)).astype(bf16)
    pack_ref[:, :BLOCK] = mm(one_ref[...].astype(f32).T.astype(bf16), gkv).astype(bf16)
    sums = sums_ref[...]
    rows = jnp.concatenate(
        [
            jnp.sum(grad_one * normed, 0, keepdims=True),
            jnp.sum(grad_one, 0, keepdims=True),
            jnp.sum(gq.astype(f32), 0, keepdims=True),
            sums,
            jnp.zeros((5, D), f32),
        ],
        0,
    )
    high, low = split_low(rows)
    value = jnp.sum(gkv.astype(f32), 0, keepdims=True)[:, HD:]
    value_high, value_low = split_low(value)
    lane = lax.broadcasted_iota(jnp.int32, (16, HD), 1)
    mine = (lane & 15) == lax.broadcasted_iota(jnp.int32, (16, HD), 0)
    group = lax.broadcasted_iota(jnp.int32, (HD, D), 0) // 16
    spread = jnp.where(group == lax.broadcasted_iota(jnp.int32, (HD, D), 1) % 6, 1.0, 0.0).astype(bf16)
    put_high = mm(jnp.where(mine, value_high.astype(f32), 0.0).astype(bf16), spread)
    put_low = mm(jnp.where(mine, value_low.astype(f32), 0.0).astype(bf16), spread)
    packed = jnp.concatenate(
        [high.astype(f32), low.astype(f32), put_high, put_low, jnp.zeros((64, D), f32)], 0
    )
    pack_ref[:, BLOCK:] = packed.T.astype(bf16)
    deal_rows(pack_ref, keep_ref, send_ref)


SMEM = pl.BlockSpec(memory_space=pltpu.SMEM)
VMEM = pl.BlockSpec(memory_space=pltpu.VMEM)
ANY = pl.BlockSpec(memory_space=pl.ANY)


def shape(*dims, dtype=bf16):
    return jax.ShapeDtypeStruct(dims, dtype)


def add_all(parts, dtype=bf16):
    total = parts[0].astype(f32)
    for part in parts[1:]:
        total = total + part.astype(f32)
    return total.astype(dtype)


def call(kernel, name, outs, args, scratch=(), smem=0, hbm=(), hbm_out=0, flops=0, moved=0, exps=0):
    places = [SMEM if i < smem else ANY if i in hbm else VMEM for i in range(len(args))]
    return pl.pallas_call(
        kernel,
        out_shape=outs,
        in_specs=places,
        out_specs=[VMEM] * (len(outs) - hbm_out) + [ANY] * hbm_out,
        scratch_shapes=list(scratch),
        compiler_params=pltpu.CompilerParams(vmem_limit_bytes=56 * 1024 * 1024),
        cost_estimate=pl.CostEstimate(flops=flops, bytes_accessed=moved, transcendentals=exps),
        name=name,
    )(*args)


def tie(value, after):
    return lax.optimization_barrier((value, after))[0]


def local(
    layer_input,
    cotangent,
    lengths,
    order,
    files,
    ln1_gain,
    ln1_bias,
    w_attn,
    query_bias,
    value_bias,
    w_out,
    out_bias,
    ln2_gain,
    ln2_bias,
    w_fc,
    fc_bias,
    w_proj,
    proj_bias,
):
    x = layer_input[0]
    cot = cotangent[0]
    vectors = [ln1_gain, ln1_bias, query_bias, out_bias, ln2_gain, ln2_bias, proj_bias, fc_bias]
    (pieces,) = call(
        piece_kernel,
        "pieces",
        [shape(16, 24, FOLD)],
        [*vectors, w_attn, w_out, w_fc, w_proj],
        [pltpu.VMEM((8, WIDE), f32)],
        smem=8,
        moved=2_000_000,
    )
    attn_block, feed_block = call(
        block_kernel,
        "blocks",
        [shape(4, 2 * ROWS, FC), shape(2 * ROWS, 2 * FF)],
        [lax.all_to_all(pieces, ("zl", "y", "zh"), 0, 0)],
        [pltpu.VMEM((2 * ROWS + 8, WIDE), f32)],
        moved=4_000_000,
    )
    feed = lax.all_gather(feed_block, ("x", "core"), axis=0, tiled=True)
    attn = lax.all_to_all(attn_block, "x", 0, 0).reshape(8, ROWS, FC)
    parts = [attn, send(attn, dc=1)]
    one, kv, vec, early = call(
        first_kernel,
        "first",
        [
            shape(TOK, D),
            shape(8, TOK, BLOCK),
            shape(16, D, dtype=f32),
            shape(D, 2 * BLOCK),
        ],
        [x, value_bias[None], *parts],
        [pltpu.SemaphoreType.DMA],
        hbm=(2, 3),
        flops=100_000_000,
        moved=4_000_000,
    )
    kv = lax.all_to_all(kv, CTX, 0, 0).reshape(LENGTH, BLOCK)

    wide = (PAIRS, 2 * BLOCK, 2 * BLOCK)
    plan = [lengths, order, files]
    q, qt, fcb, wq = call(
        query_kernel,
        "query",
        [shape(TOK, D), shape(2, *wide), shape(1, FF, dtype=f32), shape(D, D)],
        [*plan, one, vec, early, *parts],
        [pltpu.SemaphoreType.DMA],
        smem=2,
        hbm=(6, 7),
        flops=300_000_000,
        moved=4_000_000,
    )
    att, lse = call(
        forward_kernel,
        "attend",
        [shape(TOK, D), shape(2, PAIRS, 8, 2 * BLOCK, dtype=f32)],
        [*plan, kv, qt],
        [
            pltpu.VMEM((LENGTH, 2 * BLOCK), bf16),
            pltpu.VMEM((HD, LENGTH), bf16),
            pltpu.VMEM((PAIRS, LENGTH, 2 * BLOCK), f32),
            pltpu.VMEM((PAIRS, 8, 2 * BLOCK), f32),
            pltpu.VMEM((PAIRS, 8, 2 * BLOCK), f32),
            pltpu.VMEM((PAIRS, HD, 2 * BLOCK), f32),
        ],
        smem=2,
        flops=10_000_000_000,
        moved=4_000_000,
        exps=6_000_000,
    )

    half = shape(8, ROWS, D)
    sliced = shape(4, 8, ROWS, SENT)
    output, grad_middle, grad_att, sums, keep_proj, send_proj, grad_fc = call(
        middle_kernel,
        "feed",
        [
            shape(TOK, D),
            shape(TOK, D, dtype=f32),
            shape(TOK, D),
            shape(8, D, dtype=f32),
            sliced,
            sliced,
            shape(4, 2, 2, ROWS, REDUCED),
        ],
        [feed, *parts, x, cot, att, vec, fcb],
        [
            pltpu.VMEM((2, D, SLICE), bf16),
            pltpu.VMEM((2, D, SLICE), bf16),
            pltpu.VMEM((2, D, SLICE), bf16),
            pltpu.VMEM((2, D, SLICE), bf16),
            pltpu.SemaphoreType.DMA((2, 2)),
            pltpu.SemaphoreType.DMA((2, 2)),
            pltpu.SemaphoreType.DMA,
            pltpu.VMEM((D, D), bf16),
            pltpu.VMEM((D, D), bf16),
            pltpu.VMEM((TOK, D), bf16),
            pltpu.VMEM((D, TOK), bf16),
            pltpu.VMEM((D, TOK), bf16),
            pltpu.VMEM((TOK, D), f32),
            pltpu.VMEM((TOK, D), f32),
            pltpu.VMEM((TOK, D), f32),
            pltpu.VMEM((1, FF), f32),
        ],
        hbm=(0, 1, 2),
        hbm_out=3,
        flops=8_000_000_000,
        moved=30_000_000,
        exps=1_000_000,
    )
    grad_fc = grad_fc.reshape(8, 2, ROWS, REDUCED)
    grad_fc = lax.psum_scatter(grad_fc, ("x", "core"), scatter_dimension=0, tiled=True)[0]
    grad_proj = add_all([keep_proj, send(send_proj, dc=1)])
    grad_att = tie(grad_att, grad_proj)
    grad_proj = add_all(list(lax.all_to_all(grad_proj, "y", 0, 0)))

    gq, keep_q, send_q, grad_kv = call(
        backward_kernel,
        "attend_back",
        [shape(TOK, D), half, half, shape(BLOCKS, BLOCK, BLOCK)],
        [*plan, q, grad_att, att, lse, one, kv],
        [
            pltpu.VMEM((LENGTH, 2 * BLOCK), bf16),
            pltpu.VMEM(wide, bf16),
            pltpu.VMEM(wide, bf16),
            pltpu.VMEM((PAIRS * 4 * BLOCK, BLOCK), bf16),
            pltpu.VMEM((4 * BLOCK, PAIRS * 4 * BLOCK), bf16),
            pltpu.VMEM((HD, LENGTH), bf16),
            pltpu.VMEM((PAIRS, HD, 2 * BLOCK), f32),
            pltpu.VMEM((LENGTH, BLOCK), f32),
            pltpu.VMEM((D, D), bf16),
        ],
        smem=2,
        flops=20_000_000_000,
        moved=6_000_000,
        exps=6_000_000,
    )
    got_q = send(send_q, dc=1)
    parts_q = [add_all([keep_q[2 * k : 2 * k + 2], got_q[2 * k : 2 * k + 2]]) for k in range(4)]
    parts_q = [parts_q[0]] + [send(parts_q[k], dx=k) for k in (1, 2, 3)]
    grad_q = add_all(parts_q).reshape(2 * ROWS, D)
    grad_kv = tie(grad_kv.reshape(8, TOK, BLOCK), grad_proj)
    grad_kv = lax.all_to_all(grad_kv, CTX, 0, 0)

    small = shape(8, ROWS, 2 * BLOCK)
    grad_x, keep_pack, send_pack = call(
        last_kernel,
        "last",
        [shape(TOK, D), small, small],
        [x, one, gq, grad_middle, wq, early, vec, sums, grad_kv],
        [pltpu.VMEM((D, 2 * BLOCK), bf16)],
        flops=1_000_000_000,
        moved=5_000_000,
    )
    grad_pack = add_all([keep_pack, send(send_pack, dc=1)])
    both = jnp.concatenate([grad_pack, grad_proj], 2).reshape(4, 2 * ROWS, G_QUERY)
    both = tie(both, grad_q)
    both = lax.all_to_all(both, "x", 0, 0)
    (pieces,) = call(
        unblock_kernel,
        "unblock",
        [shape(16, 24, G_FOLD)],
        [both, grad_q, grad_fc],
        [pltpu.VMEM((2 * ROWS + 8, 4 * G_FOLD), f32)],
    )
    results = call(
        finish_kernel,
        "finish",
        [
            shape(6, D + BLOCK, dtype=f32),
            shape(6, D, dtype=f32),
            shape(6, FF, dtype=f32),
            shape(6, FF, dtype=f32),
        ]
        + [shape(1, 6, dtype=f32)] * 7
        + [shape(1, 24, dtype=f32), shape(1, HD, dtype=f32)],
        [lax.all_to_all(pieces, ("zl", "y", "zh"), 0, 0)],
        [pltpu.VMEM((8, 4 * G_FOLD), f32)],
    )
    grad_w_attn, grad_w_out, grad_w_fc, grad_w_proj = results[:4]
    gain_one, bias_one, bias_query, bias_out, gain_two, bias_two, bias_proj, bias_fc = (
        value.reshape(-1) for value in results[4:12]
    )
    return (
        output[None],
        grad_x[None],
        gain_one,
        bias_one,
        grad_w_attn,
        bias_query,
        results[12].reshape(HD),
        grad_w_out,
        bias_out,
        gain_two,
        bias_two,
        grad_w_fc,
        bias_fc,
        grad_w_proj,
        bias_proj,
    )


def solution(mesh):
    cells = Mesh(mesh.devices.reshape(SIZES), AXES)
    every = P(AXES)
    tall = P(AXES, None)
    tokens = P(DP, CTX, None)
    in_specs = (
        tokens,
        tokens,
        P(DP),
        P(DP, None),
        P(DP, None),
        every,
        every,
        tall,
        every,
        P(),
        tall,
        every,
        every,
        every,
        tall,
        every,
        tall,
        every,
    )
    out_specs = (
        tokens,
        tokens,
        every,
        every,
        tall,
        every,
        P(),
        tall,
        every,
        every,
        every,
        tall,
        every,
        tall,
        every,
    )
    return jax.shard_map(local, mesh=cells, in_specs=in_specs, out_specs=out_specs, check_vma=False)
```
